32 devices in a mesh: batch: 2 (over x), seq: 16 (over z, y, core).
Axes of the slice: x: 2, y: 2, z: 4, core: 2. Of those that a mesh axis runs over, the one named last changes fastest.
Arguments:
- tokens: bfloat16 [16, 2048, 640], P('batch', 'seq'), may hold values from -6 to 6
- attention_params: bfloat16 [1640192], P(('batch', 'seq')), may hold values from -1.3 to 1.3
- feed_params: bfloat16 [3933440], P(('batch', 'seq')), may hold values from -1.3 to 1.3
- positions: int32 [16, 2048], P('batch', 'seq'), may hold values from 0 to 2047, as said below
- cotangent: bfloat16 [16, 2048, 640], P('batch', 'seq'), may hold values from -6 to 6
Outputs:
- mixed: bfloat16 [16, 2048, 640], P('batch', 'seq')
- grad_tokens: float32 [16, 2048, 640], P('batch', 'seq')
- grad_attention: float32 [1640192], P(('batch', 'seq'))
- grad_feed: float32 [3933440], P(('batch', 'seq'))
The draws below stay inside these ranges and needn't reach their ends.
Inputs may be any that keep to these rules, and one draw needn't show every extreme that they name: `positions`: in each sequence a position is one more than that of the token before it, or 0 where a document starts; every sequence starts a document at its first token and holds at most 4 documents; the first sequence is a single document.
All inputs are finite; a program needn't handle non-finite values.
Results may differ from the reference program's by a relative error of at most 0.012.
Values may be sent and summed in bfloat16 or wider, within the bound.
A program may use at most 192 MiB of HBM per device.

```python
import math
import jax
import jax.numpy as jnp
from jax import lax

D = 640
HEADS = 4
HEAD_DIM = 256
FF = 2048
WINDOW = 512
SEQS = 16
SEQ_LEN = 2048
PARAMS_A = 1640192
PARAMS_F = 3933440


def matrix_piece(piece_key, length, fan_in):
    base = jnp.clip(jax.random.normal(piece_key, (length,), jnp.float32), -4.0, 4.0)
    return base * fan_in ** (-0.5)


def gain_piece(piece_key, length, center, spread):
    return center + spread * jax.random.uniform(piece_key, (length,), jnp.float32, -1.0, 1.0)


def draw_attention_params(key, part):
    subkeys = jax.random.split(jax.random.fold_in(key, 11), 8)
    query_width = HEADS * HEAD_DIM
    pieces = [matrix_piece(subkeys[0], D * query_width, D), matrix_piece(subkeys[1], D * HEAD_DIM, D), matrix_piece(subkeys[2], D * HEAD_DIM, D), matrix_piece(subkeys[3], query_width * D, query_width), gain_piece(subkeys[4], D, 1.0, 0.3), gain_piece(subkeys[5], HEAD_DIM, 1.0, 0.3), gain_piece(subkeys[6], HEAD_DIM, 1.0, 0.3), gain_piece(subkeys[7], D, 1.0, 0.3)]
    return jnp.concatenate(pieces).astype(jnp.bfloat16)


def draw_feed_params(key, part):
    subkeys = jax.random.split(jax.random.fold_in(key, 23), 5)
    pieces = [matrix_piece(subkeys[0], D * FF, D), matrix_piece(subkeys[1], D * FF, D), matrix_piece(subkeys[2], FF * D, FF), gain_piece(subkeys[3], D, 1.0, 0.3), gain_piece(subkeys[4], D, 0.3, 0.15)]
    return jnp.concatenate(pieces).astype(jnp.bfloat16)


def draw_positions(key, part):
    starts = jax.random.randint(jax.random.fold_in(key, 37), (SEQS, 3), 1, SEQ_LEN)
    first_row = (jnp.arange(SEQS, dtype=jnp.int32) == 0)[:, None]
    starts = jnp.where(first_row, 0, starts)
    index = jnp.arange(SEQ_LEN, dtype=jnp.int32)
    marked = jnp.any(index[None, None, :] == starts[:, :, None], axis=1)
    latest = lax.cummax(jnp.where(marked, index[None, :], 0), axis=1)
    return (index[None, :] - latest).astype(jnp.int32)


def shard_levels(own_key, shape, cuts, least, top_value):
    factor_of = 1.0
    for axis_at, shards_of in cuts:
        draws = jax.random.uniform(jax.random.fold_in(jax.random.fold_in(own_key, 6), axis_at), (shards_of,), jnp.float32, least / len(cuts), top_value / len(cuts))
        factor_of = factor_of * jnp.repeat(jnp.exp(draws), shape[axis_at] // shards_of).reshape((-1,) + (1,) * (len(shape) - 1 - axis_at))
    return factor_of


def gaussian(rng, extent, deviation, reach, cuts=(), kind=jnp.bfloat16):
    entries = jax.random.normal(rng, extent, jnp.float32) * deviation
    if len(cuts) > 0:
        entries = shard_levels(rng, extent, cuts, -0.22, 0.18) * entries
    return jnp.clip(entries, min=-reach, max=reach).astype(kind)


def setup_inputs(seed: int = 0) -> dict:
    streams_of = jax.random.split(jax.random.key(seed), 6)
    tokens = gaussian(streams_of[0], (SEQS, SEQ_LEN, D), 1.0, 6.0, ((0, 2), (1, 16)))
    attention_params = draw_attention_params(jax.random.fold_in(streams_of[5], 71), 0)
    feed_params = draw_feed_params(jax.random.fold_in(streams_of[5], 71), 0)
    positions = draw_positions(jax.random.fold_in(streams_of[5], 71), 0)
    cotangent = gaussian(streams_of[4], (SEQS, SEQ_LEN, D), 1.0, 6.0, ((0, 2), (1, 16)))
    return dict(tokens=tokens, attention_params=attention_params, feed_params=feed_params, positions=positions, cotangent=cotangent)


@jax.custom_vjp
def low(v):
    return lax.optimization_barrier(v.astype(jnp.bfloat16)).astype(jnp.float32)

@jax.custom_vjp
def low_back(v):
    return v

def low_keep(v):
    return (low(v), None)

def low_pass(kept, grad):
    return (grad,)

def back_keep(v):
    return (v, None)

def back_low(kept, grad):
    return (low(grad),)
low.defvjp(low_keep, low_pass)
low_back.defvjp(back_keep, back_low)
epsilon = 1e-06
rope_base = 10000.0
highest = lax.Precision.HIGHEST

def rms_norm(vector, scaling):
    return vector * lax.rsqrt(lax.optimization_barrier(jnp.mean(vector * vector, axis=-1, keepdims=True)) + epsilon) * scaling

def rotate(vector, cosine_table, sine_table):
    half_width = vector.shape[-1] // 2
    first_half = vector[..., :half_width]
    second_half = vector[..., half_width:]
    return jnp.concatenate([first_half * cosine_table - second_half * sine_table, second_half * cosine_table + first_half * sine_table], axis=-1)

def angles(positions):
    half_width = HEAD_DIM // 2
    frequency = rope_base ** (-(jnp.arange(half_width, dtype=jnp.float32) * 2.0 / HEAD_DIM))
    turned = positions.astype(jnp.float32)[..., None] * frequency
    return (jnp.cos(turned), jnp.sin(turned))

def split_flat(flat_vector, layouts):
    pieces = []
    offset = 0
    for layout in layouts:
        length = math.prod(layout)
        pieces.append(flat_vector[offset:offset + length].reshape(layout))
        offset += length
    return pieces

def attention_layouts():
    query_width = HEADS * HEAD_DIM
    return [(D, query_width), (D, HEAD_DIM), (D, HEAD_DIM), (query_width, D), (D,), (HEAD_DIM,), (HEAD_DIM,), (D,)]

def feed_layouts():
    return [(D, FF), (D, FF), (FF, D), (D,), (D,)]

def attend(queries, key_rows, value_rows, positions):
    padding = jnp.zeros((WINDOW, HEAD_DIM), jnp.float32)
    padded_keys = jnp.concatenate([padding, key_rows], axis=0)
    padded_values = jnp.concatenate([padding, value_rows], axis=0)
    query_iota = jnp.arange(WINDOW, dtype=jnp.int32)
    key_iota = jnp.arange(2 * WINDOW, dtype=jnp.int32)
    distance = query_iota[:, None] + WINDOW - key_iota[None, :]
    score_scale = HEAD_DIM ** (-0.5)

    def one_block(block_start):
        block_queries = lax.dynamic_slice_in_dim(queries, block_start, WINDOW, 1)
        block_keys = lax.dynamic_slice_in_dim(padded_keys, block_start, 2 * WINDOW, 0)
        block_values = lax.dynamic_slice_in_dim(padded_values, block_start, 2 * WINDOW, 0)
        block_positions = lax.dynamic_slice_in_dim(positions, block_start, WINDOW, 0)
        logits = low_back(jnp.einsum('hqd,kd->hqk', block_queries, block_keys, precision=highest))
        allowed = (distance >= 0) & (distance < WINDOW) & (distance <= block_positions[:, None])
        scores = jnp.where(allowed[None], logits * score_scale, -1e+30)
        row_peak = lax.optimization_barrier(jnp.max(scores, axis=-1, keepdims=True))
        raised = jnp.exp(scores - row_peak)
        probability = raised / lax.optimization_barrier(jnp.sum(raised, axis=-1, keepdims=True))
        return jnp.einsum('hqk,kd->hqd', low(probability), block_values, precision=highest)
    starts = jnp.arange(SEQ_LEN // WINDOW, dtype=jnp.int32) * WINDOW
    blocks = lax.map(jax.checkpoint(one_block), starts)
    return jnp.transpose(blocks, (0, 2, 1, 3)).reshape(SEQ_LEN, HEADS * HEAD_DIM)

def layer_forward(inputs, attention_flat, feed_flat, positions):
    weight_query, weight_key, weight_value, weight_out, gain_attention, gain_query, gain_key, gain_post = split_flat(attention_flat, attention_layouts())
    cosine_table, sine_table = angles(positions)
    normed = low(rms_norm(inputs, gain_attention))
    query_raw = low_back(jnp.dot(normed, weight_query, precision=highest)).reshape(SEQ_LEN, HEADS, HEAD_DIM)
    key_raw = low_back(jnp.dot(normed, weight_key, precision=highest))
    value_raw = jnp.dot(normed, weight_value, precision=highest)
    queries = low(rotate(rms_norm(query_raw, gain_query), cosine_table[:, None, :], sine_table[:, None, :]))
    key_rows = low(rotate(rms_norm(key_raw, gain_key), cosine_table, sine_table))
    value_rows = low(low_back(value_raw))
    attended = attend(jnp.transpose(queries, (1, 0, 2)), key_rows, value_rows, positions)
    merged = low(low_back(attended))
    projected = low_back(jnp.dot(merged, weight_out, precision=highest))
    hidden_state = inputs + rms_norm(projected, gain_post)
    weight_gate, weight_up, weight_down, gain_feed, gain_out = split_flat(feed_flat, feed_layouts())
    feed_in = low(rms_norm(hidden_state, gain_feed))
    gate_values = low_back(jnp.dot(feed_in, weight_gate, precision=highest))
    up_values = low_back(jnp.dot(feed_in, weight_up, precision=highest))
    activation = low(jax.nn.gelu(gate_values, approximate=True) * up_values)
    down_values = low_back(jnp.dot(activation, weight_down, precision=highest))
    return hidden_state + rms_norm(down_values, gain_out)

def reference(tokens, attention_params, feed_params, positions, cotangent):
    attention_flat = attention_params.astype(jnp.float32)
    feed_flat = feed_params.astype(jnp.float32)

    def one_sequence(running, sequence_item):
        inputs, sequence_positions, sequence_cotangent = sequence_item

        def forward(inputs_arg, attention_arg, feed_arg):
            return layer_forward(inputs_arg, attention_arg, feed_arg, sequence_positions)
        output, pullback = jax.vjp(forward, inputs.astype(jnp.float32), attention_flat, feed_flat)
        grad_inputs, grad_attention, grad_feed = pullback(sequence_cotangent.astype(jnp.float32))
        return ((running[0] + grad_attention, running[1] + grad_feed), (output.astype(jnp.bfloat16), grad_inputs))
    start_state = (jnp.zeros((PARAMS_A,), jnp.float32), jnp.zeros((PARAMS_F,), jnp.float32))
    (grad_attention, grad_feed), (mixed, grad_tokens) = lax.scan(one_sequence, start_state, (tokens, positions, cotangent))
    return (mixed, grad_tokens, grad_attention, grad_feed)
```

```python
import functools
import math

import jax
import jax.numpy as jnp
import numpy as np
from jax import lax
from jax.experimental import pallas as pl
from jax.experimental.pallas import tpu as pltpu
from jax.sharding import PartitionSpec as P

MESH = pl.DeviceIdType.MESH
LANES = 128

D = 640
HEADS = 4
HEAD_DIM = 256
FF = 2048
WINDOW = 512


epsilon = 1e-06
rope_base = 10000.0


def shifted(block, axis, distance):
    devices = range(lax.axis_size(axis))
    route = [(i - distance, i) for i in devices if i - distance in devices]
    return lax.ppermute(block, axis, route)


def rms_norm(vector, scaling):
    return vector * lax.rsqrt(jnp.mean(vector * vector, axis=-1, keepdims=True) + epsilon) * scaling


def rotate(vector, cosine_table, sine_table):
    half_width = vector.shape[-1] // 2
    first_half = vector[..., :half_width]
    second_half = vector[..., half_width:]
    return jnp.concatenate(
        [
            first_half * cosine_table - second_half * sine_table,
            second_half * cosine_table + first_half * sine_table,
        ],
        axis=-1,
    )


def angles(positions):
    half_width = HEAD_DIM // 2
    frequency = rope_base ** (-(jnp.arange(half_width, dtype=jnp.float32) * 2.0 / HEAD_DIM))
    turned = positions.astype(jnp.float32)[..., None] * frequency
    return (jnp.cos(turned), jnp.sin(turned))


def split_flat(flat_vector, layouts):
    pieces = []
    offset = 0
    for layout in layouts:
        length = math.prod(layout)
        pieces.append(flat_vector[offset : offset + length].reshape(layout))
        offset += length
    return pieces


def attention_layouts():
    query_width = HEADS * HEAD_DIM
    return [
        (D, query_width),
        (D, HEAD_DIM),
        (D, HEAD_DIM),
        (query_width, D),
        (D,),
        (HEAD_DIM,),
        (HEAD_DIM,),
        (D,),
    ]


def feed_layouts():
    return [(D, FF), (D, FF), (FF, D), (D,), (D,)]


def contract_rows(left, right):
    return lax.dot_general(
        left, right, (((0,), (0,)), ((), ())), preferred_element_type=jnp.float32
    )


def contract_cols(left, right):
    return lax.dot_general(
        left, right, (((1,), (1,)), ((), ())), preferred_element_type=jnp.float32
    )


def flatten_all(arrays):
    return jnp.concatenate([array_item.reshape(-1) for array_item in arrays])


class Place:
    def __init__(self):
        self.devices_seq = lax.axis_size("seq")
        self.outer = self.devices_seq // 4
        self.count = 2 * self.devices_seq
        self.b = lax.axis_index("batch")
        s = lax.axis_index("seq")
        self.hi = lax.div(s, 4)
        self.y = lax.rem(lax.div(s, 2), 2)
        self.c = lax.rem(s, 2)

    def block(self, b, hi, y, c):
        return b * self.devices_seq + hi * 4 + y * 2 + c

    def seq_id(self, hi, y, c):
        return (self.b, hi * 4 + y * 2 + c)

    def mine(self):
        return self.block(self.b, self.hi, self.y, self.c)

    def x_peer(self):
        return (1 - self.b, self.hi * 4 + self.y * 2 + self.c)

    def y_peer(self):
        return self.seq_id(self.hi, 1 - self.y, self.c)

    def sibling(self):
        return self.seq_id(self.hi, self.y, 1 - self.c)

    def outer_at(self, k):
        return lax.rem(self.hi + k, self.outer)

    def outer_peer(self, k):
        return self.seq_id(self.outer_at(k), self.y, self.c)

    def peers(self):
        return [self.x_peer(), self.y_peer(), self.sibling()] + [
            self.outer_peer(k) for k in range(1, self.outer)
        ]


def greet(place):
    barrier = pltpu.get_barrier_semaphore()
    peers = place.peers()
    for peer in peers:
        pl.semaphore_signal(barrier, inc=1, device_id=peer, device_id_type=MESH)
    pl.semaphore_wait(barrier, len(peers))


class Wires:
    def __init__(self, send_sems, recv_sems):
        self.send_sems, self.recv_sems = send_sems, recv_sems
        self.used = 0
        self.sent = []

    def copy(self, src, dst, peer):
        made = pltpu.make_async_remote_copy(
            src_ref=src,
            dst_ref=dst,
            send_sem=self.send_sems.at[self.used],
            recv_sem=self.recv_sems.at[self.used],
            device_id=peer,
            device_id_type=MESH,
        )
        self.used += 1
        self.sent.append(made)
        made.start()
        return made

    def drain(self):
        for made in self.sent:
            made.wait_send()
        self.sent = []


def gather_wires(outer):
    return outer - 1 + 4 * outer + 4 * outer


class Gather:
    def __init__(self, place, wires, held, cut):
        self.place, self.wires, self.held, self.cut = place, wires, held, cut
        self.rows = held.shape[1]
        self.from_outer = {}
        self.from_x, self.from_y, self.diag, self.twin = {}, {}, {}, []

    def part(self, index, first=0, last=None):
        last = self.rows if last is None else last
        if first == 0 and last == self.rows:
            return self.held.at[index]
        return self.held.at[index, pl.ds(first, last - first)]

    def send(self, index, peer, first=0, last=None):
        ref = self.part(index, first, last)
        return self.wires.copy(ref, ref, peer)

    def begin(self):
        p = self.place
        for k in range(1, p.outer):
            self.from_outer[k] = self.send(p.mine(), p.outer_peer(k))
        self.spread(0)

    def spread(self, j):
        p = self.place
        if j:
            self.from_outer[j].wait_recv()
        index = p.block(p.b, p.outer_at(p.outer - j), p.y, p.c)
        self.from_y[j] = self.send(index, p.y_peer())
        self.from_x[j] = self.send(index, p.x_peer())
        self.twin.append(self.send(index, p.sibling()))

    def corner(self, j):
        p = self.place
        at = p.outer_at(p.outer - j)
        self.from_y[j].wait_recv()
        got = p.block(p.b, at, 1 - p.y, p.c)
        down = self.send(got, p.x_peer(), 0, self.cut)
        self.twin.append(self.send(got, p.sibling()))
        self.from_x[j].wait_recv()
        got = p.block(1 - p.b, at, p.y, p.c)
        across = self.send(got, p.y_peer(), self.cut)
        self.twin.append(self.send(got, p.sibling()))
        self.diag[j] = (down, across)

    def finish(self, j):
        p = self.place
        for made in self.diag[j]:
            made.wait_recv()
        self.twin.append(
            self.send(p.block(1 - p.b, p.outer_at(p.outer - j), 1 - p.y, p.c), p.sibling())
        )

    def end(self):
        for made in self.twin:
            made.wait_recv()


class Blocks:
    def __init__(self, length, count):
        self.length, self.count = length, count
        self.stride, self.rest = divmod(length, LANES)
        needed = -(-(length + self.rest * (count - 1)) // LANES)
        self.rows = -(-needed // 16) * 16
        self.tail = self.rows - self.stride
        self.total = length * count

    def pad(self, shard):
        return jnp.pad(shard, (0, self.rows * LANES - self.length)).reshape(self.rows, LANES)

    def take(self, block, index):
        return lax.dynamic_slice(block.reshape(-1), (self.rest * index,), (self.length,))

    def join(self, held):
        first = held[:, : self.stride]
        tails = jnp.concatenate([jnp.zeros_like(held[:1, self.stride :]), held[:-1, self.stride :]])
        top = first[:, : self.tail] + tails
        whole = jnp.concatenate([top, first[:, self.tail :]], axis=1).reshape(-1)
        return jnp.concatenate([whole, held[-1, self.stride :].reshape(-1)])[: self.total]

    def split(self, flat):
        room = self.count * self.stride * LANES + self.tail * LANES
        rows = jnp.pad(flat, (0, room - self.total)).reshape(-1, LANES)
        first = rows[: self.count * self.stride].reshape(self.count, self.stride, LANES)
        last = rows[self.count * self.stride :]
        tails = jnp.concatenate([first[1:, : self.tail], last[None]])
        return jnp.concatenate([first, tails], axis=1)


class Scatter:
    def __init__(self, place, wires, held, lands, result, first, last):
        self.place, self.wires, self.held, self.result = place, wires, held, result
        self.by_core, self.by_x, self.by_y, self.by_outer = lands
        self.first, self.last = first, last
        self.cut = first + (last - first) // 32 * 16

    def rows(self, first, last):
        return pl.ds(first, last - first)

    def add(self, index, land, at, first, last):
        rows = self.rows(first, last)
        self.held[index, rows] = (
            self.held[index, rows].astype(jnp.float32) + land[at, rows].astype(jnp.float32)
        ).astype(self.held.dtype)

    def core(self):
        p, rows = self.place, self.rows(self.first, self.last)
        self.from_core = []
        for i in range(2 * p.outer * 2):
            b, hi, y = i // (2 * p.outer), i // 2 % p.outer, i % 2
            self.from_core.append(
                self.wires.copy(
                    self.held.at[p.block(b, hi, y, 1 - p.c), rows],
                    self.by_core.at[i, rows],
                    p.sibling(),
                )
            )

    def plane(self):
        p = self.place
        for i, made in enumerate(self.from_core):
            b, hi, y = i // (2 * p.outer), i // 2 % p.outer, i % 2
            made.wait_recv()
            self.add(p.block(b, hi, y, p.c), self.by_core, i, self.first, self.last)
        self.from_x, self.from_y = [], []
        for i in range(2 * p.outer):
            hi, other = i // 2, i % 2
            rows = self.rows(self.first, self.cut)
            self.from_x.append(
                self.wires.copy(
                    self.held.at[p.block(1 - p.b, hi, other, p.c), rows],
                    self.by_x.at[i, rows],
                    p.x_peer(),
                )
            )
            rows = self.rows(self.cut, self.last)
            self.from_y.append(
                self.wires.copy(
                    self.held.at[p.block(other, hi, 1 - p.y, p.c), rows],
                    self.by_y.at[i, rows],
                    p.y_peer(),
                )
            )

    def cross(self):
        p = self.place
        for i, (made_x, made_y) in enumerate(zip(self.from_x, self.from_y)):
            hi, other = i // 2, i % 2
            made_x.wait_recv()
            self.add(p.block(p.b, hi, other, p.c), self.by_x, i, self.first, self.cut)
            made_y.wait_recv()
            self.add(p.block(other, hi, p.y, p.c), self.by_y, i, self.cut, self.last)
        self.over_x, self.over_y = [], []
        for hi in range(p.outer):
            rows = self.rows(self.first, self.cut)
            self.over_y.append(
                self.wires.copy(
                    self.held.at[p.block(p.b, hi, 1 - p.y, p.c), rows],
                    self.by_y.at[hi, rows],
                    p.y_peer(),
                )
            )
            rows = self.rows(self.cut, self.last)
            self.over_x.append(
                self.wires.copy(
                    self.held.at[p.block(1 - p.b, hi, p.y, p.c), rows],
                    self.by_x.at[hi, rows],
                    p.x_peer(),
                )
            )

    def column(self):
        p = self.place
        for hi in range(p.outer):
            index = p.block(p.b, hi, p.y, p.c)
            self.over_y[hi].wait_recv()
            self.add(index, self.by_y, hi, self.first, self.cut)
            self.over_x[hi].wait_recv()
            self.add(index, self.by_x, hi, self.cut, self.last)
        rows = self.rows(self.first, self.last)
        self.from_outer = []
        for k in range(1, p.outer):
            self.from_outer.append(
                self.wires.copy(
                    self.held.at[p.block(p.b, p.outer_at(k), p.y, p.c), rows],
                    self.by_outer.at[k - 1, rows],
                    p.outer_peer(k),
                )
            )

    def end(self):
        rows = self.rows(self.first, self.last)
        total = self.held[self.place.mine(), rows].astype(jnp.float32)
        for k, made in enumerate(self.from_outer):
            made.wait_recv()
            total = total + self.by_outer[k, rows].astype(jnp.float32)
        self.result[rows] = total


def scatter_wires(outer):
    return 4 * outer + 4 * outer + 2 * outer + outer - 1


def land_shapes(rows, outer):
    return [
        pltpu.VMEM((4 * outer, rows, LANES), jnp.bfloat16),
        pltpu.VMEM((2 * outer, rows, LANES), jnp.bfloat16),
        pltpu.VMEM((2 * outer, rows, LANES), jnp.bfloat16),
        pltpu.VMEM((outer - 1, rows, LANES), jnp.bfloat16),
    ]


def scatter_kernel(pieces, attention_held, feed_held, attention_out, feed_out, *scratch):
    lands_attention, lands_feed, (send, recv) = scratch[:4], scratch[4:8], scratch[8:]
    place = Place()
    greet(place)
    wires = Wires(send, recv)
    parts = []
    for which, first, last in pieces:
        held, lands, out = (
            (attention_held, lands_attention, attention_out)
            if which == 0
            else (feed_held, lands_feed, feed_out)
        )
        parts.append(Scatter(place, wires, held, lands, out, first, last))
    stages = [Scatter.core, Scatter.plane, Scatter.cross, Scatter.column, Scatter.end]
    for step in range(len(parts) + len(stages) - 1):
        for at in reversed(range(len(stages))):
            if 0 <= step - at < len(parts):
                stages[at](parts[step - at])
    wires.drain()


def scatter_all(attention_held, feed_held, outer):
    rows = [attention_held.shape[1], feed_held.shape[1]]
    middle = rows[1] // 32 * 16
    pieces = [(1, 0, middle), (1, middle, rows[1]), (0, 0, rows[0])]
    wires = len(pieces) * scatter_wires(outer)
    return pl.pallas_call(
        functools.partial(scatter_kernel, pieces),
        out_shape=[jax.ShapeDtypeStruct((count, LANES), jnp.float32) for count in rows],
        in_specs=[pl.BlockSpec(memory_space=pltpu.VMEM)] * 2,
        out_specs=[pl.BlockSpec(memory_space=pltpu.VMEM)] * 2,
        scratch_shapes=land_shapes(rows[0], outer)
        + land_shapes(rows[1], outer)
        + [pltpu.SemaphoreType.DMA((wires,)), pltpu.SemaphoreType.DMA((wires,))],
        compiler_params=pltpu.CompilerParams(
            collective_id=1, has_side_effects=True, vmem_limit_bytes=56 << 20
        ),
    )(attention_held, feed_held)


EPS = 1e-06


def root_inverse(rows):
    return lax.rsqrt(jnp.mean(rows * rows, axis=-1, keepdims=True) + EPS)


def turn(rows, cosine, sine):
    half = rows.shape[-1] // 2
    first, second = rows[:, :half], rows[:, half:]
    return jnp.concatenate([first * cosine - second * sine, second * cosine + first * sine], axis=-1)


def turn_back(rows, cosine, sine):
    half = rows.shape[-1] // 2
    first, second = rows[:, :half], rows[:, half:]
    return jnp.concatenate([first * cosine + second * sine, second * cosine - first * sine], axis=-1)


def dot_nn(left, right):
    return jnp.dot(left, right, preferred_element_type=jnp.float32)


def dot_nt(left, right):
    return lax.dot_general(left, right, (((1,), (1,)), ((), ())), preferred_element_type=jnp.float32)


def dot_tn(left, right):
    return lax.dot_general(left, right, (((0,), (0,)), ((), ())), preferred_element_type=jnp.float32)


def align_shard(blocks, place, padded_ref, shifted, aligned):
    offset = blocks.rest * place.mine()
    down, right = lax.div(offset, LANES), lax.rem(offset, LANES)
    rows = blocks.rows
    shifted[0:16] = jnp.zeros((16, LANES), jnp.float32)
    shifted[16 : 16 + rows] = pltpu.roll(padded_ref[...].astype(jnp.float32), right, 1)
    lane = lax.broadcasted_iota(jnp.int32, (rows, LANES), 1)
    aligned[...] = jnp.where(
        lane >= right, shifted[pl.ds(16 - down, rows)], shifted[pl.ds(15 - down, rows)]
    ).astype(aligned.dtype)


def flatten_held(blocks, held, flat):
    stride, tail, rows = blocks.stride, blocks.tail, blocks.rows
    if stride % 16 == 0 and tail == 16:
        flat[0:tail] = held[0, 0:tail].astype(jnp.float32)
        flat[tail:rows] = held[0, tail:rows].astype(jnp.float32)

        def body(d, carry):
            start = pl.multiple_of(d * stride, 16)
            flat[pl.ds(start, tail)] += held[d, 0:tail].astype(jnp.float32)
            start = pl.multiple_of(d * stride + tail, 16)
            flat[pl.ds(start, stride)] = held[d, tail:rows].astype(jnp.float32)
            return carry

        lax.fori_loop(1, blocks.count, body, 0)
    else:
        flat[...] = jnp.zeros_like(flat)

        def body(d, carry):
            flat[pl.ds(d * stride, rows)] += held[d].astype(jnp.float32)
            return carry

        lax.fori_loop(0, blocks.count, body, 0)


def unflatten(flat, base, matrix, first, width):
    height, steps = matrix.shape[0], width // LANES
    for i in range(steps):
        matrix[:, first + i * LANES : first + (i + 1) * LANES] = flat[
            pl.ds(base + i, height, stride=steps), :
        ].astype(matrix.dtype)


def read_gain(flat, base, width):
    return jnp.concatenate([flat[base + i : base + i + 1, :] for i in range(width // LANES)], axis=-1)


class Halo:
    def __init__(self, place, wires, kv, block, first, size):
        self.place, self.wires, self.kv, self.block = place, wires, kv, block
        self.first, self.size = first, size

    def slot(self, at):
        return self.kv.at[pl.ds(self.first, self.size), pl.ds(pl.multiple_of(at * self.block, 128), self.block)]

    def outward(self):
        p = self.place
        self.outer = self.wires.copy(self.slot(4), self.slot(0), p.outer_peer(1))

    def plane(self):
        p = self.place
        self.outer.wait_recv()
        self.across = self.wires.copy(self.slot(4 * (1 - p.y)), self.slot(2), p.y_peer())
        self.near = self.wires.copy(self.slot(4 * (1 - p.c)), self.slot(3 - 2 * p.c), p.sibling())

    def relay(self):
        p = self.place
        self.across.wait_recv()
        self.far = self.wires.copy(self.slot(2), self.slot(1 + 2 * p.c), p.sibling())

    def end(self):
        self.near.wait_recv()
        self.far.wait_recv()


HALO_WIRES = 4


class Locals:
    def __init__(self, sems):
        self.sems, self.used, self.open = sems, 0, []

    def copy(self, src, dst):
        made = pltpu.make_async_copy(src, dst, self.sems.at[self.used])
        self.used += 1
        self.open.append(made)
        made.start()
        return made

    def finish(self, made):
        made.wait()
        self.open.remove(made)

    def drain(self):
        for made in self.open:
            made.wait()
        self.open = []


class Geo:
    def __init__(self, tokens, attention_params, feed_params):
        self.seqs, self.block = tokens.shape[:2]
        self.rows = self.seqs * self.block
        self.count = lax.axis_size("batch") * lax.axis_size("seq")
        self.outer = lax.axis_size("seq") // 4
        self.attention = Blocks(attention_params.shape[0], self.count)
        self.feed = Blocks(feed_params.shape[0], self.count)
        self.reach = 5 * self.block


QUERY = HEADS * HEAD_DIM
BASE_KEY = D * QUERY // LANES
BASE_VALUE = BASE_KEY + D * HEAD_DIM // LANES
BASE_OUT = BASE_VALUE + D * HEAD_DIM // LANES
BASE_GAINS = BASE_OUT + QUERY * D // LANES
STEP = 256


def forward_kernel(geo, tokens, positions, frequency, attention_in, feed_in, *refs):
    (
        feed_held,
        out_wqkv,
        out_wo,
        out_gains,
        out_q,
        out_kv,
        out_merged,
        out_projected,
        out_hidden,
        out_cosine,
        out_sine,
    ) = refs[:11]
    (
        held,
        own_feed,
        shifted,
        flat,
        wqkv,
        wo,
        gains,
        cosine,
        sine,
        lows,
        normed,
        q,
        kv,
        scores,
        probs,
        merged,
        projected,
        hidden,
        send,
        recv,
        local,
    ) = refs[11:]
    place = Place()
    wires, locals_ = Wires(send, recv), Locals(local)
    seqs, block, reach = geo.seqs, geo.block, geo.reach
    align_shard(geo.attention, place, attention_in, shifted, held.at[place.mine()])
    align_shard(geo.feed, place, feed_in, shifted, own_feed)
    lead = locals_.copy(own_feed, feed_held.at[place.mine()])
    greet(place)
    gather_a = Gather(place, wires, held, geo.attention.rows // 32 * 16)
    gather_f = Gather(place, wires, feed_held, geo.feed.rows // 32 * 16)
    gather_a.begin()

    columns = positions[...].astype(jnp.float32).T
    row = lax.broadcasted_iota(jnp.int32, (block, LANES), 0)
    for s in range(seqs):
        spot = columns[:, s : s + 1]
        angle = spot * frequency[...]
        rows = slice(s * block, (s + 1) * block)
        cosine[rows] = jnp.cos(angle)
        sine[rows] = jnp.sin(angle)
        lows[s] = jnp.maximum(row + 1, row + WINDOW - spot.astype(jnp.int32))

    gather_a.corner(0)
    for j in range(1, geo.outer):
        gather_a.spread(j)
        gather_a.corner(j)
        gather_a.finish(j - 1)
    gather_a.finish(geo.outer - 1)
    locals_.finish(lead)
    gather_f.begin()
    gather_a.end()
    pending = [functools.partial(gather_f.corner, 0)]
    for j in range(1, geo.outer):
        pending.append(functools.partial(gather_f.spread, j))
        pending.append(functools.partial(gather_f.corner, j))
        pending.append(functools.partial(gather_f.finish, j - 1))
    pending.append(functools.partial(gather_f.finish, geo.outer - 1))

    def tick(amount=1):
        for _ in range(amount):
            if pending:
                pending.pop(0)()

    flatten_held(geo.attention, held, flat)
    at = BASE_GAINS
    for i, width in enumerate((D, HEAD_DIM, HEAD_DIM, D)):
        gains[i : i + 1, :width] = read_gain(flat, at, width)
        at += width // LANES
    unflatten(flat, BASE_KEY, wqkv, QUERY, HEAD_DIM)
    unflatten(flat, BASE_VALUE, wqkv, QUERY + HEAD_DIM, HEAD_DIM)
    gain = gains[0:1, :]
    gain_key = gains[2:3, :HEAD_DIM]
    halos = []
    per_step = STEP // block
    for s in range(0, seqs, per_step):
        rows = slice(s * block, (s + per_step) * block)
        x = tokens[rows].astype(jnp.float32)
        normed[rows] = (x * root_inverse(x) * gain).astype(jnp.bfloat16)
        made = dot_nn(normed[rows], wqkv[:, QUERY:])
        keys = made[:, :HEAD_DIM]
        keys = turn(keys * root_inverse(keys) * gain_key, cosine[rows], sine[rows])
        for i in range(per_step):
            part = slice(i * block, (i + 1) * block)
            kv[s + i, reach - block :, :HEAD_DIM] = keys[part].astype(jnp.bfloat16)
            kv[s + i, reach - block :, HEAD_DIM:] = made[part, HEAD_DIM:].astype(jnp.bfloat16)
        if (s + per_step) % (seqs // 2) == 0:
            halo = Halo(place, wires, kv, block, s + per_step - seqs // 2, seqs // 2)
            halo.outward()
            halos.append(halo)
    unflatten(flat, 0, wqkv, 0, QUERY)
    tick(2)
    gain_query = gains[1:2, :HEAD_DIM] * HEAD_DIM**-0.5
    for s in range(0, seqs, per_step):
        rows = slice(s * block, (s + per_step) * block)
        made = dot_nn(normed[rows], wqkv[:, :QUERY])
        for h in range(HEADS):
            one = made[:, h * HEAD_DIM : (h + 1) * HEAD_DIM]
            one = turn(one * root_inverse(one) * gain_query, cosine[rows], sine[rows])
            q[h, rows] = one.astype(jnp.bfloat16)
        tick()
    unflatten(flat, BASE_OUT, wo, 0, D)
    for src, dst in (
        (wqkv, out_wqkv),
        (wo, out_wo),
        (gains, out_gains),
        (q, out_q),
        (cosine, out_cosine),
        (sine, out_sine),
    ):
        locals_.copy(src, dst)
    for halo in halos:
        halo.plane()
    tick()
    for halo in halos:
        halo.relay()
    tick()

    chunk = 32
    lane = lax.broadcasted_iota(jnp.int32, (chunk, reach), 1)
    over = lax.broadcasted_iota(jnp.int32, (chunk, reach), 1) - lax.broadcasted_iota(
        jnp.int32, (chunk, reach), 0
    )

    def attend(s, carry):
        start = pl.multiple_of(s * block, block)
        rows = pl.ds(start, block)
        queries = q[:, rows, :].reshape(HEADS * block, HEAD_DIM)
        scores[...] = dot_nt(queries, kv[s, :, :HEAD_DIM])
        for r in range(0, HEADS * block, chunk):
            i = r % block
            low = jnp.concatenate([lows[s, i : i + chunk, :]] * (reach // LANES), axis=-1)
            seen = (lane >= low) & (over <= WINDOW + i)
            raised = jnp.where(seen, jnp.exp(scores[r : r + chunk]), 0.0)
            share = 1.0 / jnp.sum(raised, axis=-1, keepdims=True)
            probs[r : r + chunk] = (raised * share).astype(jnp.bfloat16)
        made = dot_nn(probs[...], kv[s, :, HEAD_DIM:])
        for h in range(HEADS):
            merged[rows, h * HEAD_DIM : (h + 1) * HEAD_DIM] = made[
                h * block : (h + 1) * block
            ].astype(jnp.bfloat16)
        return carry

    halves = seqs // 2
    for g, halo in enumerate(halos):
        halo.end()
        for first in range(g * halves, (g + 1) * halves, 2):
            lax.fori_loop(first, first + 2, attend, 0)
            tick()
    locals_.copy(kv, out_kv)
    locals_.copy(merged, out_merged)
    gain_post = gains[3:4, :]
    for s in range(0, seqs, per_step):
        rows = slice(s * block, (s + per_step) * block)
        made = dot_nn(merged[rows], wo[...])
        projected[rows] = made
        hidden[rows] = tokens[rows].astype(jnp.float32) + made * root_inverse(made) * gain_post
        locals_.copy(projected.at[rows], out_projected.at[rows])
        locals_.copy(hidden.at[rows], out_hidden.at[rows])
    tick(len(pending))
    gather_f.end()
    wires.drain()
    locals_.drain()


def vmem(shape, dtype):
    return pltpu.VMEM(shape, dtype)


def forward_pass(geo, tokens, positions, attention_block, feed_block):
    count, rows, seqs, block = geo.count, geo.rows, geo.seqs, geo.block
    bf, f4 = jnp.bfloat16, jnp.float32
    half = HEAD_DIM // 2
    frequency = (
        rope_base ** (-(np.arange(half, dtype=np.float32) * np.float32(2.0) / HEAD_DIM))
    ).astype(np.float32)[None]
    wires = 2 * gather_wires(geo.outer) + 2 * HALO_WIRES
    outs = [
        ((count, geo.feed.rows, LANES), bf),
        ((D, QUERY + 2 * HEAD_DIM), bf),
        ((QUERY, D), bf),
        ((8, D), f4),
        ((HEADS, rows, HEAD_DIM), bf),
        ((seqs, geo.reach, 2 * HEAD_DIM), bf),
        ((rows, QUERY), bf),
        ((rows, D), f4),
        ((rows, D), f4),
        ((rows, half), f4),
        ((rows, half), f4),
    ]
    flat_rows = geo.attention.count * geo.attention.stride + geo.attention.tail
    return pl.pallas_call(
        functools.partial(forward_kernel, geo),
        out_shape=[jax.ShapeDtypeStruct(*out) for out in outs],
        in_specs=[pl.BlockSpec(memory_space=pltpu.VMEM)] * 5,
        out_specs=[pl.BlockSpec(memory_space=pl.ANY)] * len(outs),
        scratch_shapes=[
            vmem((count, geo.attention.rows, LANES), bf),
            vmem((geo.feed.rows, LANES), bf),
            vmem((16 + geo.feed.rows, LANES), f4),
            vmem((flat_rows, LANES), f4),
            vmem((D, QUERY + 2 * HEAD_DIM), bf),
            vmem((QUERY, D), bf),
            vmem((8, D), f4),
            vmem((rows, half), f4),
            vmem((rows, half), f4),
            vmem((seqs, block, LANES), jnp.int32),
            vmem((rows, D), bf),
            vmem((HEADS, rows, HEAD_DIM), bf),
            vmem((seqs, geo.reach, 2 * HEAD_DIM), bf),
            vmem((HEADS * block, geo.reach), f4),
            vmem((HEADS * block, geo.reach), bf),
            vmem((rows, QUERY), bf),
            vmem((rows, D), f4),
            vmem((rows, D), f4),
            pltpu.SemaphoreType.DMA((wires,)),
            pltpu.SemaphoreType.DMA((wires,)),
            pltpu.SemaphoreType.DMA((32,)),
        ],
        compiler_params=pltpu.CompilerParams(
            collective_id=0, has_side_effects=True, vmem_limit_bytes=60 << 20
        ),
    )(tokens.reshape(rows, D), positions, jnp.asarray(frequency), attention_block, feed_block)


def on_device(tokens, attention_params, feed_params, positions, cotangent):
    seq_count, block, model_width = tokens.shape
    total_rows = seq_count * block
    halo_rows = WINDOW - 1
    hop_count = -(-halo_rows // block)
    needed_rows = [
        min(block, halo_rows - (hop_index - 1) * block) for hop_index in range(1, hop_count + 1)
    ]
    halo_starts = {}
    cursor = 0
    for hop_index in range(hop_count, 0, -1):
        halo_starts[hop_index] = cursor
        cursor += needed_rows[hop_index - 1]
    geo = Geo(tokens, attention_params, feed_params)
    device = lax.axis_index("batch") * lax.axis_size("seq") + lax.axis_index("seq")
    (
        feed_held, wqkv, weight_out, gains, q, kv, merged, projected, hidden_state,
        cosine_table, sine_table,
    ) = forward_pass(
        geo, tokens, positions, geo.attention.pad(attention_params), geo.feed.pad(feed_params)
    )
    feed_flat = geo.feed.join(feed_held)
    weight_query, weight_key, weight_value = wqkv[:, :QUERY], wqkv[:, QUERY:QUERY+HEAD_DIM], wqkv[:, QUERY+HEAD_DIM:]
    gain_attention, gain_query, gain_key, gain_post = gains[0], gains[1, :HEAD_DIM], gains[2, :HEAD_DIM], gains[3]
    inputs = tokens.astype(jnp.float32).reshape(total_rows, model_width)

    def query_prep(raw_rows, scaling):
        return rotate(rms_norm(raw_rows, scaling), cosine_table[:, None, :], sine_table[:, None, :])

    def key_prep(raw_rows, scaling):
        return rotate(rms_norm(raw_rows, scaling), cosine_table, sine_table)

    normed = rms_norm(inputs, gain_attention).astype(jnp.bfloat16)
    query_raw = jnp.dot(normed, weight_query, preferred_element_type=jnp.float32).reshape(
        total_rows, HEADS, HEAD_DIM
    )
    key_raw = jnp.dot(normed, weight_key, preferred_element_type=jnp.float32)
    queries = (q.transpose(1, 0, 2) * 16).reshape(seq_count, block, HEADS, HEAD_DIM)
    extended_keys, extended_values = kv[:, 1:, :HEAD_DIM], kv[:, 1:, HEAD_DIM:]
    extended_len = halo_rows + block
    distance = (
        jnp.arange(block, dtype=jnp.int32)[:, None]
        + halo_rows
        - jnp.arange(extended_len, dtype=jnp.int32)[None, :]
    )
    allowed = (distance >= 0) & (distance < WINDOW)
    allowed = allowed[None] & (distance[None] <= positions[:, :, None])
    allowed = allowed[:, None]
    score_scale = HEAD_DIM ** (-0.5)

    def score_of(query_block, key_block):
        logits = jnp.einsum(
            "sqhd,skd->shqk", query_block, key_block, preferred_element_type=jnp.float32
        )
        return jnp.where(allowed, logits * score_scale, -1e30)

    weight_gate, weight_up, weight_down, gain_feed, gain_out = split_flat(feed_flat, feed_layouts())
    gain_feed = gain_feed.astype(jnp.float32)
    gain_out = gain_out.astype(jnp.float32)

    def gated(gate_values, up_values):
        return jax.nn.gelu(gate_values, approximate=True) * up_values

    feed_in = rms_norm(hidden_state, gain_feed).astype(jnp.bfloat16)
    gate_values = jnp.dot(feed_in, weight_gate, preferred_element_type=jnp.float32)
    up_values = jnp.dot(feed_in, weight_up, preferred_element_type=jnp.float32)
    activation = gated(gate_values, up_values).astype(jnp.bfloat16)
    down_values = jnp.dot(activation, weight_down, preferred_element_type=jnp.float32)
    output = hidden_state + rms_norm(down_values, gain_out)
    mixed = output.astype(jnp.bfloat16).reshape(seq_count, block, model_width)
    grad_output = cotangent.astype(jnp.float32).reshape(total_rows, model_width)
    unused, pullback = jax.vjp(rms_norm, down_values, gain_out)
    grad_down, grad_gain_out = pullback(grad_output)
    grad_down = grad_down.astype(jnp.bfloat16)
    grad_weight_down = contract_rows(activation, grad_down)
    grad_activation = contract_cols(grad_down, weight_down)
    unused, pullback = jax.vjp(gated, gate_values, up_values)
    grad_gate, grad_up = pullback(grad_activation)
    grad_gate = grad_gate.astype(jnp.bfloat16)
    grad_up = grad_up.astype(jnp.bfloat16)
    grad_weight_gate = contract_rows(feed_in, grad_gate)
    grad_weight_up = contract_rows(feed_in, grad_up)
    grad_feed_in = contract_cols(grad_gate, weight_gate) + contract_cols(grad_up, weight_up)
    unused, pullback = jax.vjp(rms_norm, hidden_state, gain_feed)
    grad_hidden_part, grad_gain_feed = pullback(grad_feed_in)
    grad_hidden = grad_output + grad_hidden_part
    feed_grads = flatten_all(
        [grad_weight_gate, grad_weight_up, grad_weight_down, grad_gain_feed, grad_gain_out]
    )
    unused, pullback = jax.vjp(rms_norm, projected, gain_post)
    grad_projected, grad_gain_post = pullback(grad_hidden)
    grad_projected = grad_projected.astype(jnp.bfloat16)
    grad_weight_out = contract_rows(merged, grad_projected)
    grad_merged = (
        contract_cols(grad_projected, weight_out)
        .astype(jnp.bfloat16)
        .reshape(seq_count, block, HEADS, HEAD_DIM)
    )
    scores = score_of(queries, extended_keys)
    probability = jax.nn.softmax(scores, axis=-1)
    weights_rounded = probability.astype(jnp.bfloat16)
    grad_probs = jnp.einsum(
        "sqhd,skd->shqk", grad_merged, extended_values, preferred_element_type=jnp.float32
    )
    inner = jnp.sum(probability * grad_probs, axis=-1, keepdims=True)
    grad_logits = (probability * (grad_probs - inner) * score_scale).astype(jnp.bfloat16)
    grad_queries = jnp.einsum(
        "shqk,skd->sqhd", grad_logits, extended_keys, preferred_element_type=jnp.float32
    )
    grad_ext_keys = jnp.einsum(
        "shqk,sqhd->skd", grad_logits, queries, preferred_element_type=jnp.float32
    )
    grad_ext_values = jnp.einsum(
        "shqk,sqhd->skd", weights_rounded, grad_merged, preferred_element_type=jnp.float32
    )

    def halo_part(array_item, hop_index):
        first_row = halo_starts[hop_index]
        return array_item[:, first_row : first_row + needed_rows[hop_index - 1]]

    local_keys_grad = grad_ext_keys[:, halo_rows:]
    local_values_grad = grad_ext_values[:, halo_rows:]
    for hop_index in range(1, hop_count + 1):
        needed = needed_rows[hop_index - 1]
        back_keys, back_values = (
            shifted(
                halo_part(grad_ext_keys, hop_index).astype(jnp.bfloat16), "seq", -hop_index
            ).astype(jnp.float32),
            shifted(
                halo_part(grad_ext_values, hop_index).astype(jnp.bfloat16), "seq", -hop_index
            ).astype(jnp.float32),
        )
        local_keys_grad = local_keys_grad.at[:, block - needed :].add(back_keys)
        local_values_grad = local_values_grad.at[:, block - needed :].add(back_values)
    unused, pullback = jax.vjp(query_prep, query_raw, gain_query)
    grad_query_raw, grad_gain_query = pullback(grad_queries.reshape(total_rows, HEADS, HEAD_DIM))
    grad_query_raw = grad_query_raw.reshape(total_rows, HEADS * HEAD_DIM).astype(jnp.bfloat16)
    unused, pullback = jax.vjp(key_prep, key_raw, gain_key)
    grad_key_raw, grad_gain_key = pullback(local_keys_grad.reshape(total_rows, HEAD_DIM))
    grad_key_raw = grad_key_raw.astype(jnp.bfloat16)
    grad_value_raw = local_values_grad.reshape(total_rows, HEAD_DIM).astype(jnp.bfloat16)
    grad_weight_query = contract_rows(normed, grad_query_raw)
    grad_weight_key = contract_rows(normed, grad_key_raw)
    grad_weight_value = contract_rows(normed, grad_value_raw)
    grad_normed = (
        contract_cols(grad_query_raw, weight_query)
        + contract_cols(grad_key_raw, weight_key)
        + contract_cols(grad_value_raw, weight_value)
    )
    unused, pullback = jax.vjp(rms_norm, inputs, gain_attention)
    grad_input_part, grad_gain_attention = pullback(grad_normed)
    grad_tokens = (grad_hidden + grad_input_part).reshape(seq_count, block, model_width)
    attention_grads = flatten_all(
        [
            grad_weight_query,
            grad_weight_key,
            grad_weight_value,
            grad_weight_out,
            grad_gain_attention,
            grad_gain_query,
            grad_gain_key,
            grad_gain_post,
        ]
    )
    attention_sum, feed_sum = scatter_all(
        geo.attention.split(attention_grads).astype(jnp.bfloat16),
        geo.feed.split(feed_grads).astype(jnp.bfloat16),
        geo.outer,
    )
    attention_piece = geo.attention.take(attention_sum, device)
    feed_piece = geo.feed.take(feed_sum, device)
    return (mixed, grad_tokens, attention_piece, feed_piece)


def solution(mesh):
    return jax.shard_map(
        on_device,
        mesh=mesh,
        in_specs=(
            P("batch", "seq", None),
            P(("batch", "seq")),
            P(("batch", "seq")),
            P("batch", "seq"),
            P("batch", "seq", None),
        ),
        out_specs=(
            P("batch", "seq", None),
            P("batch", "seq", None),
            P(("batch", "seq")),
            P(("batch", "seq")),
        ),
        check_vma=False,
    )
```

```python
import functools
import math

import jax
import jax.numpy as jnp
import numpy as np
from jax import lax
from jax.experimental import pallas as pl
from jax.experimental.pallas import tpu as pltpu
from jax.sharding import PartitionSpec as P

MESH = pl.DeviceIdType.MESH
LANES = 128

D = 640
HEADS = 4
HEAD_DIM = 256
FF = 2048
WINDOW = 512


rope_base = 10000.0


class Place:
    def __init__(self):
        self.devices_seq = lax.axis_size("seq")
        self.outer = self.devices_seq // 4
        self.count = 2 * self.devices_seq
        self.b = lax.axis_index("batch")
        s = lax.axis_index("seq")
        self.hi = lax.div(s, 4)
        self.y = lax.rem(lax.div(s, 2), 2)
        self.c = lax.rem(s, 2)

    def block(self, b, hi, y, c):
        return b * self.devices_seq + hi * 4 + y * 2 + c

    def seq_id(self, hi, y, c):
        return (self.b, hi * 4 + y * 2 + c)

    def mine(self):
        return self.block(self.b, self.hi, self.y, self.c)

    def x_peer(self):
        return (1 - self.b, self.hi * 4 + self.y * 2 + self.c)

    def y_peer(self):
        return self.seq_id(self.hi, 1 - self.y, self.c)

    def sibling(self):
        return self.seq_id(self.hi, self.y, 1 - self.c)

    def outer_at(self, k):
        return lax.rem(self.hi + k, self.outer)

    def outer_peer(self, k):
        return self.seq_id(self.outer_at(k), self.y, self.c)

    def peers(self):
        return [self.x_peer(), self.y_peer(), self.sibling()] + [
            self.outer_peer(k) for k in range(1, self.outer)
        ]


def greet(place):
    barrier = pltpu.get_barrier_semaphore()
    peers = place.peers()
    for peer in peers:
        pl.semaphore_signal(barrier, inc=1, device_id=peer, device_id_type=MESH)
    pl.semaphore_wait(barrier, len(peers))


class Wires:
    def __init__(self, send_sems, recv_sems):
        self.send_sems, self.recv_sems = send_sems, recv_sems
        self.used = 0
        self.sent = []

    def copy(self, src, dst, peer):
        made = pltpu.make_async_remote_copy(
            src_ref=src,
            dst_ref=dst,
            send_sem=self.send_sems.at[self.used],
            recv_sem=self.recv_sems.at[self.used],
            device_id=peer,
            device_id_type=MESH,
        )
        self.used += 1
        self.sent.append(made)
        made.start()
        return made

    def drain(self):
        for made in self.sent:
            made.wait_send()
        self.sent = []


def gather_wires(outer):
    return outer - 1 + 4 * outer + 4 * outer


class Gather:
    def __init__(self, place, wires, held, cut):
        self.place, self.wires, self.held, self.cut = place, wires, held, cut
        self.rows = held.shape[1]
        self.from_outer = {}
        self.from_x, self.from_y, self.diag, self.twin = {}, {}, {}, []

    def part(self, index, first=0, last=None):
        last = self.rows if last is None else last
        if first == 0 and last == self.rows:
            return self.held.at[index]
        return self.held.at[index, pl.ds(first, last - first)]

    def send(self, index, peer, first=0, last=None):
        ref = self.part(index, first, last)
        return self.wires.copy(ref, ref, peer)

    def begin(self):
        p = self.place
        for k in range(1, p.outer):
            self.from_outer[k] = self.send(p.mine(), p.outer_peer(k))
        self.spread(0)

    def spread(self, j):
        p = self.place
        if j:
            self.from_outer[j].wait_recv()
        index = p.block(p.b, p.outer_at(p.outer - j), p.y, p.c)
        self.from_y[j] = self.send(index, p.y_peer())
        self.from_x[j] = self.send(index, p.x_peer())
        self.twin.append(self.send(index, p.sibling()))

    def corner(self, j):
        p = self.place
        at = p.outer_at(p.outer - j)
        self.from_y[j].wait_recv()
        got = p.block(p.b, at, 1 - p.y, p.c)
        down = self.send(got, p.x_peer(), 0, self.cut)
        self.twin.append(self.send(got, p.sibling()))
        self.from_x[j].wait_recv()
        got = p.block(1 - p.b, at, p.y, p.c)
        across = self.send(got, p.y_peer(), self.cut)
        self.twin.append(self.send(got, p.sibling()))
        self.diag[j] = (down, across)

    def finish(self, j):
        p = self.place
        for made in self.diag[j]:
            made.wait_recv()
        self.twin.append(
            self.send(p.block(1 - p.b, p.outer_at(p.outer - j), 1 - p.y, p.c), p.sibling())
        )

    def end(self):
        for made in self.twin:
            made.wait_recv()


class Blocks:
    def __init__(self, length, count):
        self.length, self.count = length, count
        self.stride, self.rest = divmod(length, LANES)
        needed = -(-(length + self.rest * (count - 1)) // LANES)
        self.rows = -(-needed // 16) * 16
        self.tail = self.rows - self.stride
        self.total = length * count

    def pad(self, shard):
        return jnp.pad(shard, (0, self.rows * LANES - self.length)).reshape(self.rows, LANES)

    def take(self, block, index):
        return lax.dynamic_slice(block.reshape(-1), (self.rest * index,), (self.length,))


EPS = 1e-06


def root_inverse(rows):
    return lax.rsqrt(jnp.mean(rows * rows, axis=-1, keepdims=True) + EPS)


def turn(rows, cosine, sine):
    half = rows.shape[-1] // 2
    first, second = rows[:, :half], rows[:, half:]
    return jnp.concatenate([first * cosine - second * sine, second * cosine + first * sine], axis=-1)


def turn_back(rows, cosine, sine):
    half = rows.shape[-1] // 2
    first, second = rows[:, :half], rows[:, half:]
    return jnp.concatenate([first * cosine + second * sine, second * cosine - first * sine], axis=-1)


def dot_nn(left, right):
    return jnp.dot(left, right, preferred_element_type=jnp.float32)


def dot_nt(left, right):
    return lax.dot_general(left, right, (((1,), (1,)), ((), ())), preferred_element_type=jnp.float32)


def dot_tn(left, right):
    return lax.dot_general(left, right, (((0,), (0,)), ((), ())), preferred_element_type=jnp.float32)


def align_shard(blocks, place, padded_ref, shifted, aligned):
    offset = blocks.rest * place.mine()
    down, right = lax.div(offset, LANES), lax.rem(offset, LANES)
    rows = blocks.rows
    shifted[0:16] = jnp.zeros((16, LANES), jnp.float32)
    shifted[16 : 16 + rows] = pltpu.roll(padded_ref[...].astype(jnp.float32), right, 1)
    lane = lax.broadcasted_iota(jnp.int32, (rows, LANES), 1)
    aligned[...] = jnp.where(
        lane >= right, shifted[pl.ds(16 - down, rows)], shifted[pl.ds(15 - down, rows)]
    ).astype(aligned.dtype)


def flatten_held(blocks, held, flat):
    stride, tail, rows = blocks.stride, blocks.tail, blocks.rows
    if stride % 16 == 0 and tail == 16:
        flat[0:tail] = held[0, 0:tail].astype(jnp.float32)
        flat[tail:rows] = held[0, tail:rows].astype(jnp.float32)

        def body(d, carry):
            start = pl.multiple_of(d * stride, 16)
            flat[pl.ds(start, tail)] += held[d, 0:tail].astype(jnp.float32)
            start = pl.multiple_of(d * stride + tail, 16)
            flat[pl.ds(start, stride)] = held[d, tail:rows].astype(jnp.float32)
            return carry

        lax.fori_loop(1, blocks.count, body, 0)
    else:
        flat[...] = jnp.zeros_like(flat)

        def body(d, carry):
            flat[pl.ds(d * stride, rows)] += held[d].astype(jnp.float32)
            return carry

        lax.fori_loop(0, blocks.count, body, 0)


def unflatten(flat, base, matrix, first, width):
    height, steps = matrix.shape[0], width // LANES
    for i in range(steps):
        matrix[:, first + i * LANES : first + (i + 1) * LANES] = flat[
            pl.ds(base + i, height, stride=steps), :
        ].astype(matrix.dtype)


def write_gain(flat, base, gain):
    for i in range(gain.shape[1] // LANES):
        flat[base + i : base + i + 1, :] = gain[:, i * LANES : (i + 1) * LANES]


def read_gain(flat, base, width):
    return jnp.concatenate([flat[base + i : base + i + 1, :] for i in range(width // LANES)], axis=-1)


class Halo:
    def __init__(self, place, wires, kv, block, first, size):
        self.place, self.wires, self.kv, self.block = place, wires, kv, block
        self.first, self.size = first, size

    def slot(self, at):
        return self.kv.at[pl.ds(self.first, self.size), pl.ds(pl.multiple_of(at * self.block, 128), self.block)]

    def outward(self):
        p = self.place
        self.outer = self.wires.copy(self.slot(4), self.slot(0), p.outer_peer(1))

    def plane(self):
        p = self.place
        self.outer.wait_recv()
        self.across = self.wires.copy(self.slot(4 * (1 - p.y)), self.slot(2), p.y_peer())
        self.near = self.wires.copy(self.slot(4 * (1 - p.c)), self.slot(3 - 2 * p.c), p.sibling())

    def relay(self):
        p = self.place
        self.across.wait_recv()
        self.far = self.wires.copy(self.slot(2), self.slot(1 + 2 * p.c), p.sibling())

    def end(self):
        self.near.wait_recv()
        self.far.wait_recv()


HALO_WIRES = 4


class Locals:
    def __init__(self, sems):
        self.sems, self.used, self.open = sems, 0, []

    def copy(self, src, dst):
        made = pltpu.make_async_copy(src, dst, self.sems.at[self.used])
        self.used += 1
        self.open.append(made)
        made.start()
        return made

    def finish(self, made):
        made.wait()
        self.open = [other for other in self.open if other is not made]

    def drain(self):
        for made in self.open:
            made.wait()
        self.open = []


class Geo:
    def __init__(self, tokens, attention_params, feed_params):
        self.seqs, self.block = tokens.shape[:2]
        self.rows = self.seqs * self.block
        self.count = lax.axis_size("batch") * lax.axis_size("seq")
        self.outer = lax.axis_size("seq") // 4
        self.attention = Blocks(attention_params.shape[0], self.count)
        self.feed = Blocks(feed_params.shape[0], self.count)
        self.reach = 5 * self.block
        self.attention_bounds = [0, self.attention.rows]
        middle = self.feed.rows // 32 * 16
        self.feed_bounds = [0, middle, self.feed.rows]


QUERY = HEADS * HEAD_DIM
BASE_KEY = D * QUERY // LANES
BASE_VALUE = BASE_KEY + D * HEAD_DIM // LANES
BASE_OUT = BASE_VALUE + D * HEAD_DIM // LANES
BASE_GAINS = BASE_OUT + QUERY * D // LANES
STEP = 256


def forward_kernel(geo, tokens, positions, frequency, attention_in, feed_in, *refs):
    (
        feed_held,
        out_wqkv,
        out_wo,
        out_gains,
        out_q,
        out_kv,
        out_merged,
        out_projected,
        out_hidden,
        out_cosine,
        out_sine,
    ) = refs[:11]
    (
        held,
        own_feed,
        shifted,
        flat,
        wqkv,
        wo,
        gains,
        cosine,
        sine,
        lows,
        normed,
        q,
        kv,
        scores,
        probs,
        merged,
        projected,
        hidden,
        send,
        recv,
        local,
    ) = refs[11:]
    place = Place()
    wires, locals_ = Wires(send, recv), Locals(local)
    seqs, block, reach = geo.seqs, geo.block, geo.reach
    align_shard(geo.attention, place, attention_in, shifted, held.at[place.mine()])
    align_shard(geo.feed, place, feed_in, shifted, own_feed)
    lead = locals_.copy(own_feed, feed_held.at[place.mine()])
    greet(place)
    gather_a = Gather(place, wires, held, geo.attention.rows // 32 * 16)
    gather_f = Gather(place, wires, feed_held, geo.feed.rows // 32 * 16)
    gather_a.begin()

    columns = positions[...].astype(jnp.float32).T
    row = lax.broadcasted_iota(jnp.int32, (block, LANES), 0)
    for s in range(seqs):
        spot = columns[:, s : s + 1]
        angle = spot * frequency[...]
        rows = slice(s * block, (s + 1) * block)
        cosine[rows] = jnp.cos(angle)
        sine[rows] = jnp.sin(angle)
        lows[s] = jnp.maximum(row + 1, row + WINDOW - spot.astype(jnp.int32))

    gather_a.corner(0)
    for j in range(1, geo.outer):
        gather_a.spread(j)
        gather_a.corner(j)
        gather_a.finish(j - 1)
    gather_a.finish(geo.outer - 1)
    locals_.finish(lead)
    gather_f.begin()
    gather_a.end()
    pending = [functools.partial(gather_f.corner, 0)]
    for j in range(1, geo.outer):
        pending.append(functools.partial(gather_f.spread, j))
        pending.append(functools.partial(gather_f.corner, j))
        pending.append(functools.partial(gather_f.finish, j - 1))
    pending.append(functools.partial(gather_f.finish, geo.outer - 1))

    def tick(amount=1):
        for _ in range(amount):
            if pending:
                pending.pop(0)()

    flatten_held(geo.attention, held, flat)
    at = BASE_GAINS
    for i, width in enumerate((D, HEAD_DIM, HEAD_DIM, D)):
        gains[i : i + 1, :width] = read_gain(flat, at, width)
        at += width // LANES
    unflatten(flat, BASE_KEY, wqkv, QUERY, HEAD_DIM)
    unflatten(flat, BASE_VALUE, wqkv, QUERY + HEAD_DIM, HEAD_DIM)
    gain = gains[0:1, :]
    gain_key = gains[2:3, :HEAD_DIM]
    halos = []
    per_step = STEP // block
    for s in range(0, seqs, per_step):
        rows = slice(s * block, (s + per_step) * block)
        x = tokens[rows].astype(jnp.float32)
        normed[rows] = (x * root_inverse(x) * gain).astype(jnp.bfloat16)
        made = dot_nn(normed[rows], wqkv[:, QUERY:])
        keys = made[:, :HEAD_DIM]
        keys = turn(keys * root_inverse(keys) * gain_key, cosine[rows], sine[rows])
        for i in range(per_step):
            part = slice(i * block, (i + 1) * block)
            kv[s + i, reach - block :, :HEAD_DIM] = keys[part].astype(jnp.bfloat16)
            kv[s + i, reach - block :, HEAD_DIM:] = made[part, HEAD_DIM:].astype(jnp.bfloat16)
        if (s + per_step) % (seqs // 2) == 0:
            halo = Halo(place, wires, kv, block, s + per_step - seqs // 2, seqs // 2)
            halo.outward()
            halos.append(halo)
    unflatten(flat, 0, wqkv, 0, QUERY)
    tick(2)
    gain_query = gains[1:2, :HEAD_DIM] * HEAD_DIM**-0.5
    for s in range(0, seqs, per_step):
        rows = slice(s * block, (s + per_step) * block)
        made = dot_nn(normed[rows], wqkv[:, :QUERY])
        for h in range(HEADS):
            one = made[:, h * HEAD_DIM : (h + 1) * HEAD_DIM]
            one = turn(one * root_inverse(one) * gain_query, cosine[rows], sine[rows])
            q[h, rows] = one.astype(jnp.bfloat16)
        tick()
    unflatten(flat, BASE_OUT, wo, 0, D)
    for src, dst in (
        (wqkv, out_wqkv),
        (wo, out_wo),
        (gains, out_gains),
        (q, out_q),
        (cosine, out_cosine),
        (sine, out_sine),
    ):
        locals_.copy(src, dst)
    for halo in halos:
        halo.plane()
    tick()
    for halo in halos:
        halo.relay()
    tick()

    chunk = 32
    lane = lax.broadcasted_iota(jnp.int32, (chunk, reach), 1)
    over = lax.broadcasted_iota(jnp.int32, (chunk, reach), 1) - lax.broadcasted_iota(
        jnp.int32, (chunk, reach), 0
    )

    def attend(s, carry):
        start = pl.multiple_of(s * block, block)
        rows = pl.ds(start, block)
        queries = q[:, rows, :].reshape(HEADS * block, HEAD_DIM)
        scores[...] = dot_nt(queries, kv[s, :, :HEAD_DIM])
        for r in range(0, HEADS * block, chunk):
            i = r % block
            low = jnp.concatenate([lows[s, i : i + chunk, :]] * (reach // LANES), axis=-1)
            seen = (lane >= low) & (over <= WINDOW + i)
            raised = jnp.where(seen, jnp.exp(scores[r : r + chunk]), 0.0)
            share = 1.0 / jnp.sum(raised, axis=-1, keepdims=True)
            probs[r : r + chunk] = (raised * share).astype(jnp.bfloat16)
        made = dot_nn(probs[...], kv[s, :, HEAD_DIM:])
        for h in range(HEADS):
            merged[rows, h * HEAD_DIM : (h + 1) * HEAD_DIM] = made[
                h * block : (h + 1) * block
            ].astype(jnp.bfloat16)
        return carry

    halves = seqs // 2
    for g, halo in enumerate(halos):
        halo.end()
        for first in range(g * halves, (g + 1) * halves, 2):
            lax.fori_loop(first, first + 2, attend, 0)
            tick()
    locals_.copy(kv, out_kv)
    locals_.copy(merged, out_merged)
    gain_post = gains[3:4, :]
    for s in range(0, seqs, per_step):
        rows = slice(s * block, (s + per_step) * block)
        made = dot_nn(merged[rows], wo[...])
        projected[rows] = made
        hidden[rows] = tokens[rows].astype(jnp.float32) + made * root_inverse(made) * gain_post
        locals_.copy(projected.at[rows], out_projected.at[rows])
        locals_.copy(hidden.at[rows], out_hidden.at[rows])
    tick(len(pending))
    gather_f.end()
    wires.drain()
    locals_.drain()


def vmem(shape, dtype):
    return pltpu.VMEM(shape, dtype)


def forward_pass(geo, tokens, positions, attention_block, feed_block):
    count, rows, seqs, block = geo.count, geo.rows, geo.seqs, geo.block
    bf, f4 = jnp.bfloat16, jnp.float32
    half = HEAD_DIM // 2
    frequency = (
        rope_base ** (-(np.arange(half, dtype=np.float32) * np.float32(2.0) / HEAD_DIM))
    ).astype(np.float32)[None]
    wires = 2 * gather_wires(geo.outer) + 2 * HALO_WIRES
    outs = [
        ((count, geo.feed.rows, LANES), bf),
        ((D, QUERY + 2 * HEAD_DIM), bf),
        ((QUERY, D), bf),
        ((8, D), f4),
        ((HEADS, rows, HEAD_DIM), bf),
        ((seqs, geo.reach, 2 * HEAD_DIM), bf),
        ((rows, QUERY), bf),
        ((rows, D), f4),
        ((rows, D), f4),
        ((rows, half), f4),
        ((rows, half), f4),
    ]
    flat_rows = geo.attention.count * geo.attention.stride + geo.attention.tail
    return pl.pallas_call(
        functools.partial(forward_kernel, geo),
        out_shape=[jax.ShapeDtypeStruct(*out) for out in outs],
        in_specs=[pl.BlockSpec(memory_space=pltpu.VMEM)] * 5,
        out_specs=[pl.BlockSpec(memory_space=pl.ANY)] * len(outs),
        scratch_shapes=[
            vmem((count, geo.attention.rows, LANES), bf),
            vmem((geo.feed.rows, LANES), bf),
            vmem((16 + geo.feed.rows, LANES), f4),
            vmem((flat_rows, LANES), f4),
            vmem((D, QUERY + 2 * HEAD_DIM), bf),
            vmem((QUERY, D), bf),
            vmem((8, D), f4),
            vmem((rows, half), f4),
            vmem((rows, half), f4),
            vmem((seqs, block, LANES), jnp.int32),
            vmem((rows, D), bf),
            vmem((HEADS, rows, HEAD_DIM), bf),
            vmem((seqs, geo.reach, 2 * HEAD_DIM), bf),
            vmem((HEADS * block, geo.reach), f4),
            vmem((HEADS * block, geo.reach), bf),
            vmem((rows, QUERY), bf),
            vmem((rows, D), f4),
            vmem((rows, D), f4),
            pltpu.SemaphoreType.DMA((wires,)),
            pltpu.SemaphoreType.DMA((wires,)),
            pltpu.SemaphoreType.DMA((32,)),
        ],
        compiler_params=pltpu.CompilerParams(
            collective_id=0, has_side_effects=True, vmem_limit_bytes=60 << 20
        ),
    )(tokens.reshape(rows, D), positions, jnp.asarray(frequency), attention_block, feed_block)


MATRIX = D * FF // LANES
BEND = 0.044715
SLOPE = math.sqrt(2.0 / math.pi)


def feed_pieces(blocks, which):
    base, stop = which * MATRIX, (which + 1) * MATRIX
    if which == 2:
        stop = blocks.count * blocks.stride + blocks.tail
    found = []
    for d in range(blocks.count):
        low = max(d * blocks.stride, base)
        high = min(d * blocks.stride + blocks.rows, stop)
        if low < high:
            found.append((d, low - base, high - base, base - d * blocks.stride))
    return found


def feed_kernel(
    geo, held_in, hidden, cotangent, mixed, grad_hidden, split_out, *refs
):
    (held, flat, twin, down, act, pair, feed_in, turned_in, grad_down, local) = refs
    locals_ = Locals(local)
    blocks = geo.feed
    ends = [-(-(m + 1) * MATRIX // blocks.stride) for m in range(3)]
    starts = [0] + ends[:-1]
    loads = [
        locals_.copy(held_in.at[pl.ds(a, b - a)], held.at[pl.ds(a, b - a)])
        for a, b in zip(starts, ends)
    ]

    def unpack(which):
        for d, low, high, shift in feed_pieces(blocks, which):
            mid = min(high, max(low, d * blocks.stride - which * MATRIX + blocks.tail))
            if d and low < mid:
                flat[low:mid] += held[d, low + shift : mid + shift].astype(jnp.float32)
            else:
                mid = low
            flat[mid:high] = held[d, mid + shift : high + shift].astype(jnp.float32)

    def pack(which):
        for d, low, high, shift in feed_pieces(blocks, which):
            held[d, low + shift : high + shift] = flat[low:high].astype(jnp.bfloat16)

    for which, (matrix, first, width) in enumerate(
        ((twin, 0, FF), (twin, FF, FF), (down, 0, D))
    ):
        locals_.finish(loads[which])
        unpack(which)
        unflatten(flat, 0, matrix, first, width)
    gain_feed = read_gain(flat, MATRIX, D)
    gain_out = read_gain(flat, MATRIX + D // LANES, D)

    total, step = geo.rows, STEP
    spans = [slice(r, r + step) for r in range(0, total, step)]
    for rows in spans:
        h = hidden[rows]
        feed_in[rows] = (h * root_inverse(h) * gain_feed).astype(jnp.bfloat16)

    def rise(i, carry):
        columns = pl.ds(pl.multiple_of(i * step, step), step)
        others = pl.ds(pl.multiple_of(FF + i * step, step), step)
        for rows in spans:
            g = dot_nn(feed_in[rows], twin[:, columns])
            u = dot_nn(feed_in[rows], twin[:, others])
            square = g * g
            t = jnp.tanh(g * (SLOPE + SLOPE * BEND * square))
            half = 0.5 + 0.5 * t
            soft = g * half
            act[rows, columns] = (soft * u).astype(jnp.bfloat16)
            pair[rows, others] = soft.astype(jnp.bfloat16)
            slope = half * (1.0 + g * (1.0 - t) * (SLOPE + 3.0 * SLOPE * BEND * square))
            pair[rows, columns] = (u * slope).astype(jnp.bfloat16)
        return carry

    lax.fori_loop(0, FF // step, rise, 0)

    def settle(i, sum_out):
        rows = pl.ds(pl.multiple_of(i * step, step), step)
        made = dot_nn(act[rows], down[...])
        r = root_inverse(made)
        mixed[rows] = (hidden[rows] + made * r * gain_out).astype(jnp.bfloat16)
        e = cotangent[rows].astype(jnp.float32)
        unit = made * r
        sum_out = sum_out + jnp.sum(e * unit, axis=0, keepdims=True)
        c = e * gain_out
        grad_down[rows] = (
            r * (c - unit * jnp.mean(unit * c, axis=-1, keepdims=True))
        ).astype(jnp.bfloat16)
        return sum_out

    sum_out = lax.fori_loop(0, total // step, settle, jnp.zeros((1, D), jnp.float32))

    def fall(i, carry):
        columns = pl.ds(pl.multiple_of(i * step, step), step)
        others = pl.ds(pl.multiple_of(FF + i * step, step), step)
        for rows in spans:
            made = dot_nt(grad_down[rows], down[columns, :])
            for at in (columns, others):
                pair[rows, at] = (made * pair[rows, at].astype(jnp.float32)).astype(jnp.bfloat16)
        return carry

    lax.fori_loop(0, FF // step, fall, 0)

    def back(i, sum_feed):
        rows = pl.ds(pl.multiple_of(i * step, step), step)
        made = dot_nt(pair[rows], twin[...])
        h = hidden[rows]
        r = root_inverse(h)
        unit = h * r
        sum_feed = sum_feed + jnp.sum(made * unit, axis=0, keepdims=True)
        c = made * gain_feed
        grad_hidden[rows] = cotangent[rows].astype(jnp.float32) + r * (
            c - unit * jnp.mean(unit * c, axis=-1, keepdims=True)
        )
        return sum_feed

    sum_feed = lax.fori_loop(0, total // step, back, jnp.zeros((1, D), jnp.float32))
    turned_in[...] = feed_in[...].T

    def wide(i, carry, first):
        made = dot_nn(turned_in[...], pair[:, pl.ds(pl.multiple_of(first + i * step, step), step)])
        for k in range(step // LANES):
            flat[pl.ds(i * (step // LANES) + k, D, stride=FF // LANES), :] = made[
                :, k * LANES : (k + 1) * LANES
            ]
        return carry

    lax.fori_loop(0, FF // step, functools.partial(wide, first=0), 0)
    pack(0)
    lax.fori_loop(0, FF // step, functools.partial(wide, first=FF), 0)
    pack(1)

    def tall(i, carry):
        columns = pl.ds(pl.multiple_of(i * step, step), step)
        made = dot_tn(act[:, columns], grad_down[...])
        for k in range(D // LANES):
            flat[pl.ds(i * (step * D // LANES) + k, step, stride=D // LANES), :] = made[
                :, k * LANES : (k + 1) * LANES
            ]
        return carry

    lax.fori_loop(0, FF // step, tall, 0)
    flat[MATRIX:] = jnp.zeros_like(flat[MATRIX:])
    write_gain(flat, MATRIX, sum_feed)
    write_gain(flat, MATRIX + D // LANES, sum_out)
    pack(2)
    locals_.copy(held, split_out)
    locals_.drain()


def feed_pass(geo, feed_held, hidden, cotangent):
    bf, f4, rows = jnp.bfloat16, jnp.float32, geo.rows
    outs = [((rows, D), bf), ((rows, D), f4), (feed_held.shape, bf)]
    full, hbm = pl.BlockSpec(memory_space=pltpu.VMEM), pl.BlockSpec(memory_space=pl.ANY)
    return pl.pallas_call(
        functools.partial(feed_kernel, geo),
        out_shape=[jax.ShapeDtypeStruct(*out) for out in outs],
        in_specs=[hbm, full, full],
        out_specs=[full, full, hbm],
        scratch_shapes=[
            vmem(feed_held.shape, bf),
            vmem((MATRIX + geo.feed.tail, LANES), f4),
            vmem((D, 2 * FF), bf),
            vmem((FF, D), bf),
            vmem((rows, FF), bf),
            vmem((rows, 2 * FF), bf),
            vmem((rows, D), bf),
            vmem((D, rows), bf),
            vmem((rows, D), bf),
            pltpu.SemaphoreType.DMA((8,)),
        ],
        compiler_params=pltpu.CompilerParams(vmem_limit_bytes=60 << 20),
    )(feed_held, hidden, cotangent.reshape(rows, D))


class Scatter:
    def __init__(self, place, wires, other, own, lands, result, piece):
        self.place, self.wires, self.other, self.own, self.result = place, wires, other, own, result
        self.by_core, self.first_x, self.first_y, self.second_x, self.second_y, self.by_outer = lands
        first, cut, last, at_x, at_y = piece
        self.all = pl.ds(first, last - first)
        self.rows_x, self.rows_y = pl.ds(first, cut - first), pl.ds(cut, last - cut)
        self.land_x, self.land_y = pl.ds(at_x, cut - first), pl.ds(at_y, last - cut)

    def add(self, i, y, rows, land):
        self.own[i, y, rows] = (
            self.own[i, y, rows].astype(jnp.float32) + land.astype(jnp.float32)
        ).astype(jnp.bfloat16)

    def column_of(self, b):
        return pl.ds(b * self.place.outer, self.place.outer)

    def core(self):
        self.from_core = self.wires.copy(
            self.other.at[:, :, 1 - self.place.c, self.all],
            self.by_core.at[:, :, self.all],
            self.place.sibling(),
        )

    def plane(self):
        p = self.place
        self.from_core.wait_recv()

        def body(i, carry):
            for y in range(2):
                self.add(i, y, self.all, self.by_core[i, y, self.all])
            return carry

        lax.fori_loop(0, 2 * p.outer, body, 0)
        self.from_x = self.wires.copy(
            self.own.at[self.column_of(1 - p.b), :, self.rows_x],
            self.first_x.at[:, :, self.land_x],
            p.x_peer(),
        )
        self.from_y = self.wires.copy(
            self.own.at[:, 1 - p.y, self.rows_y], self.first_y.at[:, self.land_y], p.y_peer()
        )

    def cross(self):
        p = self.place
        self.from_x.wait_recv()

        def body(hi, carry):
            for y in range(2):
                self.add(p.b * p.outer + hi, y, self.rows_x, self.first_x[hi, y, self.land_x])
            return carry

        lax.fori_loop(0, p.outer, body, 0)
        self.over_y = self.wires.copy(
            self.own.at[self.column_of(p.b), 1 - p.y, self.rows_x],
            self.second_y.at[:, self.land_x],
            p.y_peer(),
        )
        self.from_y.wait_recv()

        def body(i, carry):
            self.add(i, p.y, self.rows_y, self.first_y[i, self.land_y])
            return carry

        lax.fori_loop(0, 2 * p.outer, body, 0)
        self.over_x = self.wires.copy(
            self.own.at[self.column_of(1 - p.b), p.y, self.rows_y],
            self.second_x.at[:, self.land_y],
            p.x_peer(),
        )

    def column(self):
        p = self.place
        self.over_y.wait_recv()
        self.over_x.wait_recv()

        def body(hi, carry):
            i = p.b * p.outer + hi
            self.add(i, p.y, self.rows_x, self.second_y[hi, self.land_x])
            self.add(i, p.y, self.rows_y, self.second_x[hi, self.land_y])
            return carry

        lax.fori_loop(0, p.outer, body, 0)
        self.from_outer = [
            self.wires.copy(
                self.own.at[p.b * p.outer + p.outer_at(k), p.y, self.all],
                self.by_outer.at[k - 1, self.all],
                p.outer_peer(k),
            )
            for k in range(1, p.outer)
        ]

    def end(self):
        p = self.place
        total = self.own[p.b * p.outer + p.hi, p.y, self.all].astype(jnp.float32)
        for k, made in enumerate(self.from_outer):
            made.wait_recv()
            total = total + self.by_outer[k, self.all].astype(jnp.float32)
        self.result[self.all] = total

    def steps(self):
        return [self.core, self.plane, self.cross, self.column, self.end]


def scatter_wires(outer):
    return 5 + outer - 1


def cut_pieces(bounds):
    pieces, at_x, at_y = [], 0, 0
    for first, last in zip(bounds, bounds[1:]):
        cut = first + (last - first) // 32 * 16
        pieces.append((first, cut, last, at_x, at_y))
        at_x, at_y = at_x + cut - first, at_y + last - cut
    return pieces, at_x, at_y


def land_shapes(rows, bounds, outer):
    rows_x, rows_y = cut_pieces(bounds)[1:]
    return [
        pltpu.VMEM(shape + (LANES,), jnp.bfloat16)
        for shape in (
            (2 * outer, 2, rows),
            (outer, 2, rows_x),
            (2 * outer, rows_y),
            (outer, rows_y),
            (outer, rows_x),
            (outer - 1, rows),
        )
    ]


class Return:
    def __init__(self, place, wires, kv, own, by_core, by_y, by_outer, block, first, size):
        self.place, self.wires, self.kv, self.own, self.block = place, wires, kv, own, block
        self.by_core, self.by_y, self.by_outer = by_core, by_y, by_outer
        self.group = pl.ds(first, size)
        self.each = range(first, first + size)

    def rows(self, at):
        return slice(at * self.block, (at + 1) * self.block)

    def slot(self, at):
        return self.kv.at[self.group, pl.ds(at * self.block, self.block)]

    def core(self):
        p = self.place
        self.from_core = [
            self.wires.copy(
                self.slot(at), self.by_core.at[self.group, pl.ds(i * self.block, self.block)], p.sibling()
            )
            for i, at in enumerate((1, 3))
        ]

    def grow(self, s, at, extra):
        rows = self.rows(at)
        self.kv[s, rows] = (self.kv[s, rows].astype(jnp.float32) + extra).astype(jnp.bfloat16)

    def plane(self):
        p = self.place
        for made in self.from_core:
            made.wait_recv()
        for s in self.each:

            @pl.when(p.c == 0)
            def _():
                self.grow(s, 2, self.by_core[s, self.rows(0)].astype(jnp.float32))
                self.own[s] += self.by_core[s, self.rows(1)].astype(jnp.float32)

            @pl.when(p.c == 1)
            def _():
                self.grow(s, 0, self.by_core[s, self.rows(0)].astype(jnp.float32))
                self.grow(s, 2, self.by_core[s, self.rows(1)].astype(jnp.float32))

        self.from_y = self.wires.copy(self.slot(2), self.by_y.at[self.group], p.y_peer())

    def outward(self):
        p = self.place
        self.from_y.wait_recv()
        for s in self.each:

            @pl.when(p.y == 0)
            def _():
                self.own[s] += self.by_y[s].astype(jnp.float32)

            @pl.when(p.y == 1)
            def _():
                self.grow(s, 0, self.by_y[s].astype(jnp.float32))

        self.from_outer = self.wires.copy(
            self.slot(0), self.by_outer.at[self.group], p.outer_peer(p.outer - 1)
        )

    def end(self):
        self.from_outer.wait_recv()
        for s in self.each:
            self.own[s] += self.by_outer[s].astype(jnp.float32)


RETURN_WIRES = 4


def fill_blocks(blocks, split, flat, margin, base, stop):
    even = blocks.stride % 16 == 0
    for d in range(blocks.count):
        low, high = max(d * blocks.stride, base), min(d * blocks.stride + blocks.rows, stop)
        if low >= high:
            continue
        i, y, c = d // 4, d // 2 % 2, d % 2
        first, last = low - d * blocks.stride, high - d * blocks.stride
        if even:
            split[i, y, c, first:last] = flat[low - base + margin : high - base + margin].astype(
                jnp.bfloat16
            )
        else:
            start, end = first // 16 * 16, -(-last // 16) * 16
            source = low - base + margin - (first - start)
            split[i, y, c, start:end] = (
                split[i, y, c, start:end].astype(jnp.float32)
                + flat[source : source + end - start]
            ).astype(jnp.bfloat16)


MARGIN = 16


def backward_kernel(
    geo, tokens, positions, gains, wqkv_in, wo_in, q_in, kv_in, merged_in, projected_in,
    hidden_in, cosine_in, sine_in, feed_split, *refs
):
    grad_tokens, attention_sum, feed_sum = refs[:3]
    (
        wqkv, wo, q, kv, pair, grad, cosine, sine, projected, normed, turned, grad_out, out_rows,
        scores, slopes, probs, logits, own_kv, own_feed, split, flat, by_core_kv, by_y_kv, by_outer_kv,
    ) = refs[3:27]
    lands_a, lands_f = refs[27:33], refs[33:39]
    send, recv, local = refs[39:]
    place = Place()
    wires, locals_ = Wires(send, recv), Locals(local)
    seqs, block, reach, total, step = geo.seqs, geo.block, geo.reach, geo.rows, STEP
    own_load = locals_.copy(feed_split.at[:, :, place.c], own_feed)
    load_projected = locals_.copy(projected_in, projected)
    load_grad = locals_.copy(hidden_in, grad)
    load_wo = locals_.copy(wo_in, wo)
    load_merged = locals_.copy(merged_in, pair.at[:, pl.ds(0, QUERY)])
    load_q, load_kv = locals_.copy(q_in, q), locals_.copy(kv_in, kv)
    load_rest = [
        locals_.copy(wqkv_in, wqkv), locals_.copy(cosine_in, cosine), locals_.copy(sine_in, sine)
    ]
    greet(place)
    pieces = cut_pieces(geo.feed_bounds)[0]
    feed_parts = [
        Scatter(place, wires, feed_split, own_feed, lands_f, feed_sum, piece) for piece in pieces
    ]
    for part in feed_parts:
        part.core()
    pending = []
    count, depth = len(feed_parts), 4
    for at in range(count + depth - 1):
        for stage in reversed(range(depth)):
            if 0 <= at - stage < count:
                pending.append(feed_parts[at - stage].steps()[1 + stage])

    def tick(amount=1):
        for _ in range(amount):
            if pending:
                pending.pop(0)()

    gain_attention, gain_query = gains[0:1, :], gains[1:2, :HEAD_DIM]
    gain_key, gain_post = gains[2:3, :HEAD_DIM], gains[3:4, :]
    for made in (load_projected, load_grad, load_wo):
        locals_.finish(made)

    def start_rows(i, summed):
        rows = pl.ds(pl.multiple_of(i * step, step), step)
        made, e = projected[rows], grad[rows]
        r = root_inverse(made)
        unit = made * r
        c = e * gain_post
        out_rows[rows] = (r * (c - unit * jnp.mean(unit * c, axis=-1, keepdims=True))).astype(
            jnp.bfloat16
        )
        x = tokens[rows].astype(jnp.float32)
        normed[rows] = (x * root_inverse(x) * gain_attention).astype(jnp.bfloat16)
        for h in range(HEADS):
            grad_out[h, rows] = dot_nt(
                out_rows[rows], wo[h * HEAD_DIM : (h + 1) * HEAD_DIM, :]
            ).astype(jnp.bfloat16)
        return summed + jnp.sum(e * unit, axis=0, keepdims=True)

    sum_post = lax.fori_loop(0, total // step, start_rows, jnp.zeros((1, D), jnp.float32))
    turned[...] = normed[...].T
    locals_.finish(own_load)
    tick()
    blocks = geo.attention
    flat[0:MARGIN] = jnp.zeros((MARGIN, LANES), jnp.float32)
    flat[MARGIN + QUERY * D // LANES :] = jnp.zeros((MARGIN, LANES), jnp.float32)
    if blocks.stride % 16:
        split[...] = jnp.zeros_like(split)
    locals_.finish(load_merged)

    def tall(i, carry):
        columns = pl.ds(pl.multiple_of(i * step, step), step)
        made = dot_tn(pair[:, columns], out_rows[...])
        for k in range(D // LANES):
            flat[pl.ds(MARGIN + i * (step * D // LANES) + k, step, stride=D // LANES), :] = made[
                :, k * LANES : (k + 1) * LANES
            ]
        return carry

    lax.fori_loop(0, QUERY // step, tall, 0)
    fill_blocks(blocks, split, flat, MARGIN, BASE_OUT, BASE_GAINS)
    tick()
    for made in [load_q, load_kv] + load_rest:
        locals_.finish(made)

    wide = HEADS * block
    chunk = 32
    lane = lax.rem(lax.broadcasted_iota(jnp.int32, (chunk, wide), 1), block)
    line = lax.broadcasted_iota(jnp.int32, (chunk, wide), 0)

    def attend(s, carry):
        rows = pl.ds(pl.multiple_of(s * block, block), block)
        queries = q[:, rows, :].reshape(wide, HEAD_DIM)
        given = grad_out[:, rows, :].reshape(wide, HEAD_DIM)
        scores[...] = dot_nt(kv[s, :, :HEAD_DIM], queries)
        slopes[...] = dot_nt(kv[s, :, HEAD_DIM:], given)
        spot = jnp.concatenate([positions[pl.ds(s, 1), :]] * HEADS, axis=-1)
        low = jnp.maximum(lane[0:1] + 1, lane[0:1] + WINDOW - spot)
        total_e = jnp.zeros((8, wide), jnp.float32)
        total_d = jnp.zeros((8, wide), jnp.float32)
        for r in range(0, reach, chunk):
            seen = (line + r >= low) & (line + (r - WINDOW) <= lane)
            raised = jnp.where(seen, jnp.exp(scores[r : r + chunk]), 0.0)
            scores[r : r + chunk] = raised
            moved = raised * slopes[r : r + chunk]
            for k in range(0, chunk, 8):
                total_e = total_e + raised[k : k + 8]
                total_d = total_d + moved[k : k + 8]
        share = 1.0 / jnp.sum(total_e, axis=0, keepdims=True)
        inner = jnp.sum(total_d, axis=0, keepdims=True) * share
        for r in range(0, reach, chunk):
            p = scores[r : r + chunk] * share
            probs[r : r + chunk] = p.astype(jnp.bfloat16)
            logits[r : r + chunk] = (p * (slopes[r : r + chunk] - inner)).astype(jnp.bfloat16)
        grad_q = dot_tn(logits[...], kv[s, :, :HEAD_DIM]) * HEAD_DIM**-0.5
        grad_k = dot_nn(logits[...], queries)
        grad_v = dot_nn(probs[...], given)
        early = reach - block
        kv[s, :early, :HEAD_DIM] = grad_k[:early].astype(jnp.bfloat16)
        kv[s, :early, HEAD_DIM:] = grad_v[:early].astype(jnp.bfloat16)
        own_kv[s, :, :HEAD_DIM] = grad_k[early:]
        own_kv[s, :, HEAD_DIM:] = grad_v[early:]
        for h in range(HEADS):
            q[h, rows] = grad_q[h * block : (h + 1) * block].astype(jnp.bfloat16)
        return carry

    size = 2
    returns = [
        Return(place, wires, kv, own_kv, by_core_kv, by_y_kv, by_outer_kv, block, s, size)
        for s in range(0, seqs, size)
    ]
    for g, group in enumerate(returns):
        lax.fori_loop(g * size, (g + 1) * size, attend, 0)
        group.core()
        if g >= 1:
            returns[g - 1].plane()
        if g >= 2:
            returns[g - 2].outward()
        if g >= 3:
            returns[g - 3].end()
        tick()
    last = len(returns) - 1

    def query_rows(i, summed):
        rows = pl.ds(pl.multiple_of(i * step, step), step)
        made = dot_nn(normed[rows], wqkv[:, :QUERY])
        for h in range(HEADS):
            raw = made[:, h * HEAD_DIM : (h + 1) * HEAD_DIM]
            e = turn_back(q[h, rows].astype(jnp.float32), cosine[rows], sine[rows])
            r = root_inverse(raw)
            unit = raw * r
            summed = summed + jnp.sum(e * unit, axis=0, keepdims=True)
            c = e * gain_query
            pair[rows, h * HEAD_DIM : (h + 1) * HEAD_DIM] = (
                r * (c - unit * jnp.mean(unit * c, axis=-1, keepdims=True))
            ).astype(jnp.bfloat16)
        return summed

    returns[last].plane()
    returns[last - 1].outward()
    returns[last - 2].end()
    sum_query = lax.fori_loop(0, total // step, query_rows, jnp.zeros((1, HEAD_DIM), jnp.float32))
    returns[last].outward()
    returns[last - 1].end()

    def broad(i, carry, first, width):
        columns = pl.ds(pl.multiple_of(first + i * step, step), step)
        made = dot_nn(turned[...], pair[:, columns])
        for k in range(step // LANES):
            start = MARGIN + i * (step // LANES) + k
            flat[pl.ds(start, D, stride=width // LANES), :] = made[:, k * LANES : (k + 1) * LANES]
        return carry

    lax.fori_loop(0, QUERY // step, functools.partial(broad, first=0, width=QUERY), 0)
    fill_blocks(blocks, split, flat, MARGIN, 0, BASE_KEY)
    returns[last].end()

    def key_rows(i, summed):
        rows = pl.ds(pl.multiple_of(i * step, step), step)
        per = step // block
        raw = dot_nn(normed[rows], wqkv[:, QUERY : QUERY + HEAD_DIM])
        both = own_kv[pl.ds(i * per, per)].reshape(step, 2 * HEAD_DIM)
        e = turn_back(both[:, :HEAD_DIM], cosine[rows], sine[rows])
        r = root_inverse(raw)
        unit = raw * r
        c = e * gain_key
        pair[rows, QUERY : QUERY + HEAD_DIM] = (
            r * (c - unit * jnp.mean(unit * c, axis=-1, keepdims=True))
        ).astype(jnp.bfloat16)
        pair[rows, QUERY + HEAD_DIM :] = both[:, HEAD_DIM:].astype(jnp.bfloat16)
        return summed + jnp.sum(e * unit, axis=0, keepdims=True)

    sum_key = lax.fori_loop(0, total // step, key_rows, jnp.zeros((1, HEAD_DIM), jnp.float32))
    for first, base in ((QUERY, BASE_KEY), (QUERY + HEAD_DIM, BASE_VALUE)):
        broad(0, 0, first, HEAD_DIM)
        size_rows = D * HEAD_DIM // LANES
        flat[MARGIN + size_rows : 2 * MARGIN + size_rows] = jnp.zeros((MARGIN, LANES), jnp.float32)
        fill_blocks(blocks, split, flat, MARGIN, base, base + size_rows)

    def end_rows(i, summed):
        rows = pl.ds(pl.multiple_of(i * step, step), step)
        made = dot_nt(pair[rows], wqkv[...])
        x = tokens[rows].astype(jnp.float32)
        r = root_inverse(x)
        unit = x * r
        c = made * gain_attention
        grad[rows] = grad[rows] + r * (c - unit * jnp.mean(unit * c, axis=-1, keepdims=True))
        return summed + jnp.sum(made * unit, axis=0, keepdims=True)

    sum_attention = lax.fori_loop(0, total // step, end_rows, jnp.zeros((1, D), jnp.float32))
    locals_.copy(grad, grad_tokens)
    tail = geo.attention.tail
    flat[MARGIN : 2 * MARGIN + tail] = jnp.zeros((MARGIN + tail, LANES), jnp.float32)
    at = MARGIN
    for made in (sum_attention, sum_query, sum_key, sum_post):
        write_gain(flat, at, made)
        at += made.shape[1] // LANES
    fill_blocks(blocks, split, flat, MARGIN, BASE_GAINS, blocks.count * blocks.stride + tail)
    own = split.at[:, :, place.c]
    parts = [
        Scatter(place, wires, split, own, lands_a, attention_sum, piece)
        for piece in cut_pieces(geo.attention_bounds)[0]
    ]
    for part in parts:
        part.core()
    tick(len(pending))
    count = len(parts)
    for at in range(count + depth - 1):
        for stage in reversed(range(depth)):
            if 0 <= at - stage < count:
                parts[at - stage].steps()[1 + stage]()
    wires.drain()
    locals_.drain()


def backward_pass(geo, tokens, positions, saved, grad_hidden, feed_split):
    bf, f4, rows, seqs, block = jnp.bfloat16, jnp.float32, geo.rows, geo.seqs, geo.block
    wqkv, wo, gains, q, kv, merged, projected, cosine, sine = saved
    rows_a, rows_f, outer = geo.attention.rows, geo.feed.rows, geo.outer
    outs = [((rows, D), f4), ((rows_a, LANES), f4), ((rows_f, LANES), f4)]
    full, hbm = pl.BlockSpec(memory_space=pltpu.VMEM), pl.BlockSpec(memory_space=pl.ANY)
    wires = (len(geo.feed_bounds) + len(geo.attention_bounds) - 2) * scatter_wires(
        outer
    ) + seqs // 2 * RETURN_WIRES
    half = HEAD_DIM // 2
    return pl.pallas_call(
        functools.partial(backward_kernel, geo),
        out_shape=[jax.ShapeDtypeStruct(*out) for out in outs],
        in_specs=[full] * 3 + [hbm] * 10,
        out_specs=[hbm, full, full],
        scratch_shapes=[
            vmem(wqkv.shape, bf),
            vmem(wo.shape, bf),
            vmem(q.shape, bf),
            vmem(kv.shape, bf),
            vmem((rows, QUERY + 2 * HEAD_DIM), bf),
            vmem((rows, D), f4),
            vmem((rows, half), f4),
            vmem((rows, half), f4),
            vmem((rows, D), f4),
            vmem((rows, D), bf),
            vmem((D, rows), bf),
            vmem((HEADS, rows, HEAD_DIM), bf),
            vmem((rows, D), bf),
            vmem((geo.reach, HEADS * block), f4),
            vmem((geo.reach, HEADS * block), f4),
            vmem((geo.reach, HEADS * block), bf),
            vmem((geo.reach, HEADS * block), bf),
            vmem((seqs, block, 2 * HEAD_DIM), f4),
            vmem((2 * outer, 2, rows_f, LANES), bf),
            vmem((2 * outer, 2, 2, rows_a, LANES), bf),
            vmem((2 * MARGIN + QUERY * D // LANES, LANES), f4),
            vmem((seqs, 2 * block, 2 * HEAD_DIM), bf),
            vmem((seqs, block, 2 * HEAD_DIM), bf),
            vmem((seqs, block, 2 * HEAD_DIM), bf),
        ]
        + land_shapes(rows_a, geo.attention_bounds, outer)
        + land_shapes(rows_f, geo.feed_bounds, outer)
        + [
            pltpu.SemaphoreType.DMA((wires,)),
            pltpu.SemaphoreType.DMA((wires,)),
            pltpu.SemaphoreType.DMA((16,)),
        ],
        compiler_params=pltpu.CompilerParams(
            collective_id=1, has_side_effects=True, vmem_limit_bytes=63 << 20
        ),
    )(
        tokens.reshape(rows, D), positions, gains, wqkv, wo, q, kv, merged, projected,
        grad_hidden, cosine, sine, feed_split.reshape(2 * outer, 2, 2, rows_f, LANES),
    )


def on_device(tokens, attention_params, feed_params, positions, cotangent):
    geo = Geo(tokens, attention_params, feed_params)
    device = lax.axis_index("batch") * lax.axis_size("seq") + lax.axis_index("seq")
    (
        feed_held, wqkv, weight_out, gains, q, kv, merged, projected, hidden, cosine, sine,
    ) = forward_pass(
        geo, tokens, positions, geo.attention.pad(attention_params), geo.feed.pad(feed_params)
    )
    mixed, grad_hidden, feed_split = feed_pass(geo, feed_held, hidden, cotangent)
    grad_tokens, attention_sum, feed_sum = backward_pass(
        geo,
        tokens,
        positions,
        (wqkv, weight_out, gains, q, kv, merged, projected, cosine, sine),
        grad_hidden,
        feed_split,
    )
    return (
        mixed.reshape(tokens.shape),
        grad_tokens.reshape(tokens.shape),
        geo.attention.take(attention_sum, device),
        geo.feed.take(feed_sum, device),
    )


def solution(mesh):
    return jax.shard_map(
        on_device,
        mesh=mesh,
        in_specs=(
            P("batch", "seq", None),
            P(("batch", "seq")),
            P(("batch", "seq")),
            P("batch", "seq"),
            P("batch", "seq", None),
        ),
        out_specs=(
            P("batch", "seq", None),
            P("batch", "seq", None),
            P(("batch", "seq")),
            P(("batch", "seq")),
        ),
        check_vma=False,
    )
```

```python
import functools
import math

import jax
import jax.numpy as jnp
import numpy as np
from jax import lax
from jax.experimental import pallas as pl
from jax.experimental.pallas import tpu as pltpu
from jax.sharding import PartitionSpec as P

MESH = pl.DeviceIdType.MESH
LANES = 128

D = 640
HEADS = 4
HEAD_DIM = 256
FF = 2048
WINDOW = 512


rope_base = 10000.0


class Place:
    def __init__(self):
        self.devices_seq = lax.axis_size("seq")
        self.outer = self.devices_seq // 4
        self.count = 2 * self.devices_seq
        self.b = lax.axis_index("batch")
        s = lax.axis_index("seq")
        self.hi = lax.div(s, 4)
        self.y = lax.rem(lax.div(s, 2), 2)
        self.c = lax.rem(s, 2)

    def block(self, b, hi, y, c):
        return b * self.devices_seq + hi * 4 + y * 2 + c

    def seq_id(self, hi, y, c):
        return (self.b, hi * 4 + y * 2 + c)

    def mine(self):
        return self.block(self.b, self.hi, self.y, self.c)

    def x_peer(self):
        return (1 - self.b, self.hi * 4 + self.y * 2 + self.c)

    def y_peer(self):
        return self.seq_id(self.hi, 1 - self.y, self.c)

    def sibling(self):
        return self.seq_id(self.hi, self.y, 1 - self.c)

    def outer_at(self, k):
        return lax.rem(self.hi + k, self.outer)

    def flip(self, k):
        found, bit = 0, 1
        while bit < self.outer:
            own = lax.rem(lax.div(self.hi, bit), 2)
            found = found + bit * ((1 - own) if k & bit else own)
            bit *= 2
        return found

    def flip_peer(self, k):
        return self.seq_id(self.flip(k), self.y, self.c)

    def outer_peer(self, k):
        return self.seq_id(self.outer_at(k), self.y, self.c)

    def peers(self):
        return [self.x_peer(), self.y_peer(), self.sibling()] + [
            self.outer_peer(k) for k in range(1, self.outer)
        ]


def greet(place):
    barrier = pltpu.get_barrier_semaphore()
    peers = place.peers()
    for peer in peers:
        pl.semaphore_signal(barrier, inc=1, device_id=peer, device_id_type=MESH)
    pl.semaphore_wait(barrier, len(peers))


def guarded(when, action):
    if when is None:
        action()
    else:
        pl.when(when)(action)


class Wires:
    def __init__(self, send_sems, recv_sems):
        self.send_sems, self.recv_sems = send_sems, recv_sems
        self.used = 0
        self.sent = []

    def plan(self, src, dst, peer, when=None):
        made = pltpu.make_async_remote_copy(
            src_ref=src,
            dst_ref=dst,
            send_sem=self.send_sems.at[self.used],
            recv_sem=self.recv_sems.at[self.used],
            device_id=peer,
            device_id_type=MESH,
        )
        self.used += 1
        self.sent.append((made, when))
        return made

    def copy(self, src, dst, peer, when=None):
        made = self.plan(src, dst, peer, when)
        guarded(when, made.start)
        return made

    def drain(self):
        for made, when in self.sent:
            guarded(when, made.wait_send)
        self.sent = []


def gather_wires(outer):
    return outer - 1 + 4 * outer + 4 * outer


class Gather:
    def __init__(self, place, wires, held, first, last, share):
        self.place, self.wires, self.held = place, wires, held
        self.first, self.last = first, last
        self.cut = first + int((last - first) * share) // 16 * 16
        self.from_outer = {}
        self.from_x, self.from_y, self.diag, self.twin = {}, {}, {}, []

    def send(self, index, peer, first=None, last=None):
        first = self.first if first is None else first
        last = self.last if last is None else last
        ref = self.held.at[index, pl.ds(first, last - first)]
        return self.wires.copy(ref, ref, peer)

    def begin(self):
        p = self.place
        for k in range(1, p.outer):
            self.from_outer[k] = self.send(p.mine(), p.flip_peer(k))

    def spread(self, j):
        p = self.place
        if j:
            self.from_outer[j].wait_recv()
        index = p.block(p.b, p.flip(j), p.y, p.c)
        self.from_y[j] = self.send(index, p.y_peer())
        self.from_x[j] = self.send(index, p.x_peer())
        self.twin.append(self.send(index, p.sibling()))

    def corner(self, j):
        p = self.place
        at = p.flip(j)
        self.from_y[j].wait_recv()
        got = p.block(p.b, at, 1 - p.y, p.c)
        down = self.send(got, p.x_peer(), self.first, self.cut)
        self.twin.append(self.send(got, p.sibling()))
        self.from_x[j].wait_recv()
        got = p.block(1 - p.b, at, p.y, p.c)
        across = self.send(got, p.y_peer(), self.cut, self.last)
        self.twin.append(self.send(got, p.sibling()))
        self.diag[j] = (down, across)

    def finish(self, j):
        p = self.place
        for made in self.diag[j]:
            made.wait_recv()
        self.twin.append(self.send(p.block(1 - p.b, p.flip(j), 1 - p.y, p.c), p.sibling()))

    def end(self):
        for made in self.twin:
            made.wait_recv()


class Blocks:
    def __init__(self, length, count):
        self.length, self.count = length, count
        self.stride, self.rest = divmod(length, LANES)
        needed = -(-(length + self.rest * (count - 1)) // LANES)
        self.rows = -(-needed // 16) * 16
        self.tail = self.rows - self.stride
        self.total = length * count

    def pad(self, shard):
        return jnp.pad(shard, (0, self.rows * LANES - self.length)).reshape(self.rows, LANES)

    def take(self, block, index):
        return lax.dynamic_slice(block.reshape(-1), (self.rest * index,), (self.length,))


EPS = 1e-06


def root_inverse(rows):
    return lax.rsqrt(jnp.mean(rows * rows, axis=-1, keepdims=True) + EPS)


def turn(rows, cosine, sine):
    half = rows.shape[-1] // 2
    first, second = rows[:, :half], rows[:, half:]
    return jnp.concatenate([first * cosine - second * sine, second * cosine + first * sine], axis=-1)


def turn_back(rows, cosine, sine):
    half = rows.shape[-1] // 2
    first, second = rows[:, :half], rows[:, half:]
    return jnp.concatenate([first * cosine + second * sine, second * cosine - first * sine], axis=-1)


def dot_nn(left, right):
    return jnp.dot(left, right, preferred_element_type=jnp.float32)


def dot_nt(left, right):
    return lax.dot_general(left, right, (((1,), (1,)), ((), ())), preferred_element_type=jnp.float32)


def dot_tn(left, right):
    return lax.dot_general(left, right, (((0,), (0,)), ((), ())), preferred_element_type=jnp.float32)


def align_shard(blocks, place, padded_ref, shifted, aligned):
    offset = blocks.rest * place.mine()
    down, right = lax.div(offset, LANES), lax.rem(offset, LANES)
    rows = blocks.rows
    shifted[0:16] = jnp.zeros((16, LANES), jnp.float32)
    shifted[16 : 16 + rows] = pltpu.roll(padded_ref[...].astype(jnp.float32), right, 1)
    lane = lax.broadcasted_iota(jnp.int32, (rows, LANES), 1)
    aligned[...] = jnp.where(
        lane >= right, shifted[pl.ds(16 - down, rows)], shifted[pl.ds(15 - down, rows)]
    ).astype(aligned.dtype)


def flatten_held(blocks, held, flat):
    stride, tail, rows = blocks.stride, blocks.tail, blocks.rows
    if stride % 16 == 0 and tail == 16:
        flat[0:tail] = held[0, 0:tail].astype(jnp.float32)
        flat[tail:rows] = held[0, tail:rows].astype(jnp.float32)

        def body(d, carry):
            start = pl.multiple_of(d * stride, 16)
            flat[pl.ds(start, tail)] += held[d, 0:tail].astype(jnp.float32)
            start = pl.multiple_of(d * stride + tail, 16)
            flat[pl.ds(start, stride)] = held[d, tail:rows].astype(jnp.float32)
            return carry

        lax.fori_loop(1, blocks.count, body, 0)
    else:
        flat[...] = jnp.zeros_like(flat)

        def body(d, carry):
            flat[pl.ds(d * stride, rows)] += held[d].astype(jnp.float32)
            return carry

        lax.fori_loop(0, blocks.count, body, 0)


def unflatten(flat, base, matrix, first, width):
    height, steps = matrix.shape[0], width // LANES
    for i in range(steps):
        matrix[:, first + i * LANES : first + (i + 1) * LANES] = flat[
            pl.ds(base + i, height, stride=steps), :
        ].astype(matrix.dtype)


def write_gain(flat, base, gain):
    for i in range(gain.shape[1] // LANES):
        flat[base + i : base + i + 1, :] = gain[:, i * LANES : (i + 1) * LANES]


def read_gain(flat, base, width):
    return jnp.concatenate([flat[base + i : base + i + 1, :] for i in range(width // LANES)], axis=-1)


class Halo:
    def __init__(self, place, wires, kv, block, first, size):
        self.place, self.wires, self.kv, self.block = place, wires, kv, block
        self.first, self.size = first, size

    def slot(self, at):
        return self.kv.at[pl.ds(self.first, self.size), pl.ds(pl.multiple_of(at * self.block, 128), self.block)]

    def outward(self):
        p = self.place
        self.outer = self.wires.copy(
            self.slot(4), self.slot(0), p.outer_peer(1), p.hi + 1 < p.outer
        )

    def plane(self):
        p = self.place
        guarded(p.hi > 0, self.outer.wait_recv)
        self.across = self.wires.copy(self.slot(4 * (1 - p.y)), self.slot(2), p.y_peer())
        self.near = self.wires.copy(self.slot(4 * (1 - p.c)), self.slot(3 - 2 * p.c), p.sibling())

    def relay(self):
        p = self.place
        self.across.wait_recv()
        self.far = self.wires.copy(self.slot(2), self.slot(1 + 2 * p.c), p.sibling())

    def end(self):
        self.near.wait_recv()
        self.far.wait_recv()


HALO_WIRES = 4


class Locals:
    def __init__(self, sems):
        self.sems, self.used, self.open = sems, 0, []

    def copy(self, src, dst):
        made = pltpu.make_async_copy(src, dst, self.sems.at[self.used])
        self.used += 1
        self.open.append(made)
        made.start()
        return made

    def finish(self, made):
        made.wait()
        self.open = [other for other in self.open if other is not made]

    def drain(self):
        for made in self.open:
            made.wait()
        self.open = []


class Geo:
    def __init__(self, tokens, attention_params, feed_params):
        self.seqs, self.block = tokens.shape[:2]
        self.rows = self.seqs * self.block
        self.count = lax.axis_size("batch") * lax.axis_size("seq")
        self.outer = lax.axis_size("seq") // 4
        self.attention = Blocks(attention_params.shape[0], self.count)
        self.feed = Blocks(feed_params.shape[0], self.count)
        self.reach = 5 * self.block
        self.gather_bounds = [0, self.feed.rows]
        rows = self.attention.rows
        early = (rows - 16) // 32 * 16
        self.attention_bounds = [0, early, rows - 16, rows]
        rows = self.feed.rows
        early = rows - 16
        self.feed_bounds = [0, early // 48 * 16, early // 48 * 32, early, rows]


QUERY = HEADS * HEAD_DIM
BASE_KEY = D * QUERY // LANES
BASE_VALUE = BASE_KEY + D * HEAD_DIM // LANES
BASE_OUT = BASE_VALUE + D * HEAD_DIM // LANES
BASE_GAINS = BASE_OUT + QUERY * D // LANES
STEP = 256


def forward_kernel(geo, tokens, positions, frequency, attention_in, feed_in, *refs):
    (
        feed_held,
        out_wqkv,
        out_wo,
        out_gains,
        out_q,
        out_kv,
        out_merged,
        out_projected,
        out_hidden,
        out_cosine,
        out_sine,
    ) = refs[:11]
    (
        held,
        own_feed,
        shifted,
        flat,
        wqkv,
        wo,
        gains,
        cosine,
        sine,
        lows,
        normed,
        q,
        kv,
        scores,
        probs,
        merged,
        projected,
        hidden,
        send,
        recv,
        local,
    ) = refs[11:]
    place = Place()
    wires, locals_ = Wires(send, recv), Locals(local)
    seqs, block, reach = geo.seqs, geo.block, geo.reach
    align_shard(geo.attention, place, attention_in, shifted, held.at[place.mine()])
    greet(place)
    gather_a = Gather(place, wires, held, 0, geo.attention.rows, 0.5)
    gather_a.begin()
    gather_a.spread(0)
    align_shard(geo.feed, place, feed_in, shifted, own_feed)
    lead = locals_.copy(own_feed, feed_held.at[place.mine()])
    bounds = geo.gather_bounds
    gather_f = [
        Gather(place, wires, feed_held, first, last, 0.875)
        for first, last in zip(bounds, bounds[1:])
    ]

    @pl.when(place.hi == 0)
    def _():
        kv[:, :block] = jnp.zeros((seqs, block, 2 * HEAD_DIM), jnp.bfloat16)

    columns = positions[...].astype(jnp.float32).T
    row = lax.broadcasted_iota(jnp.int32, (block, LANES), 0)
    for s in range(seqs):
        spot = columns[:, s : s + 1]
        angle = spot * frequency[...]
        rows = slice(s * block, (s + 1) * block)
        cosine[rows] = jnp.cos(angle)
        sine[rows] = jnp.sin(angle)
        lows[s] = jnp.maximum(row + 1, row + WINDOW - spot.astype(jnp.int32))

    for j in range(1, geo.outer):
        gather_a.spread(j)
    locals_.finish(lead)
    gather_f[0].begin()
    for j in range(geo.outer):
        gather_a.corner(j)
    gather_f[0].spread(0)
    for j in range(geo.outer):
        gather_a.finish(j)
    gather_a.end()
    pending = []
    for n, part in enumerate(gather_f):
        pending.append([functools.partial(part.spread, j) for j in range(0 if n else 1, geo.outer)])
        if n + 1 < len(gather_f):
            pending[-1].append(gather_f[n + 1].begin)
        for j in range(geo.outer):
            pending.append([functools.partial(part.corner, j)])
        for j in range(geo.outer):
            pending.append([functools.partial(part.finish, j)])

    def tick(amount=1):
        for _ in range(amount):
            if pending:
                for action in pending.pop(0):
                    action()

    flatten_held(geo.attention, held, flat)
    at = BASE_GAINS
    for i, width in enumerate((D, HEAD_DIM, HEAD_DIM, D)):
        gains[i : i + 1, :width] = read_gain(flat, at, width)
        at += width // LANES
    unflatten(flat, BASE_KEY, wqkv, QUERY, HEAD_DIM)
    unflatten(flat, BASE_VALUE, wqkv, QUERY + HEAD_DIM, HEAD_DIM)
    gain = gains[0:1, :]
    gain_key = gains[2:3, :HEAD_DIM]
    halos = []
    per_step = STEP // block
    for s in range(0, seqs, per_step):
        rows = slice(s * block, (s + per_step) * block)
        x = tokens[rows].astype(jnp.float32)
        normed[rows] = (x * root_inverse(x) * gain).astype(jnp.bfloat16)
        made = dot_nn(normed[rows], wqkv[:, QUERY:])
        keys = made[:, :HEAD_DIM]
        keys = turn(keys * root_inverse(keys) * gain_key, cosine[rows], sine[rows])
        for i in range(per_step):
            part = slice(i * block, (i + 1) * block)
            kv[s + i, reach - block :, :HEAD_DIM] = keys[part].astype(jnp.bfloat16)
            kv[s + i, reach - block :, HEAD_DIM:] = made[part, HEAD_DIM:].astype(jnp.bfloat16)
        halo = Halo(place, wires, kv, block, s, per_step)
        halo.outward()
        halos.append(halo)
    unflatten(flat, 0, wqkv, 0, QUERY)
    gain_query = gains[1:2, :HEAD_DIM] * HEAD_DIM**-0.5
    for s in range(0, seqs, per_step):
        rows = slice(s * block, (s + per_step) * block)
        made = dot_nn(normed[rows], wqkv[:, :QUERY])
        for h in range(HEADS):
            one = made[:, h * HEAD_DIM : (h + 1) * HEAD_DIM]
            one = turn(one * root_inverse(one) * gain_query, cosine[rows], sine[rows])
            q[h, rows] = one.astype(jnp.bfloat16)
    unflatten(flat, BASE_OUT, wo, 0, D)
    for src, dst in (
        (wqkv, out_wqkv),
        (wo, out_wo),
        (gains, out_gains),
        (q, out_q),
        (cosine, out_cosine),
        (sine, out_sine),
    ):
        locals_.copy(src, dst)
    chunk = 32
    lane = lax.broadcasted_iota(jnp.int32, (chunk, reach), 1)
    over = lax.broadcasted_iota(jnp.int32, (chunk, reach), 1) - lax.broadcasted_iota(
        jnp.int32, (chunk, reach), 0
    )

    def attend(s, carry):
        start = pl.multiple_of(s * block, block)
        rows = pl.ds(start, block)
        queries = q[:, rows, :].reshape(HEADS * block, HEAD_DIM)
        scores[...] = dot_nt(queries, kv[s, :, :HEAD_DIM])
        for r in range(0, HEADS * block, chunk):
            i = r % block
            low = jnp.concatenate([lows[s, i : i + chunk, :]] * (reach // LANES), axis=-1)
            seen = (lane >= low) & (over <= WINDOW + i)
            raised = jnp.where(seen, jnp.exp(scores[r : r + chunk]), 0.0)
            share = 1.0 / jnp.sum(raised, axis=-1, keepdims=True)
            probs[r : r + chunk] = (raised * share).astype(jnp.bfloat16)
        made = dot_nn(probs[...], kv[s, :, HEAD_DIM:])
        for h in range(HEADS):
            merged[rows, h * HEAD_DIM : (h + 1) * HEAD_DIM] = made[
                h * block : (h + 1) * block
            ].astype(jnp.bfloat16)
        return carry

    count = len(halos)
    for g in range(count + 2):
        tick()
        if g < count:
            halos[g].plane()
        if 1 <= g <= count:
            halos[g - 1].relay()
        tick()
        if g >= 2:
            halos[g - 2].end()
            lax.fori_loop((g - 2) * per_step, (g - 1) * per_step, attend, 0)
    locals_.copy(kv, out_kv)
    locals_.copy(merged, out_merged)
    gain_post = gains[3:4, :]
    for s in range(0, seqs, per_step):
        rows = slice(s * block, (s + per_step) * block)
        made = dot_nn(merged[rows], wo[...])
        projected[rows] = made
        hidden[rows] = tokens[rows].astype(jnp.float32) + made * root_inverse(made) * gain_post
        locals_.copy(projected.at[rows], out_projected.at[rows])
        locals_.copy(hidden.at[rows], out_hidden.at[rows])
    tick(len(pending))
    for part in gather_f:
        part.end()
    wires.drain()
    locals_.drain()


def vmem(shape, dtype):
    return pltpu.VMEM(shape, dtype)


def forward_pass(geo, tokens, positions, attention_block, feed_block):
    count, rows, seqs, block = geo.count, geo.rows, geo.seqs, geo.block
    bf, f4 = jnp.bfloat16, jnp.float32
    half = HEAD_DIM // 2
    frequency = (
        rope_base ** (-(np.arange(half, dtype=np.float32) * np.float32(2.0) / HEAD_DIM))
    ).astype(np.float32)[None]
    wires = len(geo.gather_bounds) * gather_wires(geo.outer) + geo.seqs // 2 * HALO_WIRES
    outs = [
        ((count, geo.feed.rows, LANES), bf),
        ((D, QUERY + 2 * HEAD_DIM), bf),
        ((QUERY, D), bf),
        ((8, D), f4),
        ((HEADS, rows, HEAD_DIM), bf),
        ((seqs, geo.reach, 2 * HEAD_DIM), bf),
        ((rows, QUERY), bf),
        ((rows, D), f4),
        ((rows, D), f4),
        ((rows, half), f4),
        ((rows, half), f4),
    ]
    flat_rows = geo.attention.count * geo.attention.stride + geo.attention.tail
    return pl.pallas_call(
        functools.partial(forward_kernel, geo),
        out_shape=[jax.ShapeDtypeStruct(*out) for out in outs],
        in_specs=[pl.BlockSpec(memory_space=pltpu.VMEM)] * 5,
        out_specs=[pl.BlockSpec(memory_space=pl.ANY)] * len(outs),
        scratch_shapes=[
            vmem((count, geo.attention.rows, LANES), bf),
            vmem((geo.feed.rows, LANES), bf),
            vmem((16 + geo.feed.rows, LANES), f4),
            vmem((flat_rows, LANES), f4),
            vmem((D, QUERY + 2 * HEAD_DIM), bf),
            vmem((QUERY, D), bf),
            vmem((8, D), f4),
            vmem((rows, half), f4),
            vmem((rows, half), f4),
            vmem((seqs, block, LANES), jnp.int32),
            vmem((rows, D), bf),
            vmem((HEADS, rows, HEAD_DIM), bf),
            vmem((seqs, geo.reach, 2 * HEAD_DIM), bf),
            vmem((HEADS * block, geo.reach), f4),
            vmem((HEADS * block, geo.reach), bf),
            vmem((rows, QUERY), bf),
            vmem((rows, D), f4),
            vmem((rows, D), f4),
            pltpu.SemaphoreType.DMA((wires,)),
            pltpu.SemaphoreType.DMA((wires,)),
            pltpu.SemaphoreType.DMA((32,)),
        ],
        compiler_params=pltpu.CompilerParams(
            collective_id=0, has_side_effects=True, vmem_limit_bytes=60 << 20
        ),
    )(tokens.reshape(rows, D), positions, jnp.asarray(frequency), attention_block, feed_block)


MATRIX = D * FF // LANES
BEND = 0.044715
SLOPE = math.sqrt(2.0 / math.pi)


def feed_pieces(blocks, which):
    base, stop = which * MATRIX, (which + 1) * MATRIX
    if which == 2:
        stop = blocks.count * blocks.stride + blocks.tail
    found = []
    for d in range(blocks.count):
        low = max(d * blocks.stride, base)
        high = min(d * blocks.stride + blocks.rows, stop)
        if low < high:
            found.append((d, low - base, high - base, base - d * blocks.stride))
    return found


def feed_phase(geo, locals_, held_in, cotangent_in, mixed_out, split, grad, begin, tick, *refs):
    (flat, twin, down, act, pair, feed_in, turned_in, grad_down) = refs
    mixed = cotangent = feed_in
    blocks = geo.feed
    ends = [-(-(-(-(m + 1) * MATRIX // blocks.stride)) // 4) for m in range(3)]
    starts = [0] + ends[:-1]
    loads = [
        locals_.copy(held_in.at[pl.ds(a, b - a)], split.at[pl.ds(a, b - a)])
        for a, b in zip(starts, ends)
    ]
    load_cotangent = locals_.copy(cotangent_in, grad_down)

    def index(d):
        return d // 4, d // 2 % 2, d % 2

    def unpack(which):
        for d, low, high, shift in feed_pieces(blocks, which):
            mid = min(high, max(low, d * blocks.stride - which * MATRIX + blocks.tail))
            if d and low < mid:
                flat[low:mid] += split[*index(d), low + shift : mid + shift].astype(jnp.float32)
            else:
                mid = low
            flat[mid:high] = split[*index(d), mid + shift : high + shift].astype(jnp.float32)

    def pack(which):
        for d, low, high, shift in feed_pieces(blocks, which):
            split[*index(d), low + shift : high + shift] = flat[low:high].astype(jnp.bfloat16)

    for which, (matrix, first, width) in enumerate(
        ((twin, 0, FF), (twin, FF, FF), (down, 0, D))
    ):
        locals_.finish(loads[which])
        unpack(which)
        unflatten(flat, 0, matrix, first, width)
    gain_feed = read_gain(flat, MATRIX, D)
    gain_out = read_gain(flat, MATRIX + D // LANES, D)

    total, step = geo.rows, STEP
    spans = [slice(r, r + step) for r in range(0, total, step)]
    for rows in spans:
        h = grad[rows]
        feed_in[rows] = (h * root_inverse(h) * gain_feed).astype(jnp.bfloat16)

    def rise(i, carry):
        columns = pl.ds(pl.multiple_of(i * step, step), step)
        others = pl.ds(pl.multiple_of(FF + i * step, step), step)
        for rows in spans:
            g = dot_nn(feed_in[rows], twin[:, columns])
            u = dot_nn(feed_in[rows], twin[:, others])
            square = g * g
            t = jnp.tanh(g * (SLOPE + SLOPE * BEND * square))
            half = 0.5 + 0.5 * t
            soft = g * half
            act[rows, columns] = (soft * u).astype(jnp.bfloat16)
            pair[rows, others] = soft.astype(jnp.bfloat16)
            slope = half * (1.0 + g * (1.0 - t) * (SLOPE + 3.0 * SLOPE * BEND * square))
            pair[rows, columns] = (u * slope).astype(jnp.bfloat16)
        return carry

    lax.fori_loop(0, FF // step, rise, 0)
    turned_in[...] = feed_in[...].T

    def settle(i, sum_out):
        rows = pl.ds(pl.multiple_of(i * step, step), step)
        made = dot_nn(act[rows], down[...])
        r = root_inverse(made)
        mixed[rows] = (grad[rows] + made * r * gain_out).astype(jnp.bfloat16)
        e = grad_down[rows].astype(jnp.float32)
        unit = made * r
        sum_out = sum_out + jnp.sum(e * unit, axis=0, keepdims=True)
        c = e * gain_out
        grad_down[rows] = (
            r * (c - unit * jnp.mean(unit * c, axis=-1, keepdims=True))
        ).astype(jnp.bfloat16)
        return sum_out

    locals_.finish(load_cotangent)
    sum_out = lax.fori_loop(0, total // step, settle, jnp.zeros((1, D), jnp.float32))
    store_mixed = locals_.copy(mixed, mixed_out)

    def fall(i, carry):
        columns = pl.ds(pl.multiple_of(i * step, step), step)
        others = pl.ds(pl.multiple_of(FF + i * step, step), step)
        for rows in spans:
            made = dot_nt(grad_down[rows], down[columns, :])
            for at in (columns, others):
                pair[rows, at] = (made * pair[rows, at].astype(jnp.float32)).astype(jnp.bfloat16)
        return carry

    lax.fori_loop(0, FF // step, fall, 0)

    def back(i, sum_feed):
        rows = pl.ds(pl.multiple_of(i * step, step), step)
        made = dot_nt(pair[rows], twin[...])
        h = grad[rows]
        r = root_inverse(h)
        unit = h * r
        sum_feed = sum_feed + jnp.sum(made * unit, axis=0, keepdims=True)
        c = made * gain_feed
        grad[rows] = cotangent[rows].astype(jnp.float32) + r * (
            c - unit * jnp.mean(unit * c, axis=-1, keepdims=True)
        )
        return sum_feed

    def wide(i, carry, first):
        made = dot_nn(turned_in[...], pair[:, pl.ds(pl.multiple_of(first + i * step, step), step)])
        for k in range(step // LANES):
            flat[pl.ds(i * (step // LANES) + k, D, stride=FF // LANES), :] = made[
                :, k * LANES : (k + 1) * LANES
            ]
        return carry

    locals_.finish(store_mixed)
    load_cotangent = locals_.copy(cotangent_in, cotangent)
    lax.fori_loop(0, FF // step, functools.partial(wide, first=0), 0)
    pack(0)
    lax.fori_loop(0, FF // step, functools.partial(wide, first=FF), 0)
    pack(1)

    def tall(i, carry):
        columns = pl.ds(pl.multiple_of(i * step, step), step)
        made = dot_tn(act[:, columns], grad_down[...])
        for k in range(D // LANES):
            flat[pl.ds(i * (step * D // LANES) + k, step, stride=D // LANES), :] = made[
                :, k * LANES : (k + 1) * LANES
            ]
        return carry

    lax.fori_loop(0, FF // step, tall, 0)
    flat[MATRIX:] = jnp.zeros_like(flat[MATRIX:])
    pack(2)
    begin()
    locals_.finish(load_cotangent)
    sum_feed = jnp.zeros((1, D), jnp.float32)
    for i in range(total // step):
        sum_feed = lax.fori_loop(i, i + 1, back, sum_feed)
        tick()
    write_gain(flat, MATRIX, sum_feed)
    write_gain(flat, MATRIX + D // LANES, sum_out)
    last = blocks.count - 1
    low = blocks.count * blocks.stride - 2 * MATRIX
    split[*index(last), blocks.stride :] = flat[low:].astype(jnp.bfloat16)


class Scatter:
    def __init__(self, place, wires, other, own, lands, result, piece):
        self.place, self.wires, self.other, self.own, self.result = place, wires, other, own, result
        self.by_core, self.first_x, self.first_y, self.second_x, self.second_y, self.by_outer = lands
        first, cut, last, at_x, at_y = piece
        self.split = cut < last
        self.all = pl.ds(first, last - first)
        self.rows_x, self.rows_y = pl.ds(first, cut - first), pl.ds(cut, last - cut)
        self.land_x, self.land_y = pl.ds(at_x, cut - first), pl.ds(at_y, last - cut)
        p, plan = place, wires.plan
        mine, theirs = self.column_of(p.b), self.column_of(1 - p.b)
        self.from_core = plan(
            other.at[:, :, 1 - p.c, self.all], self.by_core.at[:, :, self.all], p.sibling()
        )
        self.from_x = plan(
            own.at[theirs, :, self.rows_x], self.first_x.at[:, :, self.land_x], p.x_peer()
        )
        self.over_y = plan(
            own.at[mine, 1 - p.y, self.rows_x], self.second_y.at[:, self.land_x], p.y_peer()
        )
        if self.split:
            self.from_y = plan(
                own.at[:, 1 - p.y, self.rows_y], self.first_y.at[:, self.land_y], p.y_peer()
            )
            self.over_x = plan(
                own.at[theirs, p.y, self.rows_y], self.second_x.at[:, self.land_y], p.x_peer()
            )
        self.from_outer = [
            plan(
                own.at[p.b * p.outer + p.flip(k), p.y, self.all],
                self.by_outer.at[k - 1, self.all],
                p.flip_peer(k),
            )
            for k in range(1, p.outer)
        ]

    def add(self, i, y, rows, land):
        self.own[i, y, rows] = (
            self.own[i, y, rows].astype(jnp.float32) + land.astype(jnp.float32)
        ).astype(jnp.bfloat16)

    def column_of(self, b):
        return pl.ds(b * self.place.outer, self.place.outer)

    def core(self):
        self.from_core.start()

    def plane(self):
        p = self.place
        self.from_core.wait_recv()

        def body(i, carry):
            for y in range(2):
                self.add(i, y, self.all, self.by_core[i, y, self.all])
            return carry

        lax.fori_loop(0, 2 * p.outer, body, 0)
        self.from_x.start()
        if self.split:
            self.from_y.start()

    def cross(self):
        p = self.place
        self.from_x.wait_recv()

        def body(hi, carry):
            for y in range(2):
                self.add(p.b * p.outer + hi, y, self.rows_x, self.first_x[hi, y, self.land_x])
            return carry

        lax.fori_loop(0, p.outer, body, 0)
        self.over_y.start()
        if self.split:
            self.from_y.wait_recv()

            def body(i, carry):
                self.add(i, p.y, self.rows_y, self.first_y[i, self.land_y])
                return carry

            lax.fori_loop(0, 2 * p.outer, body, 0)
            self.over_x.start()

    def column(self):
        p = self.place
        self.over_y.wait_recv()
        if self.split:
            self.over_x.wait_recv()

        def body(hi, carry):
            i = p.b * p.outer + hi
            self.add(i, p.y, self.rows_x, self.second_y[hi, self.land_x])
            if self.split:
                self.add(i, p.y, self.rows_y, self.second_x[hi, self.land_y])
            return carry

        lax.fori_loop(0, p.outer, body, 0)
        for made in self.from_outer:
            made.start()

    def end(self):
        p = self.place
        total = self.own[p.b * p.outer + p.hi, p.y, self.all].astype(jnp.float32)
        for k, made in enumerate(self.from_outer):
            made.wait_recv()
            total = total + self.by_outer[k, self.all].astype(jnp.float32)
        self.result[self.all] = total


def scatter_wires(outer):
    return 5 + outer - 1


def cut_pieces(bounds):
    pieces, at_x, at_y = [], 0, 0
    for first, last in zip(bounds, bounds[1:]):
        cut = first + max(16, (last - first) // 32 * 16)
        pieces.append((first, cut, last, at_x, at_y))
        at_x, at_y = at_x + cut - first, at_y + last - cut
    return pieces, at_x, at_y


def land_shapes(rows, bounds, outer):
    rows_x, rows_y = cut_pieces(bounds)[1:]
    return [
        pltpu.VMEM(shape + (LANES,), jnp.bfloat16)
        for shape in (
            (2 * outer, 2, rows),
            (outer, 2, rows_x),
            (2 * outer, rows_y),
            (outer, rows_y),
            (outer, rows_x),
            (outer - 1, rows),
        )
    ]


class Return:
    def __init__(self, place, wires, kv, own, by_core, by_y, by_outer, block, first, size):
        self.place, self.wires, self.kv, self.own, self.block = place, wires, kv, own, block
        self.by_core, self.by_y, self.by_outer = by_core, by_y, by_outer
        self.group = pl.ds(first, size)
        self.each = range(first, first + size)

    def rows(self, at):
        return slice(at * self.block, (at + 1) * self.block)

    def slot(self, at):
        return self.kv.at[self.group, pl.ds(at * self.block, self.block)]

    def core(self):
        p = self.place
        self.from_core = [
            self.wires.copy(
                self.slot(at), self.by_core.at[self.group, pl.ds(i * self.block, self.block)], p.sibling()
            )
            for i, at in enumerate((1, 3))
        ]

    def grow(self, s, at, extra):
        rows = self.rows(at)
        self.kv[s, rows] = (self.kv[s, rows].astype(jnp.float32) + extra).astype(jnp.bfloat16)

    def plane(self):
        p = self.place
        for made in self.from_core:
            made.wait_recv()
        for s in self.each:

            @pl.when(p.c == 0)
            def _():
                self.grow(s, 2, self.by_core[s, self.rows(0)].astype(jnp.float32))
                self.own[s] += self.by_core[s, self.rows(1)].astype(jnp.float32)

            @pl.when(p.c == 1)
            def _():
                self.grow(s, 0, self.by_core[s, self.rows(0)].astype(jnp.float32))
                self.grow(s, 2, self.by_core[s, self.rows(1)].astype(jnp.float32))

        self.from_y = self.wires.copy(self.slot(2), self.by_y.at[self.group], p.y_peer())

    def outward(self):
        p = self.place
        self.from_y.wait_recv()
        for s in self.each:

            @pl.when(p.y == 0)
            def _():
                self.own[s] += self.by_y[s].astype(jnp.float32)

            @pl.when(p.y == 1)
            def _():
                self.grow(s, 0, self.by_y[s].astype(jnp.float32))

        self.from_outer = self.wires.copy(
            self.slot(0), self.by_outer.at[self.group], p.outer_peer(p.outer - 1)
        )

    def end(self):
        self.from_outer.wait_recv()
        for s in self.each:
            self.own[s] += self.by_outer[s].astype(jnp.float32)


RETURN_WIRES = 4


def fill_blocks(blocks, split, flat, margin, base, stop):
    even = blocks.stride % 16 == 0
    for d in range(blocks.count):
        low, high = max(d * blocks.stride, base), min(d * blocks.stride + blocks.rows, stop)
        if low >= high:
            continue
        i, y, c = d // 4, d // 2 % 2, d % 2
        first, last = low - d * blocks.stride, high - d * blocks.stride
        if even:
            split[i, y, c, first:last] = flat[low - base + margin : high - base + margin].astype(
                jnp.bfloat16
            )
        else:
            start, end = first // 16 * 16, -(-last // 16) * 16
            source = low - base + margin - (first - start)
            split[i, y, c, start:end] = (
                split[i, y, c, start:end].astype(jnp.float32)
                + flat[source : source + end - start]
            ).astype(jnp.bfloat16)


MARGIN = 16


def backward_kernel(
    geo, positions, gains, tokens_in, wqkv_in, wo_in, q_in, kv_in, merged_in, projected_in,
    hidden_in, cosine_in, sine_in, held_in, cotangent_in, *refs
):
    grad_tokens, mixed_out, attention_sum, feed_sum = refs[:4]
    grad, split_f, split_a, by_core_kv, by_y_kv, by_outer_kv = refs[4:10]
    lands_a, lands_f = refs[10:16], refs[16:22]
    send, recv, local = refs[22:]
    place = Place()
    wires, locals_ = Wires(send, recv), Locals(local)
    bf, f4, rows, half = jnp.bfloat16, jnp.float32, geo.rows, HEAD_DIM // 2
    load_hidden = locals_.copy(hidden_in, grad)
    greet(place)
    pieces = cut_pieces(geo.feed_bounds)[0]
    own_f = split_f.at[:, :, place.c]
    one, two, three, four = [
        Scatter(place, wires, split_f, own_f, lands_f, feed_sum, piece) for piece in pieces
    ]

    def begin():
        for part in (one, two, three):
            part.core()

    pending = [
        [], [one.plane], [], [two.plane],
        [three.plane],
        [one.cross], [], [two.cross, one.column], [three.cross],
        [],
        [two.column, four.plane],
        [three.column, one.end, four.cross],
        [two.end, four.column],
        [three.end, four.end],
    ]

    def tick():
        for action in pending.pop(0):
            action()

    locals_.finish(load_hidden)
    pl.run_scoped(
        functools.partial(
            feed_phase, geo, locals_, held_in, cotangent_in, mixed_out, split_f, grad, begin, tick
        ),
        vmem((MATRIX + geo.feed.tail, LANES), f4),
        vmem((D, 2 * FF), bf),
        vmem((FF, D), bf),
        vmem((rows, FF), bf),
        vmem((rows, 2 * FF), bf),
        vmem((rows, D), bf),
        vmem((D, rows), bf),
        vmem((rows, D), bf),
    )
    four.core()
    pl.run_scoped(
        functools.partial(
            attention_phase, geo, place, wires, locals_, positions, gains,
            (tokens_in, wqkv_in, wo_in, q_in, kv_in, merged_in, projected_in, cosine_in, sine_in),
            grad_tokens, attention_sum, grad, split_a, by_core_kv, by_y_kv, by_outer_kv, lands_a,
            pending, tick,
        ),
        vmem((rows, D), bf),
        vmem(wqkv_in.shape, bf),
        vmem(wo_in.shape, bf),
        vmem(q_in.shape, bf),
        vmem(kv_in.shape, bf),
        vmem((rows, QUERY + 2 * HEAD_DIM), bf),
        vmem((rows, half), f4),
        vmem((rows, half), f4),
        vmem((2 * geo.reach, D), f4),
        vmem((rows, D), bf),
        vmem((max(D, geo.reach), max(rows, 2 * HEADS * geo.block)), bf),
        vmem((HEADS, rows, HEAD_DIM), bf),
        vmem((rows, D), bf),
        vmem((geo.seqs, geo.block, 2 * HEAD_DIM), f4),
        vmem((2 * MARGIN + QUERY * D // LANES, LANES), f4),
    )


def attention_phase(
    geo, place, wires, locals_, positions, gains, saved, grad_tokens, attention_sum, grad,
    split, by_core_kv, by_y_kv, by_outer_kv, lands_a, pending, tick, *refs
):
    tokens_in, wqkv_in, wo_in, q_in, kv_in, merged_in, projected_in, cosine_in, sine_in = saved
    (
        tokens, wqkv, wo, q, kv, pair, cosine, sine, work, normed, shared, grad_out, out_rows,
        own_kv, flat,
    ) = refs
    seqs, block, reach, total, step = geo.seqs, geo.block, geo.reach, geo.rows, STEP
    turned = shared.at[pl.ds(0, D), pl.ds(0, total)]
    probs = shared.at[pl.ds(0, reach), pl.ds(0, HEADS * block)]
    logits = shared.at[pl.ds(0, reach), pl.ds(HEADS * block, HEADS * block)]
    projected = work.at[pl.ds(0, total)]
    scores = work.at[pl.ds(0, reach), pl.ds(0, HEADS * block)]
    slopes = work.at[pl.ds(reach, reach), pl.ds(0, HEADS * block)]
    load_projected = locals_.copy(projected_in, projected)
    load_wo = locals_.copy(wo_in, wo)
    load_tokens = locals_.copy(tokens_in, tokens)
    load_merged = locals_.copy(merged_in, pair.at[:, pl.ds(0, QUERY)])
    load_q, load_kv = locals_.copy(q_in, q), locals_.copy(kv_in, kv)
    load_rest = [
        locals_.copy(wqkv_in, wqkv), locals_.copy(cosine_in, cosine), locals_.copy(sine_in, sine)
    ]
    gain_attention, gain_query = gains[0:1, :], gains[1:2, :HEAD_DIM]
    gain_key, gain_post = gains[2:3, :HEAD_DIM], gains[3:4, :]
    for made in (load_projected, load_wo, load_tokens):
        locals_.finish(made)

    def start_rows(i, summed):
        rows = pl.ds(pl.multiple_of(i * step, step), step)
        made, e = projected[rows], grad[rows]
        r = root_inverse(made)
        unit = made * r
        c = e * gain_post
        out_rows[rows] = (r * (c - unit * jnp.mean(unit * c, axis=-1, keepdims=True))).astype(
            jnp.bfloat16
        )
        x = tokens[rows].astype(jnp.float32)
        normed[rows] = (x * root_inverse(x) * gain_attention).astype(jnp.bfloat16)
        for h in range(HEADS):
            grad_out[h, rows] = dot_nt(
                out_rows[rows], wo[h * HEAD_DIM : (h + 1) * HEAD_DIM, :]
            ).astype(jnp.bfloat16)
        return summed + jnp.sum(e * unit, axis=0, keepdims=True)

    sum_post = lax.fori_loop(0, total // step, start_rows, jnp.zeros((1, D), jnp.float32))
    tick()
    blocks = geo.attention
    flat[0:MARGIN] = jnp.zeros((MARGIN, LANES), jnp.float32)
    flat[MARGIN + QUERY * D // LANES :] = jnp.zeros((MARGIN, LANES), jnp.float32)
    if blocks.stride % 16:
        split[...] = jnp.zeros_like(split)
    locals_.finish(load_merged)

    for made in [load_q, load_kv] + load_rest:
        locals_.finish(made)

    wide = HEADS * block
    chunk = 32
    lane = lax.rem(lax.broadcasted_iota(jnp.int32, (chunk, wide), 1), block)
    line = lax.broadcasted_iota(jnp.int32, (chunk, wide), 0)

    def attend(s, carry):
        rows = pl.ds(pl.multiple_of(s * block, block), block)
        queries = q[:, rows, :].reshape(wide, HEAD_DIM)
        given = grad_out[:, rows, :].reshape(wide, HEAD_DIM)
        scores[...] = dot_nt(kv[s, :, :HEAD_DIM], queries)
        slopes[...] = dot_nt(kv[s, :, HEAD_DIM:], given)
        spot = jnp.concatenate([positions[pl.ds(s, 1), :]] * HEADS, axis=-1)
        low = jnp.maximum(lane[0:1] + 1, lane[0:1] + WINDOW - spot)
        total_e = jnp.zeros((8, wide), jnp.float32)
        total_d = jnp.zeros((8, wide), jnp.float32)
        for r in range(0, reach, chunk):
            seen = (line + r >= low) & (line + (r - WINDOW) <= lane)
            raised = jnp.where(seen, jnp.exp(scores[r : r + chunk]), 0.0)
            scores[r : r + chunk] = raised
            moved = raised * slopes[r : r + chunk]
            for k in range(0, chunk, 8):
                total_e = total_e + raised[k : k + 8]
                total_d = total_d + moved[k : k + 8]
        share = 1.0 / jnp.sum(total_e, axis=0, keepdims=True)
        inner = jnp.sum(total_d, axis=0, keepdims=True) * share
        for r in range(0, reach, chunk):
            p = scores[r : r + chunk] * share
            probs[r : r + chunk] = p.astype(jnp.bfloat16)
            logits[r : r + chunk] = (p * (slopes[r : r + chunk] - inner)).astype(jnp.bfloat16)
        grad_q = dot_tn(logits[...], kv[s, :, :HEAD_DIM]) * HEAD_DIM**-0.5
        grad_k = dot_nn(logits[...], queries)
        grad_v = dot_nn(probs[...], given)
        early = reach - block
        kv[s, :early, :HEAD_DIM] = grad_k[:early].astype(jnp.bfloat16)
        kv[s, :early, HEAD_DIM:] = grad_v[:early].astype(jnp.bfloat16)
        own_kv[s, :, :HEAD_DIM] = grad_k[early:]
        own_kv[s, :, HEAD_DIM:] = grad_v[early:]
        for h in range(HEADS):
            q[h, rows] = grad_q[h * block : (h + 1) * block].astype(jnp.bfloat16)
        return carry

    size = 2
    returns = [
        Return(place, wires, kv, own_kv, by_core_kv, by_y_kv, by_outer_kv, block, s, size)
        for s in range(0, seqs, size)
    ]
    for g, group in enumerate(returns):
        lax.fori_loop(g * size, (g + 1) * size, attend, 0)
        group.core()
        if g >= 1:
            returns[g - 1].plane()
        if g >= 2:
            returns[g - 2].outward()
        tick()
    last = len(returns) - 1
    turned[...] = normed[...].T

    def tall(i, carry):
        columns = pl.ds(pl.multiple_of(i * step, step), step)
        made = dot_tn(pair[:, columns], out_rows[...])
        for k in range(D // LANES):
            flat[pl.ds(MARGIN + i * (step * D // LANES) + k, step, stride=D // LANES), :] = made[
                :, k * LANES : (k + 1) * LANES
            ]
        return carry

    lax.fori_loop(0, QUERY // step, tall, 0)
    fill_blocks(blocks, split, flat, MARGIN, BASE_OUT, BASE_GAINS)
    def query_rows(i, summed):
        rows = pl.ds(pl.multiple_of(i * step, step), step)
        made = dot_nn(normed[rows], wqkv[:, :QUERY])
        for h in range(HEADS):
            raw = made[:, h * HEAD_DIM : (h + 1) * HEAD_DIM]
            e = turn_back(q[h, rows].astype(jnp.float32), cosine[rows], sine[rows])
            r = root_inverse(raw)
            unit = raw * r
            summed = summed + jnp.sum(e * unit, axis=0, keepdims=True)
            c = e * gain_query
            pair[rows, h * HEAD_DIM : (h + 1) * HEAD_DIM] = (
                r * (c - unit * jnp.mean(unit * c, axis=-1, keepdims=True))
            ).astype(jnp.bfloat16)
        return summed

    returns[last].plane()
    returns[last - 1].outward()
    tick()
    sum_query = lax.fori_loop(0, total // step, query_rows, jnp.zeros((1, HEAD_DIM), jnp.float32))
    returns[last].outward()
    tick()

    def broad(i, carry, first, width):
        columns = pl.ds(pl.multiple_of(first + i * step, step), step)
        made = dot_nn(turned[...], pair[:, columns])
        for k in range(step // LANES):
            start = MARGIN + i * (step // LANES) + k
            flat[pl.ds(start, D, stride=width // LANES), :] = made[:, k * LANES : (k + 1) * LANES]
        return carry

    lax.fori_loop(0, QUERY // step, functools.partial(broad, first=0, width=QUERY), 0)
    fill_blocks(blocks, split, flat, MARGIN, 0, BASE_KEY)
    tick()
    for group in returns:
        group.end()

    def key_rows(i, summed):
        rows = pl.ds(pl.multiple_of(i * step, step), step)
        per = step // block
        raw = dot_nn(normed[rows], wqkv[:, QUERY : QUERY + HEAD_DIM])
        both = own_kv[pl.ds(i * per, per)].reshape(step, 2 * HEAD_DIM)
        e = turn_back(both[:, :HEAD_DIM], cosine[rows], sine[rows])
        r = root_inverse(raw)
        unit = raw * r
        c = e * gain_key
        pair[rows, QUERY : QUERY + HEAD_DIM] = (
            r * (c - unit * jnp.mean(unit * c, axis=-1, keepdims=True))
        ).astype(jnp.bfloat16)
        pair[rows, QUERY + HEAD_DIM :] = both[:, HEAD_DIM:].astype(jnp.bfloat16)
        return summed + jnp.sum(e * unit, axis=0, keepdims=True)

    sum_key = lax.fori_loop(0, total // step, key_rows, jnp.zeros((1, HEAD_DIM), jnp.float32))
    for first, base in ((QUERY, BASE_KEY), (QUERY + HEAD_DIM, BASE_VALUE)):
        broad(0, 0, first, HEAD_DIM)
        size_rows = D * HEAD_DIM // LANES
        flat[MARGIN + size_rows : 2 * MARGIN + size_rows] = jnp.zeros((MARGIN, LANES), jnp.float32)
        fill_blocks(blocks, split, flat, MARGIN, base, base + size_rows)

    def end_rows(i, summed):
        rows = pl.ds(pl.multiple_of(i * step, step), step)
        made = dot_nt(pair[rows], wqkv[...])
        x = tokens[rows].astype(jnp.float32)
        r = root_inverse(x)
        unit = x * r
        c = made * gain_attention
        grad[rows] = grad[rows] + r * (c - unit * jnp.mean(unit * c, axis=-1, keepdims=True))
        return summed + jnp.sum(made * unit, axis=0, keepdims=True)

    tail = geo.attention.tail
    own = split.at[:, :, place.c]
    one, two, three = [
        Scatter(place, wires, split, own, lands_a, attention_sum, piece)
        for piece in cut_pieces(geo.attention_bounds)[0]
    ]
    one.core()
    two.core()
    tick()
    sum_attention = jnp.zeros((1, D), jnp.float32)
    half = total // step // 2
    one.plane()
    sum_attention = lax.fori_loop(0, half, end_rows, sum_attention)
    two.plane()
    sum_attention = lax.fori_loop(half, 2 * half, end_rows, sum_attention)
    locals_.copy(grad, grad_tokens)
    tick()
    flat[MARGIN : 2 * MARGIN + tail] = jnp.zeros((MARGIN + tail, LANES), jnp.float32)
    at = MARGIN
    for made in (sum_attention, sum_query, sum_key, sum_post):
        write_gain(flat, at, made)
        at += made.shape[1] // LANES
    fill_blocks(blocks, split, flat, MARGIN, BASE_GAINS, blocks.count * blocks.stride + tail)
    three.core()
    for action in (
        one.cross, three.plane, two.cross, one.column, three.cross, two.column, three.column,
        one.end, two.end, three.end,
    ):
        action()
    wires.drain()
    locals_.drain()


def backward_pass(geo, tokens, positions, saved, hidden, feed_held, cotangent):
    bf, f4, rows, seqs, block = jnp.bfloat16, jnp.float32, geo.rows, geo.seqs, geo.block
    wqkv, wo, gains, q, kv, merged, projected, cosine, sine = saved
    rows_a, rows_f, outer = geo.attention.rows, geo.feed.rows, geo.outer
    outs = [((rows, D), f4), ((rows, D), bf), ((rows_a, LANES), f4), ((rows_f, LANES), f4)]
    full, hbm = pl.BlockSpec(memory_space=pltpu.VMEM), pl.BlockSpec(memory_space=pl.ANY)
    wires = (len(geo.feed_bounds) + len(geo.attention_bounds) - 2) * scatter_wires(
        outer
    ) + seqs // 2 * RETURN_WIRES
    return pl.pallas_call(
        functools.partial(backward_kernel, geo),
        out_shape=[jax.ShapeDtypeStruct(*out) for out in outs],
        in_specs=[full] * 2 + [hbm] * 12,
        out_specs=[hbm, hbm, full, full],
        scratch_shapes=[
            vmem((rows, D), f4),
            vmem((2 * outer, 2, 2, rows_f, LANES), bf),
            vmem((2 * outer, 2, 2, rows_a, LANES), bf),
            vmem((seqs, 2 * block, 2 * HEAD_DIM), bf),
            vmem((seqs, block, 2 * HEAD_DIM), bf),
            vmem((seqs, block, 2 * HEAD_DIM), bf),
        ]
        + land_shapes(rows_a, geo.attention_bounds, outer)
        + land_shapes(rows_f, geo.feed_bounds, outer)
        + [
            pltpu.SemaphoreType.DMA((wires,)),
            pltpu.SemaphoreType.DMA((wires,)),
            pltpu.SemaphoreType.DMA((32,)),
        ],
        compiler_params=pltpu.CompilerParams(
            collective_id=1, has_side_effects=True, vmem_limit_bytes=63 << 20
        ),
    )(
        positions, gains, tokens.reshape(rows, D), wqkv, wo, q, kv, merged, projected, hidden,
        cosine, sine, feed_held.reshape(2 * outer, 2, 2, rows_f, LANES), cotangent.reshape(rows, D),
    )


def on_device(tokens, attention_params, feed_params, positions, cotangent):
    geo = Geo(tokens, attention_params, feed_params)
    device = lax.axis_index("batch") * lax.axis_size("seq") + lax.axis_index("seq")
    (
        feed_held, wqkv, weight_out, gains, q, kv, merged, projected, hidden, cosine, sine,
    ) = forward_pass(
        geo, tokens, positions, geo.attention.pad(attention_params), geo.feed.pad(feed_params)
    )
    grad_tokens, mixed, attention_sum, feed_sum = backward_pass(
        geo,
        tokens,
        positions,
        (wqkv, weight_out, gains, q, kv, merged, projected, cosine, sine),
        hidden,
        feed_held,
        cotangent,
    )
    return (
        mixed.reshape(tokens.shape),
        grad_tokens.reshape(tokens.shape),
        geo.attention.take(attention_sum, device),
        geo.feed.take(feed_sum, device),
    )


def solution(mesh):
    return jax.shard_map(
        on_device,
        mesh=mesh,
        in_specs=(
            P("batch", "seq", None),
            P(("batch", "seq")),
            P(("batch", "seq")),
            P("batch", "seq"),
            P("batch", "seq", None),
        ),
        out_specs=(
            P("batch", "seq", None),
            P("batch", "seq", None),
            P(("batch", "seq")),
            P(("batch", "seq")),
        ),
        check_vma=False,
    )
```

```python
import functools
import math

import jax
import jax.numpy as jnp
import numpy as np
from jax import lax
from jax.experimental import pallas as pl
from jax.experimental.pallas import tpu as pltpu
from jax.sharding import PartitionSpec as P

MESH = pl.DeviceIdType.MESH
LANES = 128

D = 640
HEADS = 4
HEAD_DIM = 256
FF = 2048
WINDOW = 512


rope_base = 10000.0


class Place:
    def __init__(self):
        self.devices_seq = lax.axis_size("seq")
        self.outer = self.devices_seq // 4
        self.count = 2 * self.devices_seq
        self.b = lax.axis_index("batch")
        s = lax.axis_index("seq")
        self.hi = lax.div(s, 4)
        self.y = lax.rem(lax.div(s, 2), 2)
        self.c = lax.rem(s, 2)

    def block(self, b, hi, y, c):
        return b * self.devices_seq + hi * 4 + y * 2 + c

    def seq_id(self, hi, y, c):
        return (self.b, hi * 4 + y * 2 + c)

    def mine(self):
        return self.block(self.b, self.hi, self.y, self.c)

    def x_peer(self):
        return (1 - self.b, self.hi * 4 + self.y * 2 + self.c)

    def y_peer(self):
        return self.seq_id(self.hi, 1 - self.y, self.c)

    def sibling(self):
        return self.seq_id(self.hi, self.y, 1 - self.c)

    def outer_at(self, k):
        return lax.rem(self.hi + k, self.outer)

    def flip(self, k):
        found, bit = 0, 1
        while bit < self.outer:
            own = lax.rem(lax.div(self.hi, bit), 2)
            found = found + bit * ((1 - own) if k & bit else own)
            bit *= 2
        return found

    def flip_peer(self, k):
        return self.seq_id(self.flip(k), self.y, self.c)

    def outer_peer(self, k):
        return self.seq_id(self.outer_at(k), self.y, self.c)

    def peers(self):
        return [self.x_peer(), self.y_peer(), self.sibling()] + [
            self.outer_peer(k) for k in range(1, self.outer)
        ]


def greet(place):
    barrier = pltpu.get_barrier_semaphore()
    peers = place.peers()
    for peer in peers:
        pl.semaphore_signal(barrier, inc=1, device_id=peer, device_id_type=MESH)
    pl.semaphore_wait(barrier, len(peers))


def guarded(when, action):
    if when is None:
        action()
    else:
        pl.when(when)(action)


class Wires:
    def __init__(self, send_sems, recv_sems):
        self.send_sems, self.recv_sems = send_sems, recv_sems
        self.used = 0
        self.sent = []

    def plan(self, src, dst, peer, when=None):
        made = pltpu.make_async_remote_copy(
            src_ref=src,
            dst_ref=dst,
            send_sem=self.send_sems.at[self.used],
            recv_sem=self.recv_sems.at[self.used],
            device_id=peer,
            device_id_type=MESH,
        )
        self.used += 1
        self.sent.append((made, when))
        return made

    def copy(self, src, dst, peer, when=None):
        made = self.plan(src, dst, peer, when)
        guarded(when, made.start)
        return made

    def drain(self):
        for made, when in self.sent:
            guarded(when, made.wait_send)
        self.sent = []


def gather_wires(outer):
    return outer - 1 + 4 * outer + 4 * outer


class Gather:
    def __init__(self, place, wires, held, first, last, share):
        self.place, self.wires, self.held = place, wires, held
        self.first, self.last = first, last
        self.cut = first + int((last - first) * share) // 16 * 16
        self.from_outer = {}
        self.from_x, self.from_y, self.diag, self.twin = {}, {}, {}, []

    def send(self, index, peer, first=None, last=None):
        first = self.first if first is None else first
        last = self.last if last is None else last
        ref = self.held.at[index, pl.ds(first, last - first)]
        return self.wires.copy(ref, ref, peer)

    def begin(self):
        p = self.place
        for k in range(1, p.outer):
            self.from_outer[k] = self.send(p.mine(), p.flip_peer(k))

    def spread(self, j):
        p = self.place
        if j:
            self.from_outer[j].wait_recv()
        index = p.block(p.b, p.flip(j), p.y, p.c)
        self.from_y[j] = self.send(index, p.y_peer())
        self.from_x[j] = self.send(index, p.x_peer())
        self.twin.append(self.send(index, p.sibling()))

    def corner(self, j):
        p = self.place
        at = p.flip(j)
        self.from_y[j].wait_recv()
        got = p.block(p.b, at, 1 - p.y, p.c)
        down = self.send(got, p.x_peer(), self.first, self.cut)
        self.twin.append(self.send(got, p.sibling()))
        self.from_x[j].wait_recv()
        got = p.block(1 - p.b, at, p.y, p.c)
        across = self.send(got, p.y_peer(), self.cut, self.last)
        self.twin.append(self.send(got, p.sibling()))
        self.diag[j] = (down, across)

    def finish(self, j):
        p = self.place
        for made in self.diag[j]:
            made.wait_recv()
        self.twin.append(self.send(p.block(1 - p.b, p.flip(j), 1 - p.y, p.c), p.sibling()))

    def end(self):
        for made in self.twin:
            made.wait_recv()


class Blocks:
    def __init__(self, length, count):
        self.length, self.count = length, count
        self.stride, self.rest = divmod(length, LANES)
        needed = -(-(length + self.rest * (count - 1)) // LANES)
        self.rows = -(-needed // 16) * 16
        self.tail = self.rows - self.stride
        self.total = length * count

    def pad(self, shard):
        return jnp.pad(shard, (0, self.rows * LANES - self.length)).reshape(self.rows, LANES)

    def take(self, block, index):
        return lax.dynamic_slice(block.reshape(-1), (self.rest * index,), (self.length,))


EPS = 1e-06


def root_inverse(rows):
    return lax.rsqrt(jnp.mean(rows * rows, axis=-1, keepdims=True) + EPS)


def turn(rows, cosine, sine):
    half = rows.shape[-1] // 2
    first, second = rows[:, :half], rows[:, half:]
    return jnp.concatenate([first * cosine - second * sine, second * cosine + first * sine], axis=-1)


def turn_back(rows, cosine, sine):
    half = rows.shape[-1] // 2
    first, second = rows[:, :half], rows[:, half:]
    return jnp.concatenate([first * cosine + second * sine, second * cosine - first * sine], axis=-1)


def dot_nn(left, right):
    return jnp.dot(left, right, preferred_element_type=jnp.float32)


def dot_nt(left, right):
    return lax.dot_general(left, right, (((1,), (1,)), ((), ())), preferred_element_type=jnp.float32)


def dot_tn(left, right):
    return lax.dot_general(left, right, (((0,), (0,)), ((), ())), preferred_element_type=jnp.float32)


def align_shard(blocks, place, padded_ref, shifted, aligned):
    offset = blocks.rest * place.mine()
    down, right = lax.div(offset, LANES), lax.rem(offset, LANES)
    rows = blocks.rows
    shifted[0:16] = jnp.zeros((16, LANES), jnp.float32)
    shifted[16 : 16 + rows] = pltpu.roll(padded_ref[...].astype(jnp.float32), right, 1)
    lane = lax.broadcasted_iota(jnp.int32, (rows, LANES), 1)
    aligned[...] = jnp.where(
        lane >= right, shifted[pl.ds(16 - down, rows)], shifted[pl.ds(15 - down, rows)]
    ).astype(aligned.dtype)


def flatten_held(blocks, held, flat):
    stride, tail, rows = blocks.stride, blocks.tail, blocks.rows
    if stride % 16 == 0 and tail == 16:
        flat[0:tail] = held[0, 0:tail].astype(jnp.float32)
        flat[tail:rows] = held[0, tail:rows].astype(jnp.float32)

        def body(d, carry):
            start = pl.multiple_of(d * stride, 16)
            flat[pl.ds(start, tail)] += held[d, 0:tail].astype(jnp.float32)
            start = pl.multiple_of(d * stride + tail, 16)
            flat[pl.ds(start, stride)] = held[d, tail:rows].astype(jnp.float32)
            return carry

        lax.fori_loop(1, blocks.count, body, 0)
    else:
        flat[...] = jnp.zeros_like(flat)

        def body(d, carry):
            flat[pl.ds(d * stride, rows)] += held[d].astype(jnp.float32)
            return carry

        lax.fori_loop(0, blocks.count, body, 0)


def unflatten(flat, base, matrix, first, width):
    height, steps = matrix.shape[0], width // LANES
    for i in range(steps):
        matrix[:, first + i * LANES : first + (i + 1) * LANES] = flat[
            pl.ds(base + i, height, stride=steps), :
        ].astype(matrix.dtype)


def write_gain(flat, base, gain):
    for i in range(gain.shape[1] // LANES):
        flat[base + i : base + i + 1, :] = gain[:, i * LANES : (i + 1) * LANES]


def read_gain(flat, base, width):
    return jnp.concatenate([flat[base + i : base + i + 1, :] for i in range(width // LANES)], axis=-1)


class Halo:
    def __init__(self, place, wires, kv, block, first, size):
        self.place, self.wires, self.kv, self.block = place, wires, kv, block
        self.first, self.size = first, size

    def slot(self, at):
        return self.kv.at[pl.ds(self.first, self.size), pl.ds(pl.multiple_of(at * self.block, 128), self.block)]

    def outward(self):
        p = self.place
        self.outer = self.wires.copy(
            self.slot(4), self.slot(0), p.outer_peer(1), p.hi + 1 < p.outer
        )

    def plane(self):
        p = self.place
        guarded(p.hi > 0, self.outer.wait_recv)
        self.across = self.wires.copy(self.slot(4 * (1 - p.y)), self.slot(2), p.y_peer())
        self.near = self.wires.copy(self.slot(4 * (1 - p.c)), self.slot(3 - 2 * p.c), p.sibling())

    def relay(self):
        p = self.place
        self.across.wait_recv()
        self.far = self.wires.copy(self.slot(2), self.slot(1 + 2 * p.c), p.sibling())

    def end(self):
        self.near.wait_recv()
        self.far.wait_recv()


HALO_WIRES = 4


class Locals:
    def __init__(self, sems):
        self.sems, self.used, self.open = sems, 0, []

    def copy(self, src, dst):
        made = pltpu.make_async_copy(src, dst, self.sems.at[self.used])
        self.used += 1
        self.open.append(made)
        made.start()
        return made

    def finish(self, made):
        made.wait()
        self.open = [other for other in self.open if other is not made]

    def drain(self):
        for made in self.open:
            made.wait()
        self.open = []


class Geo:
    def __init__(self, tokens, attention_params, feed_params):
        self.seqs, self.block = tokens.shape[:2]
        self.rows = self.seqs * self.block
        self.count = lax.axis_size("batch") * lax.axis_size("seq")
        self.outer = lax.axis_size("seq") // 4
        self.attention = Blocks(attention_params.shape[0], self.count)
        self.feed = Blocks(feed_params.shape[0], self.count)
        self.reach = 5 * self.block
        self.gather_bounds = [0, self.feed.rows]
        rows = self.attention.rows
        early = (rows - 16) // 32 * 16
        self.attention_bounds = [0, early, rows - 16, rows]
        rows = self.feed.rows
        early = rows - 16
        self.feed_bounds = [0, early // 48 * 16, early // 48 * 32, early, rows]


QUERY = HEADS * HEAD_DIM
BASE_KEY = D * QUERY // LANES
BASE_VALUE = BASE_KEY + D * HEAD_DIM // LANES
BASE_OUT = BASE_VALUE + D * HEAD_DIM // LANES
BASE_GAINS = BASE_OUT + QUERY * D // LANES
STEP = 256
WIDE = 512


def forward_kernel(geo, tokens, positions, frequency, attention_in, feed_in, *refs):
    (
        feed_held,
        out_wqkv,
        out_wo,
        out_gains,
        out_q,
        out_kv,
        out_merged,
        out_projected,
        out_hidden,
        out_cosine,
        out_sine,
    ) = refs[:11]
    (
        held,
        own_feed,
        shifted,
        flat,
        wqkv,
        wo,
        gains,
        cosine,
        sine,
        lows,
        normed,
        q,
        kv,
        scores,
        probs,
        merged,
        projected,
        hidden,
        send,
        recv,
        local,
    ) = refs[11:]
    place = Place()
    wires, locals_ = Wires(send, recv), Locals(local)
    seqs, block, reach = geo.seqs, geo.block, geo.reach
    align_shard(geo.attention, place, attention_in, shifted, held.at[place.mine()])
    greet(place)
    gather_a = Gather(place, wires, held, 0, geo.attention.rows, 0.5)
    gather_a.begin()
    gather_a.spread(0)
    align_shard(geo.feed, place, feed_in, shifted, own_feed)
    lead = locals_.copy(own_feed, feed_held.at[place.mine()])
    bounds = geo.gather_bounds
    gather_f = [
        Gather(place, wires, feed_held, first, last, 0.875)
        for first, last in zip(bounds, bounds[1:])
    ]

    @pl.when(place.hi == 0)
    def _():
        kv[:, :block] = jnp.zeros((seqs, block, 2 * HEAD_DIM), jnp.bfloat16)

    columns = positions[...].astype(jnp.float32).T
    row = lax.broadcasted_iota(jnp.int32, (block, LANES), 0)
    for s in range(seqs):
        spot = columns[:, s : s + 1]
        angle = spot * frequency[...]
        rows = slice(s * block, (s + 1) * block)
        cosine[rows] = jnp.cos(angle)
        sine[rows] = jnp.sin(angle)
        lows[s] = jnp.maximum(row + 1, row + WINDOW - spot.astype(jnp.int32))

    for j in range(1, geo.outer):
        gather_a.spread(j)
    locals_.finish(lead)
    gather_f[0].begin()
    for j in range(geo.outer):
        gather_a.corner(j)
    gather_f[0].spread(0)
    for j in range(geo.outer):
        gather_a.finish(j)
    gather_a.end()
    pending = []
    for n, part in enumerate(gather_f):
        pending.append([functools.partial(part.spread, j) for j in range(0 if n else 1, geo.outer)])
        if n + 1 < len(gather_f):
            pending[-1].append(gather_f[n + 1].begin)
        for j in range(geo.outer):
            pending.append([functools.partial(part.corner, j)])
        for j in range(geo.outer):
            pending.append([functools.partial(part.finish, j)])

    def tick(amount=1):
        for _ in range(amount):
            if pending:
                for action in pending.pop(0):
                    action()

    flatten_held(geo.attention, held, flat)
    at = BASE_GAINS
    for i, width in enumerate((D, HEAD_DIM, HEAD_DIM, D)):
        gains[i : i + 1, :width] = read_gain(flat, at, width)
        at += width // LANES
    unflatten(flat, BASE_KEY, wqkv, QUERY, HEAD_DIM)
    unflatten(flat, BASE_VALUE, wqkv, QUERY + HEAD_DIM, HEAD_DIM)
    gain = gains[0:1, :]
    gain_key = gains[2:3, :HEAD_DIM]
    halos = []
    per_step = STEP // block
    for s in range(0, seqs, per_step):
        rows = slice(s * block, (s + per_step) * block)
        x = tokens[rows].astype(jnp.float32)
        normed[rows] = (x * root_inverse(x) * gain).astype(jnp.bfloat16)
        made = dot_nn(normed[rows], wqkv[:, QUERY:])
        keys = made[:, :HEAD_DIM]
        keys = turn(keys * root_inverse(keys) * gain_key, cosine[rows], sine[rows])
        for i in range(per_step):
            part = slice(i * block, (i + 1) * block)
            kv[s + i, reach - block :, :HEAD_DIM] = keys[part].astype(jnp.bfloat16)
            kv[s + i, reach - block :, HEAD_DIM:] = made[part, HEAD_DIM:].astype(jnp.bfloat16)
        halo = Halo(place, wires, kv, block, s, per_step)
        halo.outward()
        halos.append(halo)
    unflatten(flat, 0, wqkv, 0, QUERY)
    gain_query = gains[1:2, :HEAD_DIM] * HEAD_DIM**-0.5
    for s in range(0, seqs, per_step):
        rows = slice(s * block, (s + per_step) * block)
        made = dot_nn(normed[rows], wqkv[:, :QUERY])
        for h in range(HEADS):
            one = made[:, h * HEAD_DIM : (h + 1) * HEAD_DIM]
            one = turn(one * root_inverse(one) * gain_query, cosine[rows], sine[rows])
            q[h, rows] = one.astype(jnp.bfloat16)
    unflatten(flat, BASE_OUT, wo, 0, D)
    for src, dst in (
        (wqkv, out_wqkv),
        (wo, out_wo),
        (gains, out_gains),
        (q, out_q),
        (cosine, out_cosine),
        (sine, out_sine),
    ):
        locals_.copy(src, dst)
    chunk = 32
    lane = lax.broadcasted_iota(jnp.int32, (chunk, reach), 1)
    over = lax.broadcasted_iota(jnp.int32, (chunk, reach), 1) - lax.broadcasted_iota(
        jnp.int32, (chunk, reach), 0
    )

    def attend(s, carry):
        start = pl.multiple_of(s * block, block)
        rows = pl.ds(start, block)
        queries = q[:, rows, :].reshape(HEADS * block, HEAD_DIM)
        scores[...] = dot_nt(queries, kv[s, :, :HEAD_DIM])
        for r in range(0, HEADS * block, chunk):
            i = r % block
            low = jnp.concatenate([lows[s, i : i + chunk, :]] * (reach // LANES), axis=-1)
            seen = (lane >= low) & (over <= WINDOW + i)
            raised = jnp.where(seen, jnp.exp(scores[r : r + chunk]), 0.0)
            share = 1.0 / jnp.sum(raised, axis=-1, keepdims=True)
            probs[r : r + chunk] = (raised * share).astype(jnp.bfloat16)
        made = dot_nn(probs[...], kv[s, :, HEAD_DIM:])
        for h in range(HEADS):
            merged[rows, h * HEAD_DIM : (h + 1) * HEAD_DIM] = made[
                h * block : (h + 1) * block
            ].astype(jnp.bfloat16)
        return carry

    count = len(halos)
    for g in range(count + 2):
        tick()
        if g < count:
            halos[g].plane()
        if 1 <= g <= count:
            halos[g - 1].relay()
        tick()
        if g >= 2:
            halos[g - 2].end()
            lax.fori_loop((g - 2) * per_step, (g - 1) * per_step, attend, 0)
    locals_.copy(kv, out_kv)
    locals_.copy(merged, out_merged)
    gain_post = gains[3:4, :]
    for s in range(0, seqs, per_step):
        rows = slice(s * block, (s + per_step) * block)
        made = dot_nn(merged[rows], wo[...])
        projected[rows] = made
        hidden[rows] = tokens[rows].astype(jnp.float32) + made * root_inverse(made) * gain_post
        locals_.copy(projected.at[rows], out_projected.at[rows])
        locals_.copy(hidden.at[rows], out_hidden.at[rows])
    tick(len(pending))
    for part in gather_f:
        part.end()
    wires.drain()
    locals_.drain()


def vmem(shape, dtype):
    return pltpu.VMEM(shape, dtype)


def forward_pass(geo, tokens, positions, attention_block, feed_block):
    count, rows, seqs, block = geo.count, geo.rows, geo.seqs, geo.block
    bf, f4 = jnp.bfloat16, jnp.float32
    half = HEAD_DIM // 2
    frequency = (
        rope_base ** (-(np.arange(half, dtype=np.float32) * np.float32(2.0) / HEAD_DIM))
    ).astype(np.float32)[None]
    wires = len(geo.gather_bounds) * gather_wires(geo.outer) + geo.seqs // 2 * HALO_WIRES
    outs = [
        ((count, geo.feed.rows, LANES), bf),
        ((D, QUERY + 2 * HEAD_DIM), bf),
        ((QUERY, D), bf),
        ((8, D), f4),
        ((HEADS, rows, HEAD_DIM), bf),
        ((seqs, geo.reach, 2 * HEAD_DIM), bf),
        ((rows, QUERY), bf),
        ((rows, D), f4),
        ((rows, D), f4),
        ((rows, half), f4),
        ((rows, half), f4),
    ]
    flat_rows = geo.attention.count * geo.attention.stride + geo.attention.tail
    return pl.pallas_call(
        functools.partial(forward_kernel, geo),
        out_shape=[jax.ShapeDtypeStruct(*out) for out in outs],
        in_specs=[pl.BlockSpec(memory_space=pltpu.VMEM)] * 5,
        out_specs=[pl.BlockSpec(memory_space=pl.ANY)] * len(outs),
        scratch_shapes=[
            vmem((count, geo.attention.rows, LANES), bf),
            vmem((geo.feed.rows, LANES), bf),
            vmem((16 + geo.feed.rows, LANES), f4),
            vmem((flat_rows, LANES), f4),
            vmem((D, QUERY + 2 * HEAD_DIM), bf),
            vmem((QUERY, D), bf),
            vmem((8, D), f4),
            vmem((rows, half), f4),
            vmem((rows, half), f4),
            vmem((seqs, block, LANES), jnp.int32),
            vmem((rows, D), bf),
            vmem((HEADS, rows, HEAD_DIM), bf),
            vmem((seqs, geo.reach, 2 * HEAD_DIM), bf),
            vmem((HEADS * block, geo.reach), f4),
            vmem((HEADS * block, geo.reach), bf),
            vmem((rows, QUERY), bf),
            vmem((rows, D), f4),
            vmem((rows, D), f4),
            pltpu.SemaphoreType.DMA((wires,)),
            pltpu.SemaphoreType.DMA((wires,)),
            pltpu.SemaphoreType.DMA((32,)),
        ],
        compiler_params=pltpu.CompilerParams(
            collective_id=0, has_side_effects=True, vmem_limit_bytes=60 << 20
        ),
    )(tokens.reshape(rows, D), positions, jnp.asarray(frequency), attention_block, feed_block)


MATRIX = D * FF // LANES
BEND = 0.044715
SLOPE = math.sqrt(2.0 / math.pi)


def feed_pieces(blocks, which):
    base, stop = which * MATRIX, (which + 1) * MATRIX
    if which == 2:
        stop = blocks.count * blocks.stride + blocks.tail
    found = []
    for d in range(blocks.count):
        low = max(d * blocks.stride, base)
        high = min(d * blocks.stride + blocks.rows, stop)
        if low < high:
            found.append((d, low - base, high - base, base - d * blocks.stride))
    return found


def feed_phase(geo, locals_, held_in, cotangent_in, mixed_out, split, grad, begin, tick, *refs):
    (flat, twin, down, act, pair, feed_in, turned_in, grad_down) = refs
    mixed = cotangent = feed_in
    blocks = geo.feed
    ends = [-(-(-(-(m + 1) * MATRIX // blocks.stride)) // 4) for m in range(3)]
    starts = [0] + ends[:-1]
    loads = [
        locals_.copy(held_in.at[pl.ds(a, b - a)], split.at[pl.ds(a, b - a)])
        for a, b in zip(starts, ends)
    ]
    load_cotangent = locals_.copy(cotangent_in, grad_down)

    def index(d):
        return d // 4, d // 2 % 2, d % 2

    def unpack(which):
        for d, low, high, shift in feed_pieces(blocks, which):
            mid = min(high, max(low, d * blocks.stride - which * MATRIX + blocks.tail))
            if d and low < mid:
                flat[low:mid] += split[*index(d), low + shift : mid + shift].astype(jnp.float32)
            else:
                mid = low
            flat[mid:high] = split[*index(d), mid + shift : high + shift].astype(jnp.float32)

    def pack(which):
        for d, low, high, shift in feed_pieces(blocks, which):
            split[*index(d), low + shift : high + shift] = flat[low:high].astype(jnp.bfloat16)

    for which, (matrix, first, width) in enumerate(
        ((twin, 0, FF), (twin, FF, FF), (down, 0, D))
    ):
        locals_.finish(loads[which])
        unpack(which)
        unflatten(flat, 0, matrix, first, width)
    gain_feed = read_gain(flat, MATRIX, D)
    gain_out = read_gain(flat, MATRIX + D // LANES, D)

    total, step = geo.rows, WIDE
    spans = [slice(r, r + STEP) for r in range(0, total, STEP)]
    for rows in spans:
        h = grad[rows]
        feed_in[rows] = (h * root_inverse(h) * gain_feed).astype(jnp.bfloat16)

    def rise(i, carry):
        columns = pl.ds(pl.multiple_of(i * step, step), step)
        others = pl.ds(pl.multiple_of(FF + i * step, step), step)
        for rows in spans:
            g = dot_nn(feed_in[rows], twin[:, columns])
            u = dot_nn(feed_in[rows], twin[:, others])
            square = g * g
            t = jnp.tanh(g * (SLOPE + SLOPE * BEND * square))
            half = 0.5 + 0.5 * t
            soft = g * half
            act[rows, columns] = (soft * u).astype(jnp.bfloat16)
            pair[rows, others] = soft.astype(jnp.bfloat16)
            slope = half * (1.0 + g * (1.0 - t) * (SLOPE + 3.0 * SLOPE * BEND * square))
            pair[rows, columns] = (u * slope).astype(jnp.bfloat16)
        return carry

    lax.fori_loop(0, FF // step, rise, 0)
    turned_in[...] = feed_in[...].T

    def settle(i, sum_out):
        rows = pl.ds(pl.multiple_of(i * STEP, STEP), STEP)
        made = dot_nn(act[rows], down[...])
        r = root_inverse(made)
        mixed[rows] = (grad[rows] + made * r * gain_out).astype(jnp.bfloat16)
        e = grad_down[rows].astype(jnp.float32)
        unit = made * r
        sum_out = sum_out + jnp.sum(e * unit, axis=0, keepdims=True)
        c = e * gain_out
        grad_down[rows] = (
            r * (c - unit * jnp.mean(unit * c, axis=-1, keepdims=True))
        ).astype(jnp.bfloat16)
        return sum_out

    locals_.finish(load_cotangent)
    sum_out = lax.fori_loop(0, total // STEP, settle, jnp.zeros((1, D), jnp.float32))
    store_mixed = locals_.copy(mixed, mixed_out)

    def fall(i, carry):
        columns = pl.ds(pl.multiple_of(i * step, step), step)
        others = pl.ds(pl.multiple_of(FF + i * step, step), step)
        for rows in spans:
            made = dot_nt(grad_down[rows], down[columns, :])
            for at in (columns, others):
                pair[rows, at] = (made * pair[rows, at].astype(jnp.float32)).astype(jnp.bfloat16)
        return carry

    lax.fori_loop(0, FF // step, fall, 0)

    def back(i, sum_feed):
        rows = pl.ds(pl.multiple_of(i * STEP, STEP), STEP)
        made = dot_nt(pair[rows], twin[...])
        h = grad[rows]
        r = root_inverse(h)
        unit = h * r
        sum_feed = sum_feed + jnp.sum(made * unit, axis=0, keepdims=True)
        c = made * gain_feed
        grad[rows] = cotangent[rows].astype(jnp.float32) + r * (
            c - unit * jnp.mean(unit * c, axis=-1, keepdims=True)
        )
        return sum_feed

    def wide(i, carry, first):
        made = dot_nn(turned_in[...], pair[:, pl.ds(pl.multiple_of(first + i * step, step), step)])
        for k in range(step // LANES):
            flat[pl.ds(i * (step // LANES) + k, D, stride=FF // LANES), :] = made[
                :, k * LANES : (k + 1) * LANES
            ]
        return carry

    locals_.finish(store_mixed)
    load_cotangent = locals_.copy(cotangent_in, cotangent)
    lax.fori_loop(0, FF // step, functools.partial(wide, first=0), 0)
    pack(0)
    lax.fori_loop(0, FF // step, functools.partial(wide, first=FF), 0)
    pack(1)

    def tall(i, carry):
        columns = pl.ds(pl.multiple_of(i * step, step), step)
        made = dot_tn(act[:, columns], grad_down[...])
        for k in range(D // LANES):
            flat[pl.ds(i * (step * D // LANES) + k, step, stride=D // LANES), :] = made[
                :, k * LANES : (k + 1) * LANES
            ]
        return carry

    lax.fori_loop(0, FF // step, tall, 0)
    flat[MATRIX:] = jnp.zeros_like(flat[MATRIX:])
    pack(2)
    begin()
    locals_.finish(load_cotangent)
    sum_feed = jnp.zeros((1, D), jnp.float32)
    for i in range(0, total // STEP, 2):
        sum_feed = lax.fori_loop(i, i + 2, back, sum_feed)
        tick()
    write_gain(flat, MATRIX, sum_feed)
    write_gain(flat, MATRIX + D // LANES, sum_out)
    last = blocks.count - 1
    low = blocks.count * blocks.stride - 2 * MATRIX
    split[*index(last), blocks.stride :] = flat[low:].astype(jnp.bfloat16)


class Scatter:
    def __init__(self, place, wires, other, own, lands, result, piece):
        self.place, self.wires, self.other, self.own, self.result = place, wires, other, own, result
        self.by_core, self.first_x, self.first_y, self.second_x, self.second_y, self.by_outer = lands
        first, cut, last, at_x, at_y = piece
        self.split = cut < last
        self.all = pl.ds(first, last - first)
        self.rows_x, self.rows_y = pl.ds(first, cut - first), pl.ds(cut, last - cut)
        self.land_x, self.land_y = pl.ds(at_x, cut - first), pl.ds(at_y, last - cut)
        p, plan = place, wires.plan
        mine, theirs = self.column_of(p.b), self.column_of(1 - p.b)
        self.from_core = plan(
            other.at[:, :, 1 - p.c, self.all], self.by_core.at[:, :, self.all], p.sibling()
        )
        self.from_x = plan(
            own.at[theirs, :, self.rows_x], self.first_x.at[:, :, self.land_x], p.x_peer()
        )
        self.over_y = plan(
            own.at[mine, 1 - p.y, self.rows_x], self.second_y.at[:, self.land_x], p.y_peer()
        )
        if self.split:
            self.from_y = plan(
                own.at[:, 1 - p.y, self.rows_y], self.first_y.at[:, self.land_y], p.y_peer()
            )
            self.over_x = plan(
                own.at[theirs, p.y, self.rows_y], self.second_x.at[:, self.land_y], p.x_peer()
            )
        self.from_outer = [
            plan(
                own.at[p.b * p.outer + p.flip(k), p.y, self.all],
                self.by_outer.at[k - 1, self.all],
                p.flip_peer(k),
            )
            for k in range(1, p.outer)
        ]

    def add(self, i, y, rows, land):
        self.own[i, y, rows] = (
            self.own[i, y, rows].astype(jnp.float32) + land.astype(jnp.float32)
        ).astype(jnp.bfloat16)

    def column_of(self, b):
        return pl.ds(b * self.place.outer, self.place.outer)

    def core(self):
        self.from_core.start()

    def plane(self):
        p = self.place
        self.from_core.wait_recv()

        def body(i, carry):
            for y in range(2):
                self.add(i, y, self.all, self.by_core[i, y, self.all])
            return carry

        lax.fori_loop(0, 2 * p.outer, body, 0)
        self.from_x.start()
        if self.split:
            self.from_y.start()

    def cross(self):
        p = self.place
        self.from_x.wait_recv()

        def body(hi, carry):
            for y in range(2):
                self.add(p.b * p.outer + hi, y, self.rows_x, self.first_x[hi, y, self.land_x])
            return carry

        lax.fori_loop(0, p.outer, body, 0)
        self.over_y.start()
        if self.split:
            self.from_y.wait_recv()

            def body(i, carry):
                self.add(i, p.y, self.rows_y, self.first_y[i, self.land_y])
                return carry

            lax.fori_loop(0, 2 * p.outer, body, 0)
            self.over_x.start()

    def column(self):
        p = self.place
        self.over_y.wait_recv()
        if self.split:
            self.over_x.wait_recv()

        def body(hi, carry):
            i = p.b * p.outer + hi
            self.add(i, p.y, self.rows_x, self.second_y[hi, self.land_x])
            if self.split:
                self.add(i, p.y, self.rows_y, self.second_x[hi, self.land_y])
            return carry

        lax.fori_loop(0, p.outer, body, 0)
        for made in self.from_outer:
            made.start()

    def end(self):
        p = self.place
        total = self.own[p.b * p.outer + p.hi, p.y, self.all].astype(jnp.float32)
        for k, made in enumerate(self.from_outer):
            made.wait_recv()
            total = total + self.by_outer[k, self.all].astype(jnp.float32)
        self.result[self.all] = total


def scatter_wires(outer):
    return 5 + outer - 1


def cut_pieces(bounds, shares):
    pieces, at_x, at_y = [], 0, 0
    for first, last, share in zip(bounds, bounds[1:], shares):
        cut = first + max(16, int((last - first) * share) // 16 * 16)
        pieces.append((first, cut, last, at_x, at_y))
        at_x, at_y = at_x + cut - first, at_y + last - cut
    return pieces, at_x, at_y


def land_shapes(rows, bounds, shares, outer):
    rows_x, rows_y = cut_pieces(bounds, shares)[1:]
    return [
        pltpu.VMEM(shape + (LANES,), jnp.bfloat16)
        for shape in (
            (2 * outer, 2, rows),
            (outer, 2, rows_x),
            (2 * outer, rows_y),
            (outer, rows_y),
            (outer, rows_x),
            (outer - 1, rows),
        )
    ]


class Return:
    def __init__(self, place, wires, kv, own, by_core, by_y, by_outer, block, first, size):
        self.place, self.wires, self.kv, self.own, self.block = place, wires, kv, own, block
        self.by_core, self.by_y, self.by_outer = by_core, by_y, by_outer
        self.group = pl.ds(first, size)
        self.each = range(first, first + size)

    def rows(self, at):
        return slice(at * self.block, (at + 1) * self.block)

    def slot(self, at):
        return self.kv.at[self.group, pl.ds(at * self.block, self.block)]

    def core(self):
        p = self.place
        self.from_core = [
            self.wires.copy(
                self.slot(at), self.by_core.at[self.group, pl.ds(i * self.block, self.block)], p.sibling()
            )
            for i, at in enumerate((1, 3))
        ]

    def grow(self, s, at, extra):
        rows = self.rows(at)
        self.kv[s, rows] = (self.kv[s, rows].astype(jnp.float32) + extra).astype(jnp.bfloat16)

    def plane(self):
        p = self.place
        for made in self.from_core:
            made.wait_recv()
        for s in self.each:

            @pl.when(p.c == 0)
            def _():
                self.grow(s, 2, self.by_core[s, self.rows(0)].astype(jnp.float32))
                self.own[s] += self.by_core[s, self.rows(1)].astype(jnp.float32)

            @pl.when(p.c == 1)
            def _():
                self.grow(s, 0, self.by_core[s, self.rows(0)].astype(jnp.float32))
                self.grow(s, 2, self.by_core[s, self.rows(1)].astype(jnp.float32))

        self.from_y = self.wires.copy(self.slot(2), self.by_y.at[self.group], p.y_peer())

    def outward(self):
        p = self.place
        self.from_y.wait_recv()
        for s in self.each:

            @pl.when(p.y == 0)
            def _():
                self.own[s] += self.by_y[s].astype(jnp.float32)

            @pl.when(p.y == 1)
            def _():
                self.grow(s, 0, self.by_y[s].astype(jnp.float32))

        self.from_outer = self.wires.copy(
            self.slot(0), self.by_outer.at[self.group], p.outer_peer(p.outer - 1)
        )

    def end(self):
        self.from_outer.wait_recv()
        for s in self.each:
            self.own[s] += self.by_outer[s].astype(jnp.float32)


RETURN_WIRES = 4
FEED_SHARES = (0.5, 1.0, 1.0, 1.0)
ATTENTION_SHARES = (0.5, 0.5, 1.0)


def fill_blocks(blocks, split, flat, margin, base, stop):
    even = blocks.stride % 16 == 0
    for d in range(blocks.count):
        low, high = max(d * blocks.stride, base), min(d * blocks.stride + blocks.rows, stop)
        if low >= high:
            continue
        i, y, c = d // 4, d // 2 % 2, d % 2
        first, last = low - d * blocks.stride, high - d * blocks.stride
        if even:
            split[i, y, c, first:last] = flat[low - base + margin : high - base + margin].astype(
                jnp.bfloat16
            )
        else:
            start, end = first // 16 * 16, -(-last // 16) * 16
            source = low - base + margin - (first - start)
            split[i, y, c, start:end] = (
                split[i, y, c, start:end].astype(jnp.float32)
                + flat[source : source + end - start]
            ).astype(jnp.bfloat16)


MARGIN = 16


def backward_kernel(
    geo, positions, gains, tokens_in, wqkv_in, wo_in, q_in, kv_in, merged_in, projected_in,
    hidden_in, cosine_in, sine_in, held_in, cotangent_in, *refs
):
    grad_tokens, mixed_out, attention_sum, feed_sum = refs[:4]
    grad, split_f, split_a, by_core_kv, by_y_kv, by_outer_kv = refs[4:10]
    lands_a, lands_f = refs[10:16], refs[16:22]
    send, recv, local = refs[22:]
    place = Place()
    wires, locals_ = Wires(send, recv), Locals(local)
    bf, f4, rows, half = jnp.bfloat16, jnp.float32, geo.rows, HEAD_DIM // 2
    load_hidden = locals_.copy(hidden_in, grad)
    greet(place)
    pieces = cut_pieces(geo.feed_bounds, FEED_SHARES)[0]
    own_f = split_f.at[:, :, place.c]
    one, two, three, four = [
        Scatter(place, wires, split_f, own_f, lands_f, feed_sum, piece) for piece in pieces
    ]

    def begin():
        for part in (one, two, three):
            part.core()

    pending = [
        [one.plane], [two.plane],
        [],
        [one.cross], [three.plane], [], [one.column],
        [two.cross],
        [four.plane],
        [two.column, three.cross, one.end],
        [four.cross, three.column],
        [two.end, four.column, three.end, four.end],
    ]

    def tick():
        for action in pending.pop(0):
            action()

    locals_.finish(load_hidden)
    pl.run_scoped(
        functools.partial(
            feed_phase, geo, locals_, held_in, cotangent_in, mixed_out, split_f, grad, begin, tick
        ),
        vmem((MATRIX + geo.feed.tail, LANES), f4),
        vmem((D, 2 * FF), bf),
        vmem((FF, D), bf),
        vmem((rows, FF), bf),
        vmem((rows, 2 * FF), bf),
        vmem((rows, D), bf),
        vmem((D, rows), bf),
        vmem((rows, D), bf),
    )
    four.core()
    pl.run_scoped(
        functools.partial(
            attention_phase, geo, place, wires, locals_, positions, gains,
            (tokens_in, wqkv_in, wo_in, q_in, kv_in, merged_in, projected_in, cosine_in, sine_in),
            grad_tokens, attention_sum, grad, split_a, by_core_kv, by_y_kv, by_outer_kv, lands_a,
            pending, tick,
        ),
        vmem((rows, D), bf),
        vmem(wqkv_in.shape, bf),
        vmem(wo_in.shape, bf),
        vmem(q_in.shape, bf),
        vmem(kv_in.shape, bf),
        vmem((rows, QUERY + 2 * HEAD_DIM), bf),
        vmem((rows, half), f4),
        vmem((rows, half), f4),
        vmem((2 * geo.reach, D), f4),
        vmem((rows, D), bf),
        vmem((max(D, geo.reach), max(rows, 2 * HEADS * geo.block)), bf),
        vmem((HEADS, rows, HEAD_DIM), bf),
        vmem((rows, D), bf),
        vmem((geo.seqs, geo.block, 2 * HEAD_DIM), f4),
        vmem((2 * MARGIN + QUERY * D // LANES, LANES), f4),
    )


def attention_phase(
    geo, place, wires, locals_, positions, gains, saved, grad_tokens, attention_sum, grad,
    split, by_core_kv, by_y_kv, by_outer_kv, lands_a, pending, tick, *refs
):
    tokens_in, wqkv_in, wo_in, q_in, kv_in, merged_in, projected_in, cosine_in, sine_in = saved
    (
        tokens, wqkv, wo, q, kv, pair, cosine, sine, work, normed, shared, grad_out, out_rows,
        own_kv, flat,
    ) = refs
    seqs, block, reach, total, step = geo.seqs, geo.block, geo.reach, geo.rows, STEP
    turned = shared.at[pl.ds(0, D), pl.ds(0, total)]
    probs = shared.at[pl.ds(0, reach), pl.ds(0, HEADS * block)]
    logits = shared.at[pl.ds(0, reach), pl.ds(HEADS * block, HEADS * block)]
    projected = work.at[pl.ds(0, total)]
    scores = work.at[pl.ds(0, reach), pl.ds(0, HEADS * block)]
    slopes = work.at[pl.ds(reach, reach), pl.ds(0, HEADS * block)]
    load_projected = locals_.copy(projected_in, projected)
    load_wo = locals_.copy(wo_in, wo)
    load_tokens = locals_.copy(tokens_in, tokens)
    load_merged = locals_.copy(merged_in, pair.at[:, pl.ds(0, QUERY)])
    load_q, load_kv = locals_.copy(q_in, q), locals_.copy(kv_in, kv)
    load_rest = [
        locals_.copy(wqkv_in, wqkv), locals_.copy(cosine_in, cosine), locals_.copy(sine_in, sine)
    ]
    gain_attention, gain_query = gains[0:1, :], gains[1:2, :HEAD_DIM]
    gain_key, gain_post = gains[2:3, :HEAD_DIM], gains[3:4, :]
    for made in (load_projected, load_wo, load_tokens):
        locals_.finish(made)

    def start_rows(i, summed):
        rows = pl.ds(pl.multiple_of(i * step, step), step)
        made, e = projected[rows], grad[rows]
        r = root_inverse(made)
        unit = made * r
        c = e * gain_post
        out_rows[rows] = (r * (c - unit * jnp.mean(unit * c, axis=-1, keepdims=True))).astype(
            jnp.bfloat16
        )
        x = tokens[rows].astype(jnp.float32)
        normed[rows] = (x * root_inverse(x) * gain_attention).astype(jnp.bfloat16)
        for h in range(HEADS):
            grad_out[h, rows] = dot_nt(
                out_rows[rows], wo[h * HEAD_DIM : (h + 1) * HEAD_DIM, :]
            ).astype(jnp.bfloat16)
        return summed + jnp.sum(e * unit, axis=0, keepdims=True)

    sum_post = lax.fori_loop(0, total // step, start_rows, jnp.zeros((1, D), jnp.float32))
    tick()
    blocks = geo.attention
    flat[0:MARGIN] = jnp.zeros((MARGIN, LANES), jnp.float32)
    flat[MARGIN + QUERY * D // LANES :] = jnp.zeros((MARGIN, LANES), jnp.float32)
    if blocks.stride % 16:
        split[...] = jnp.zeros_like(split)
    locals_.finish(load_merged)

    for made in [load_q, load_kv] + load_rest:
        locals_.finish(made)

    wide = HEADS * block
    chunk = 32
    lane = lax.rem(lax.broadcasted_iota(jnp.int32, (chunk, wide), 1), block)
    line = lax.broadcasted_iota(jnp.int32, (chunk, wide), 0)

    def attend(s, carry):
        rows = pl.ds(pl.multiple_of(s * block, block), block)
        queries = q[:, rows, :].reshape(wide, HEAD_DIM)
        given = grad_out[:, rows, :].reshape(wide, HEAD_DIM)
        scores[...] = dot_nt(kv[s, :, :HEAD_DIM], queries)
        slopes[...] = dot_nt(kv[s, :, HEAD_DIM:], given)
        spot = jnp.concatenate([positions[pl.ds(s, 1), :]] * HEADS, axis=-1)
        low = jnp.maximum(lane[0:1] + 1, lane[0:1] + WINDOW - spot)
        total_e = jnp.zeros((8, wide), jnp.float32)
        total_d = jnp.zeros((8, wide), jnp.float32)
        for r in range(0, reach, chunk):
            seen = (line + r >= low) & (line + (r - WINDOW) <= lane)
            raised = jnp.where(seen, jnp.exp(scores[r : r + chunk]), 0.0)
            scores[r : r + chunk] = raised
            moved = raised * slopes[r : r + chunk]
            for k in range(0, chunk, 8):
                total_e = total_e + raised[k : k + 8]
                total_d = total_d + moved[k : k + 8]
        share = 1.0 / jnp.sum(total_e, axis=0, keepdims=True)
        inner = jnp.sum(total_d, axis=0, keepdims=True) * share
        for r in range(0, reach, chunk):
            p = scores[r : r + chunk] * share
            probs[r : r + chunk] = p.astype(jnp.bfloat16)
            logits[r : r + chunk] = (p * (slopes[r : r + chunk] - inner)).astype(jnp.bfloat16)
        grad_q = dot_tn(logits[...], kv[s, :, :HEAD_DIM]) * HEAD_DIM**-0.5
        grad_k = dot_nn(logits[...], queries)
        grad_v = dot_nn(probs[...], given)
        early = reach - block
        kv[s, :early, :HEAD_DIM] = grad_k[:early].astype(jnp.bfloat16)
        kv[s, :early, HEAD_DIM:] = grad_v[:early].astype(jnp.bfloat16)
        own_kv[s, :, :HEAD_DIM] = grad_k[early:]
        own_kv[s, :, HEAD_DIM:] = grad_v[early:]
        for h in range(HEADS):
            q[h, rows] = grad_q[h * block : (h + 1) * block].astype(jnp.bfloat16)
        return carry

    size = 2
    returns = [
        Return(place, wires, kv, own_kv, by_core_kv, by_y_kv, by_outer_kv, block, s, size)
        for s in range(0, seqs, size)
    ]
    for g, group in enumerate(returns):
        lax.fori_loop(g * size, (g + 1) * size, attend, 0)
        group.core()
        if g >= 1:
            returns[g - 1].plane()
        if g >= 2:
            returns[g - 2].outward()
        tick()
    last = len(returns) - 1
    turned[...] = normed[...].T

    def tall(i, carry):
        columns = pl.ds(pl.multiple_of(i * step, step), step)
        made = dot_tn(pair[:, columns], out_rows[...])
        for k in range(D // LANES):
            flat[pl.ds(MARGIN + i * (step * D // LANES) + k, step, stride=D // LANES), :] = made[
                :, k * LANES : (k + 1) * LANES
            ]
        return carry

    lax.fori_loop(0, QUERY // step, tall, 0)
    fill_blocks(blocks, split, flat, MARGIN, BASE_OUT, BASE_GAINS)
    def query_rows(i, summed):
        rows = pl.ds(pl.multiple_of(i * step, step), step)
        made = dot_nn(normed[rows], wqkv[:, :QUERY])
        for h in range(HEADS):
            raw = made[:, h * HEAD_DIM : (h + 1) * HEAD_DIM]
            e = turn_back(q[h, rows].astype(jnp.float32), cosine[rows], sine[rows])
            r = root_inverse(raw)
            unit = raw * r
            summed = summed + jnp.sum(e * unit, axis=0, keepdims=True)
            c = e * gain_query
            pair[rows, h * HEAD_DIM : (h + 1) * HEAD_DIM] = (
                r * (c - unit * jnp.mean(unit * c, axis=-1, keepdims=True))
            ).astype(jnp.bfloat16)
        return summed

    returns[last].plane()
    returns[last - 1].outward()
    tick()
    sum_query = lax.fori_loop(0, total // step, query_rows, jnp.zeros((1, HEAD_DIM), jnp.float32))
    returns[last].outward()
    tick()

    def broad(i, carry, first, width):
        columns = pl.ds(pl.multiple_of(first + i * step, step), step)
        made = dot_nn(turned[...], pair[:, columns])
        for k in range(step // LANES):
            start = MARGIN + i * (step // LANES) + k
            flat[pl.ds(start, D, stride=width // LANES), :] = made[:, k * LANES : (k + 1) * LANES]
        return carry

    lax.fori_loop(0, QUERY // step, functools.partial(broad, first=0, width=QUERY), 0)
    fill_blocks(blocks, split, flat, MARGIN, 0, BASE_KEY)
    tick()
    for group in returns:
        group.end()

    def key_rows(i, summed):
        rows = pl.ds(pl.multiple_of(i * step, step), step)
        per = step // block
        raw = dot_nn(normed[rows], wqkv[:, QUERY : QUERY + HEAD_DIM])
        both = own_kv[pl.ds(i * per, per)].reshape(step, 2 * HEAD_DIM)
        e = turn_back(both[:, :HEAD_DIM], cosine[rows], sine[rows])
        r = root_inverse(raw)
        unit = raw * r
        c = e * gain_key
        pair[rows, QUERY : QUERY + HEAD_DIM] = (
            r * (c - unit * jnp.mean(unit * c, axis=-1, keepdims=True))
        ).astype(jnp.bfloat16)
        pair[rows, QUERY + HEAD_DIM :] = both[:, HEAD_DIM:].astype(jnp.bfloat16)
        return summed + jnp.sum(e * unit, axis=0, keepdims=True)

    sum_key = lax.fori_loop(0, total // step, key_rows, jnp.zeros((1, HEAD_DIM), jnp.float32))
    for first, base in ((QUERY, BASE_KEY), (QUERY + HEAD_DIM, BASE_VALUE)):
        broad(0, 0, first, HEAD_DIM)
        size_rows = D * HEAD_DIM // LANES
        flat[MARGIN + size_rows : 2 * MARGIN + size_rows] = jnp.zeros((MARGIN, LANES), jnp.float32)
        fill_blocks(blocks, split, flat, MARGIN, base, base + size_rows)

    def end_rows(i, summed):
        rows = pl.ds(pl.multiple_of(i * step, step), step)
        made = dot_nt(pair[rows], wqkv[...])
        x = tokens[rows].astype(jnp.float32)
        r = root_inverse(x)
        unit = x * r
        c = made * gain_attention
        grad[rows] = grad[rows] + r * (c - unit * jnp.mean(unit * c, axis=-1, keepdims=True))
        return summed + jnp.sum(made * unit, axis=0, keepdims=True)

    tail = geo.attention.tail
    own = split.at[:, :, place.c]
    one, two, three = [
        Scatter(place, wires, split, own, lands_a, attention_sum, piece)
        for piece in cut_pieces(geo.attention_bounds, ATTENTION_SHARES)[0]
    ]
    one.core()
    two.core()
    tick()
    sum_attention = jnp.zeros((1, D), jnp.float32)
    half = total // step // 2
    one.plane()
    sum_attention = lax.fori_loop(0, half, end_rows, sum_attention)
    two.plane()
    sum_attention = lax.fori_loop(half, 2 * half, end_rows, sum_attention)
    locals_.copy(grad, grad_tokens)
    tick()
    flat[MARGIN : 2 * MARGIN + tail] = jnp.zeros((MARGIN + tail, LANES), jnp.float32)
    at = MARGIN
    for made in (sum_attention, sum_query, sum_key, sum_post):
        write_gain(flat, at, made)
        at += made.shape[1] // LANES
    fill_blocks(blocks, split, flat, MARGIN, BASE_GAINS, blocks.count * blocks.stride + tail)
    three.core()
    for action in (
        one.cross, three.plane, two.cross, one.column, three.cross, two.column, three.column,
        one.end, two.end, three.end,
    ):
        action()
    wires.drain()
    locals_.drain()


def backward_pass(geo, tokens, positions, saved, hidden, feed_held, cotangent):
    bf, f4, rows, seqs, block = jnp.bfloat16, jnp.float32, geo.rows, geo.seqs, geo.block
    wqkv, wo, gains, q, kv, merged, projected, cosine, sine = saved
    rows_a, rows_f, outer = geo.attention.rows, geo.feed.rows, geo.outer
    outs = [((rows, D), f4), ((rows, D), bf), ((rows_a, LANES), f4), ((rows_f, LANES), f4)]
    full, hbm = pl.BlockSpec(memory_space=pltpu.VMEM), pl.BlockSpec(memory_space=pl.ANY)
    wires = (len(geo.feed_bounds) + len(geo.attention_bounds) - 2) * scatter_wires(
        outer
    ) + seqs // 2 * RETURN_WIRES
    return pl.pallas_call(
        functools.partial(backward_kernel, geo),
        out_shape=[jax.ShapeDtypeStruct(*out) for out in outs],
        in_specs=[full] * 2 + [hbm] * 12,
        out_specs=[hbm, hbm, full, full],
        scratch_shapes=[
            vmem((rows, D), f4),
            vmem((2 * outer, 2, 2, rows_f, LANES), bf),
            vmem((2 * outer, 2, 2, rows_a, LANES), bf),
            vmem((seqs, 2 * block, 2 * HEAD_DIM), bf),
            vmem((seqs, block, 2 * HEAD_DIM), bf),
            vmem((seqs, block, 2 * HEAD_DIM), bf),
        ]
        + land_shapes(rows_a, geo.attention_bounds, ATTENTION_SHARES, outer)
        + land_shapes(rows_f, geo.feed_bounds, FEED_SHARES, outer)
        + [
            pltpu.SemaphoreType.DMA((wires,)),
            pltpu.SemaphoreType.DMA((wires,)),
            pltpu.SemaphoreType.DMA((32,)),
        ],
        compiler_params=pltpu.CompilerParams(
            collective_id=1, has_side_effects=True, vmem_limit_bytes=63 << 20
        ),
    )(
        positions, gains, tokens.reshape(rows, D), wqkv, wo, q, kv, merged, projected, hidden,
        cosine, sine, feed_held.reshape(2 * outer, 2, 2, rows_f, LANES), cotangent.reshape(rows, D),
    )


def on_device(tokens, attention_params, feed_params, positions, cotangent):
    geo = Geo(tokens, attention_params, feed_params)
    device = lax.axis_index("batch") * lax.axis_size("seq") + lax.axis_index("seq")
    (
        feed_held, wqkv, weight_out, gains, q, kv, merged, projected, hidden, cosine, sine,
    ) = forward_pass(
        geo, tokens, positions, geo.attention.pad(attention_params), geo.feed.pad(feed_params)
    )
    grad_tokens, mixed, attention_sum, feed_sum = backward_pass(
        geo,
        tokens,
        positions,
        (wqkv, weight_out, gains, q, kv, merged, projected, cosine, sine),
        hidden,
        feed_held,
        cotangent,
    )
    return (
        mixed.reshape(tokens.shape),
        grad_tokens.reshape(tokens.shape),
        geo.attention.take(attention_sum, device),
        geo.feed.take(feed_sum, device),
    )


def solution(mesh):
    return jax.shard_map(
        on_device,
        mesh=mesh,
        in_specs=(
            P("batch", "seq", None),
            P(("batch", "seq")),
            P(("batch", "seq")),
            P("batch", "seq"),
            P("batch", "seq", None),
        ),
        out_specs=(
            P("batch", "seq", None),
            P("batch", "seq", None),
            P(("batch", "seq")),
            P(("batch", "seq")),
        ),
        check_vma=False,
    )
```

```python
import functools
import math

import jax
import jax.numpy as jnp
import numpy as np
from jax import lax
from jax.experimental import pallas as pl
from jax.experimental.pallas import tpu as pltpu
from jax.sharding import PartitionSpec as P

MESH = pl.DeviceIdType.MESH
LANES = 128

D = 640
HEADS = 4
HEAD_DIM = 256
FF = 2048
WINDOW = 512


rope_base = 10000.0


class Place:
    def __init__(self):
        self.devices_seq = lax.axis_size("seq")
        self.outer = self.devices_seq // 4
        self.count = 2 * self.devices_seq
        self.b = lax.axis_index("batch")
        s = lax.axis_index("seq")
        self.hi = lax.div(s, 4)
        self.y = lax.rem(lax.div(s, 2), 2)
        self.c = lax.rem(s, 2)

    def block(self, b, hi, y, c):
        return b * self.devices_seq + hi * 4 + y * 2 + c

    def seq_id(self, hi, y, c):
        return (self.b, hi * 4 + y * 2 + c)

    def mine(self):
        return self.block(self.b, self.hi, self.y, self.c)

    def x_peer(self):
        return (1 - self.b, self.hi * 4 + self.y * 2 + self.c)

    def y_peer(self):
        return self.seq_id(self.hi, 1 - self.y, self.c)

    def sibling(self):
        return self.seq_id(self.hi, self.y, 1 - self.c)

    def outer_at(self, k):
        return lax.rem(self.hi + k, self.outer)

    def flip(self, k):
        found, bit = 0, 1
        while bit < self.outer:
            own = lax.rem(lax.div(self.hi, bit), 2)
            found = found + bit * ((1 - own) if k & bit else own)
            bit *= 2
        return found

    def flip_peer(self, k):
        return self.seq_id(self.flip(k), self.y, self.c)

    def outer_peer(self, k):
        return self.seq_id(self.outer_at(k), self.y, self.c)

    def peers(self):
        return [self.x_peer(), self.y_peer(), self.sibling()] + [
            self.outer_peer(k) for k in range(1, self.outer)
        ]


def announce(place):
    barrier = pltpu.get_barrier_semaphore()
    for peer in place.peers():
        pl.semaphore_signal(barrier, inc=1, device_id=peer, device_id_type=MESH)


def meet(place):
    pl.semaphore_wait(pltpu.get_barrier_semaphore(), len(place.peers()))


def guarded(when, action):
    if when is None:
        action()
    else:
        pl.when(when)(action)


class Wires:
    def __init__(self, send_sems, recv_sems):
        self.send_sems, self.recv_sems = send_sems, recv_sems
        self.used = 0
        self.sent = []

    def plan(self, src, dst, peer, when=None):
        made = pltpu.make_async_remote_copy(
            src_ref=src,
            dst_ref=dst,
            send_sem=self.send_sems.at[self.used],
            recv_sem=self.recv_sems.at[self.used],
            device_id=peer,
            device_id_type=MESH,
        )
        self.used += 1
        self.sent.append((made, when))
        return made

    def copy(self, src, dst, peer, when=None):
        made = self.plan(src, dst, peer, when)
        guarded(when, made.start)
        return made

    def drain(self):
        for made, when in self.sent:
            guarded(when, made.wait_send)
        self.sent = []


def gather_wires(outer):
    return outer - 1 + 4 * outer + 4 * outer


class Gather:
    def __init__(self, place, wires, held, first, last, share):
        self.place, self.wires, self.held = place, wires, held
        self.first, self.last = first, last
        self.cut = first + int((last - first) * share) // 16 * 16
        self.from_outer = {}
        self.from_x, self.from_y, self.diag, self.twin = {}, {}, {}, []

    def send(self, index, peer, first=None, last=None):
        first = self.first if first is None else first
        last = self.last if last is None else last
        ref = self.held.at[index, pl.ds(first, last - first)]
        return self.wires.copy(ref, ref, peer)

    def begin(self):
        p = self.place
        for k in range(1, p.outer):
            self.from_outer[k] = self.send(p.mine(), p.flip_peer(k))

    def spread(self, j):
        p = self.place
        if j:
            self.from_outer[j].wait_recv()
        index = p.block(p.b, p.flip(j), p.y, p.c)
        self.from_y[j] = self.send(index, p.y_peer())
        self.from_x[j] = self.send(index, p.x_peer())
        self.twin.append(self.send(index, p.sibling()))

    def corner(self, j):
        p = self.place
        at = p.flip(j)
        self.from_y[j].wait_recv()
        got = p.block(p.b, at, 1 - p.y, p.c)
        down = self.send(got, p.x_peer(), self.first, self.cut)
        self.diag[j] = [down]
        self.twin.append(self.send(got, p.sibling()))
        self.from_x[j].wait_recv()
        got = p.block(1 - p.b, at, p.y, p.c)
        if self.cut < self.last:
            self.diag[j].append(self.send(got, p.y_peer(), self.cut, self.last))
        self.twin.append(self.send(got, p.sibling()))

    def finish(self, j):
        p = self.place
        for made in self.diag[j]:
            made.wait_recv()
        self.twin.append(self.send(p.block(1 - p.b, p.flip(j), 1 - p.y, p.c), p.sibling()))

    def end(self):
        for made in self.twin:
            made.wait_recv()


class Blocks:
    def __init__(self, length, count):
        self.length, self.count = length, count
        self.stride, self.rest = divmod(length, LANES)
        needed = -(-(length + self.rest * (count - 1)) // LANES)
        self.rows = -(-needed // 16) * 16
        self.tail = self.rows - self.stride
        self.total = length * count

    def pad(self, shard):
        return jnp.pad(shard, (0, self.rows * LANES - self.length)).reshape(self.rows, LANES)

    def take(self, block, index):
        return lax.dynamic_slice(block.reshape(-1), (self.rest * index,), (self.length,))


EPS = 1e-06


def root_inverse(rows):
    return lax.rsqrt(jnp.mean(rows * rows, axis=-1, keepdims=True) + EPS)


def turn(rows, cosine, sine):
    half = rows.shape[-1] // 2
    first, second = rows[:, :half], rows[:, half:]
    return jnp.concatenate([first * cosine - second * sine, second * cosine + first * sine], axis=-1)


def turn_back(rows, cosine, sine):
    half = rows.shape[-1] // 2
    first, second = rows[:, :half], rows[:, half:]
    return jnp.concatenate([first * cosine + second * sine, second * cosine - first * sine], axis=-1)


def dot_nn(left, right):
    return jnp.dot(left, right, preferred_element_type=jnp.float32)


def dot_nt(left, right):
    return lax.dot_general(left, right, (((1,), (1,)), ((), ())), preferred_element_type=jnp.float32)


def dot_tn(left, right):
    return lax.dot_general(left, right, (((0,), (0,)), ((), ())), preferred_element_type=jnp.float32)


def align_shard(blocks, place, padded_ref, shifted, aligned):
    offset = blocks.rest * place.mine()
    down, right = lax.div(offset, LANES), lax.rem(offset, LANES)
    rows = blocks.rows
    shifted[0:16] = jnp.zeros((16, LANES), jnp.float32)
    shifted[16 : 16 + rows] = pltpu.roll(padded_ref[...].astype(jnp.float32), right, 1)
    lane = lax.broadcasted_iota(jnp.int32, (rows, LANES), 1)
    aligned[...] = jnp.where(
        lane >= right, shifted[pl.ds(16 - down, rows)], shifted[pl.ds(15 - down, rows)]
    ).astype(aligned.dtype)


def flatten_held(blocks, held, flat):
    stride, tail, rows = blocks.stride, blocks.tail, blocks.rows
    if stride % 16 == 0 and tail == 16:
        flat[0:tail] = held[0, 0:tail].astype(jnp.float32)
        flat[tail:rows] = held[0, tail:rows].astype(jnp.float32)

        def body(d, carry):
            start = pl.multiple_of(d * stride, 16)
            flat[pl.ds(start, tail)] += held[d, 0:tail].astype(jnp.float32)
            start = pl.multiple_of(d * stride + tail, 16)
            flat[pl.ds(start, stride)] = held[d, tail:rows].astype(jnp.float32)
            return carry

        lax.fori_loop(1, blocks.count, body, 0)
    else:
        flat[...] = jnp.zeros_like(flat)

        def body(d, carry):
            flat[pl.ds(d * stride, rows)] += held[d].astype(jnp.float32)
            return carry

        lax.fori_loop(0, blocks.count, body, 0)


def unflatten(flat, base, matrix, first, width):
    height, steps = matrix.shape[0], width // LANES
    for i in range(steps):
        matrix[:, first + i * LANES : first + (i + 1) * LANES] = flat[
            pl.ds(base + i, height, stride=steps), :
        ].astype(matrix.dtype)


def write_gain(flat, base, gain):
    for i in range(gain.shape[1] // LANES):
        flat[base + i : base + i + 1, :] = gain[:, i * LANES : (i + 1) * LANES]


def read_gain(flat, base, width):
    return jnp.concatenate([flat[base + i : base + i + 1, :] for i in range(width // LANES)], axis=-1)


class Halo:
    def __init__(self, place, wires, kv, block, first, size):
        self.place, self.wires, self.kv, self.block = place, wires, kv, block
        self.first, self.size = first, size

    def slot(self, at):
        return self.kv.at[pl.ds(self.first, self.size), pl.ds(pl.multiple_of(at * self.block, 128), self.block)]

    def outward(self):
        p = self.place
        self.outer = self.wires.copy(
            self.slot(4), self.slot(0), p.outer_peer(1), p.hi + 1 < p.outer
        )

    def plane(self):
        p = self.place
        guarded(p.hi > 0, self.outer.wait_recv)
        self.across = self.wires.copy(self.slot(4 * (1 - p.y)), self.slot(2), p.y_peer())
        self.near = self.wires.copy(self.slot(4 * (1 - p.c)), self.slot(3 - 2 * p.c), p.sibling())

    def relay(self):
        p = self.place
        self.across.wait_recv()
        self.far = self.wires.copy(self.slot(2), self.slot(1 + 2 * p.c), p.sibling())

    def end(self):
        self.near.wait_recv()
        self.far.wait_recv()


HALO_WIRES = 4


class Locals:
    def __init__(self, sems):
        self.sems, self.used, self.open = sems, 0, []

    def copy(self, src, dst):
        made = pltpu.make_async_copy(src, dst, self.sems.at[self.used])
        self.used += 1
        self.open.append(made)
        made.start()
        return made

    def finish(self, made):
        made.wait()
        self.open = [other for other in self.open if other is not made]

    def drain(self):
        for made in self.open:
            made.wait()
        self.open = []


class Geo:
    def __init__(self, tokens, attention_params, feed_params):
        self.seqs, self.block = tokens.shape[:2]
        self.rows = self.seqs * self.block
        self.count = lax.axis_size("batch") * lax.axis_size("seq")
        self.outer = lax.axis_size("seq") // 4
        self.attention = Blocks(attention_params.shape[0], self.count)
        self.feed = Blocks(feed_params.shape[0], self.count)
        self.reach = 5 * self.block
        rows = self.attention.rows
        early = (rows - 16) // 32 * 16
        self.attention_bounds = [0, early, rows - 16, rows]
        rows = self.feed.rows
        early = rows - 16
        self.feed_bounds = [0, early // 48 * 16, early // 48 * 32, early, rows]


QUERY = HEADS * HEAD_DIM
BASE_KEY = D * QUERY // LANES
BASE_VALUE = BASE_KEY + D * HEAD_DIM // LANES
BASE_OUT = BASE_VALUE + D * HEAD_DIM // LANES
BASE_GAINS = BASE_OUT + QUERY * D // LANES
STEP = 256
WIDE = 512


def forward_kernel(geo, tokens, positions, frequency, attention_in, feed_in, *refs):
    (
        feed_held,
        out_wqkv,
        out_wo,
        out_gains,
        out_q,
        out_kv,
        out_merged,
        out_projected,
        out_hidden,
        out_cosine,
        out_sine,
    ) = refs[:11]
    (
        held,
        own_feed,
        shifted,
        flat,
        wqkv,
        wo,
        gains,
        cosine,
        sine,
        lows,
        normed,
        q,
        kv,
        scores,
        probs,
        merged,
        projected,
        hidden,
        send,
        recv,
        local,
    ) = refs[11:]
    place = Place()
    wires, locals_ = Wires(send, recv), Locals(local)
    seqs, block, reach = geo.seqs, geo.block, geo.reach
    announce(place)
    align_shard(geo.attention, place, attention_in, shifted, held.at[place.mine()])
    meet(place)
    gather_a = Gather(place, wires, held, 0, geo.attention.rows, 0.5)
    gather_a.begin()
    gather_a.spread(0)
    align_shard(geo.feed, place, feed_in, shifted, own_feed)
    lead = locals_.copy(own_feed, feed_held.at[place.mine()])
    gather_f = Gather(place, wires, feed_held, 0, geo.feed.rows, 1.0)

    @pl.when(place.hi == 0)
    def _():
        kv[:, :block] = jnp.zeros((seqs, block, 2 * HEAD_DIM), jnp.bfloat16)

    columns = positions[...].astype(jnp.float32).T
    row = lax.broadcasted_iota(jnp.int32, (block, LANES), 0)
    for s in range(seqs):
        spot = columns[:, s : s + 1]
        angle = spot * frequency[...]
        rows = slice(s * block, (s + 1) * block)
        cosine[rows] = jnp.cos(angle)
        sine[rows] = jnp.sin(angle)
        lows[s] = jnp.maximum(row + 1, row + WINDOW - spot.astype(jnp.int32))

    locals_.finish(lead)
    gather_f.spread(0)
    for j in range(1, geo.outer):
        gather_a.spread(j)
    gather_f.begin()
    for j in range(geo.outer):
        gather_a.corner(j)
    for j in range(geo.outer):
        gather_a.finish(j)
    gather_f.corner(0)
    gather_a.end()
    pending = [[functools.partial(gather_f.spread, j) for j in range(1, geo.outer)]]
    pending += [[functools.partial(gather_f.corner, j)] for j in range(1, geo.outer)]
    pending += [[functools.partial(gather_f.finish, j)] for j in range(geo.outer)]

    def tick(amount=1):
        for _ in range(amount):
            if pending:
                for action in pending.pop(0):
                    action()

    flatten_held(geo.attention, held, flat)
    at = BASE_GAINS
    for i, width in enumerate((D, HEAD_DIM, HEAD_DIM, D)):
        gains[i : i + 1, :width] = read_gain(flat, at, width)
        at += width // LANES
    unflatten(flat, BASE_KEY, wqkv, QUERY, HEAD_DIM)
    unflatten(flat, BASE_VALUE, wqkv, QUERY + HEAD_DIM, HEAD_DIM)
    gain = gains[0:1, :]
    gain_key = gains[2:3, :HEAD_DIM]
    halos = []
    per_step = STEP // block
    for s in range(0, seqs, per_step):
        rows = slice(s * block, (s + per_step) * block)
        x = tokens[rows].astype(jnp.float32)
        normed[rows] = (x * root_inverse(x) * gain).astype(jnp.bfloat16)
        made = dot_nn(normed[rows], wqkv[:, QUERY:])
        keys = made[:, :HEAD_DIM]
        keys = turn(keys * root_inverse(keys) * gain_key, cosine[rows], sine[rows])
        for i in range(per_step):
            part = slice(i * block, (i + 1) * block)
            kv[s + i, reach - block :, :HEAD_DIM] = keys[part].astype(jnp.bfloat16)
            kv[s + i, reach - block :, HEAD_DIM:] = made[part, HEAD_DIM:].astype(jnp.bfloat16)
        halo = Halo(place, wires, kv, block, s, per_step)
        halo.outward()
        halos.append(halo)
    tick()
    unflatten(flat, 0, wqkv, 0, QUERY)
    gain_query = gains[1:2, :HEAD_DIM] * HEAD_DIM**-0.5
    for s in range(0, seqs, per_step):
        rows = slice(s * block, (s + per_step) * block)
        made = dot_nn(normed[rows], wqkv[:, :QUERY])
        for h in range(HEADS):
            one = made[:, h * HEAD_DIM : (h + 1) * HEAD_DIM]
            one = turn(one * root_inverse(one) * gain_query, cosine[rows], sine[rows])
            q[h, rows] = one.astype(jnp.bfloat16)
    unflatten(flat, BASE_OUT, wo, 0, D)
    for src, dst in (
        (wqkv, out_wqkv),
        (wo, out_wo),
        (gains, out_gains),
        (q, out_q),
        (cosine, out_cosine),
        (sine, out_sine),
    ):
        locals_.copy(src, dst)
    chunk = 32
    lane = lax.broadcasted_iota(jnp.int32, (chunk, reach), 1)
    over = lax.broadcasted_iota(jnp.int32, (chunk, reach), 1) - lax.broadcasted_iota(
        jnp.int32, (chunk, reach), 0
    )

    def attend(s, carry):
        start = pl.multiple_of(s * block, block)
        rows = pl.ds(start, block)
        queries = q[:, rows, :].reshape(HEADS * block, HEAD_DIM)
        scores[...] = dot_nt(queries, kv[s, :, :HEAD_DIM])
        for r in range(0, HEADS * block, chunk):
            i = r % block
            low = jnp.concatenate([lows[s, i : i + chunk, :]] * (reach // LANES), axis=-1)
            seen = (lane >= low) & (over <= WINDOW + i)
            raised = jnp.where(seen, jnp.exp(scores[r : r + chunk]), 0.0)
            share = 1.0 / jnp.sum(raised, axis=-1, keepdims=True)
            probs[r : r + chunk] = (raised * share).astype(jnp.bfloat16)
        made = dot_nn(probs[...], kv[s, :, HEAD_DIM:])
        for h in range(HEADS):
            merged[rows, h * HEAD_DIM : (h + 1) * HEAD_DIM] = made[
                h * block : (h + 1) * block
            ].astype(jnp.bfloat16)
        return carry

    count = len(halos)
    for g in range(count + 2):
        tick()
        if g < count:
            halos[g].plane()
        if 1 <= g <= count:
            halos[g - 1].relay()
        if g > 1:
            tick()
        if g >= 2:
            halos[g - 2].end()
            lax.fori_loop((g - 2) * per_step, (g - 1) * per_step, attend, 0)
    locals_.copy(kv, out_kv)
    locals_.copy(merged, out_merged)
    gain_post = gains[3:4, :]
    for s in range(0, seqs, per_step):
        rows = slice(s * block, (s + per_step) * block)
        made = dot_nn(merged[rows], wo[...])
        projected[rows] = made
        hidden[rows] = tokens[rows].astype(jnp.float32) + made * root_inverse(made) * gain_post
        locals_.copy(projected.at[rows], out_projected.at[rows])
        locals_.copy(hidden.at[rows], out_hidden.at[rows])
    tick(len(pending))
    gather_f.end()
    wires.drain()
    locals_.drain()


def vmem(shape, dtype):
    return pltpu.VMEM(shape, dtype)


def forward_pass(geo, tokens, positions, attention_block, feed_block):
    count, rows, seqs, block = geo.count, geo.rows, geo.seqs, geo.block
    bf, f4 = jnp.bfloat16, jnp.float32
    half = HEAD_DIM // 2
    frequency = (
        rope_base ** (-(np.arange(half, dtype=np.float32) * np.float32(2.0) / HEAD_DIM))
    ).astype(np.float32)[None]
    wires = 2 * gather_wires(geo.outer) + geo.seqs // 2 * HALO_WIRES
    outs = [
        ((count, geo.feed.rows, LANES), bf),
        ((D, QUERY + 2 * HEAD_DIM), bf),
        ((QUERY, D), bf),
        ((8, D), f4),
        ((HEADS, rows, HEAD_DIM), bf),
        ((seqs, geo.reach, 2 * HEAD_DIM), bf),
        ((rows, QUERY), bf),
        ((rows, D), f4),
        ((rows, D), f4),
        ((rows, half), f4),
        ((rows, half), f4),
    ]
    flat_rows = geo.attention.count * geo.attention.stride + geo.attention.tail
    return pl.pallas_call(
        functools.partial(forward_kernel, geo),
        out_shape=[jax.ShapeDtypeStruct(*out) for out in outs],
        in_specs=[pl.BlockSpec(memory_space=pltpu.VMEM)] * 5,
        out_specs=[pl.BlockSpec(memory_space=pl.ANY)] * len(outs),
        scratch_shapes=[
            vmem((count, geo.attention.rows, LANES), bf),
            vmem((geo.feed.rows, LANES), bf),
            vmem((16 + geo.feed.rows, LANES), f4),
            vmem((flat_rows, LANES), f4),
            vmem((D, QUERY + 2 * HEAD_DIM), bf),
            vmem((QUERY, D), bf),
            vmem((8, D), f4),
            vmem((rows, half), f4),
            vmem((rows, half), f4),
            vmem((seqs, block, LANES), jnp.int32),
            vmem((rows, D), bf),
            vmem((HEADS, rows, HEAD_DIM), bf),
            vmem((seqs, geo.reach, 2 * HEAD_DIM), bf),
            vmem((HEADS * block, geo.reach), f4),
            vmem((HEADS * block, geo.reach), bf),
            vmem((rows, QUERY), bf),
            vmem((rows, D), f4),
            vmem((rows, D), f4),
            pltpu.SemaphoreType.DMA((wires,)),
            pltpu.SemaphoreType.DMA((wires,)),
            pltpu.SemaphoreType.DMA((32,)),
        ],
        compiler_params=pltpu.CompilerParams(
            collective_id=0, has_side_effects=True, vmem_limit_bytes=60 << 20
        ),
    )(tokens.reshape(rows, D), positions, jnp.asarray(frequency), attention_block, feed_block)


MATRIX = D * FF // LANES
BEND = 0.044715
SLOPE = math.sqrt(2.0 / math.pi)


def feed_pieces(blocks, which):
    base, stop = which * MATRIX, (which + 1) * MATRIX
    if which == 2:
        stop = blocks.count * blocks.stride + blocks.tail
    found = []
    for d in range(blocks.count):
        low = max(d * blocks.stride, base)
        high = min(d * blocks.stride + blocks.rows, stop)
        if low < high:
            found.append((d, low - base, high - base, base - d * blocks.stride))
    return found


def feed_phase(geo, locals_, held_in, cotangent_in, mixed_out, split, grad, begin, tick, *refs):
    (flat, twin, down, act, pair, feed_in, turned_in, grad_down) = refs
    mixed = cotangent = feed_in
    blocks = geo.feed
    ends = [-(-(-(-(m + 1) * MATRIX // blocks.stride)) // 4) for m in range(3)]
    starts = [0] + ends[:-1]
    loads = [
        locals_.copy(held_in.at[pl.ds(a, b - a)], split.at[pl.ds(a, b - a)])
        for a, b in zip(starts, ends)
    ]
    load_cotangent = locals_.copy(cotangent_in, grad_down)

    def index(d):
        return d // 4, d // 2 % 2, d % 2

    def unpack(which):
        for d, low, high, shift in feed_pieces(blocks, which):
            mid = min(high, max(low, d * blocks.stride - which * MATRIX + blocks.tail))
            if d and low < mid:
                flat[low:mid] += split[*index(d), low + shift : mid + shift].astype(jnp.float32)
            else:
                mid = low
            flat[mid:high] = split[*index(d), mid + shift : high + shift].astype(jnp.float32)

    def pack(which):
        for d, low, high, shift in feed_pieces(blocks, which):
            split[*index(d), low + shift : high + shift] = flat[low:high].astype(jnp.bfloat16)

    for which, (matrix, first, width) in enumerate(
        ((twin, 0, FF), (twin, FF, FF), (down, 0, D))
    ):
        locals_.finish(loads[which])
        unpack(which)
        unflatten(flat, 0, matrix, first, width)
    gain_feed = read_gain(flat, MATRIX, D)
    gain_out = read_gain(flat, MATRIX + D // LANES, D)

    total, step = geo.rows, WIDE
    spans = [slice(r, r + STEP) for r in range(0, total, STEP)]
    for rows in spans:
        h = grad[rows]
        feed_in[rows] = (h * root_inverse(h) * gain_feed).astype(jnp.bfloat16)

    def rise(i, carry):
        columns = pl.ds(pl.multiple_of(i * step, step), step)
        others = pl.ds(pl.multiple_of(FF + i * step, step), step)
        for rows in spans:
            g = dot_nn(feed_in[rows], twin[:, columns])
            u = dot_nn(feed_in[rows], twin[:, others])
            square = g * g
            t = jnp.tanh(g * (SLOPE + SLOPE * BEND * square))
            half = 0.5 + 0.5 * t
            soft = g * half
            act[rows, columns] = (soft * u).astype(jnp.bfloat16)
            pair[rows, others] = soft.astype(jnp.bfloat16)
            slope = half * (1.0 + g * (1.0 - t) * (SLOPE + 3.0 * SLOPE * BEND * square))
            pair[rows, columns] = (u * slope).astype(jnp.bfloat16)
        return carry

    lax.fori_loop(0, FF // step, rise, 0)
    turned_in[...] = feed_in[...].T

    def settle(i, sum_out):
        rows = pl.ds(pl.multiple_of(i * STEP, STEP), STEP)
        made = dot_nn(act[rows], down[...])
        r = root_inverse(made)
        mixed[rows] = (grad[rows] + made * r * gain_out).astype(jnp.bfloat16)
        e = grad_down[rows].astype(jnp.float32)
        unit = made * r
        sum_out = sum_out + jnp.sum(e * unit, axis=0, keepdims=True)
        c = e * gain_out
        grad_down[rows] = (
            r * (c - unit * jnp.mean(unit * c, axis=-1, keepdims=True))
        ).astype(jnp.bfloat16)
        return sum_out

    locals_.finish(load_cotangent)
    sum_out = lax.fori_loop(0, total // STEP, settle, jnp.zeros((1, D), jnp.float32))
    store_mixed = locals_.copy(mixed, mixed_out)

    def fall(i, carry):
        columns = pl.ds(pl.multiple_of(i * step, step), step)
        others = pl.ds(pl.multiple_of(FF + i * step, step), step)
        for rows in spans:
            made = dot_nt(grad_down[rows], down[columns, :])
            for at in (columns, others):
                pair[rows, at] = (made * pair[rows, at].astype(jnp.float32)).astype(jnp.bfloat16)
        return carry

    lax.fori_loop(0, FF // step, fall, 0)

    def back(i, sum_feed):
        rows = pl.ds(pl.multiple_of(i * STEP, STEP), STEP)
        made = dot_nt(pair[rows], twin[...])
        h = grad[rows]
        r = root_inverse(h)
        unit = h * r
        sum_feed = sum_feed + jnp.sum(made * unit, axis=0, keepdims=True)
        c = made * gain_feed
        grad[rows] = cotangent[rows].astype(jnp.float32) + r * (
            c - unit * jnp.mean(unit * c, axis=-1, keepdims=True)
        )
        return sum_feed

    def wide(i, carry, first):
        made = dot_nn(turned_in[...], pair[:, pl.ds(pl.multiple_of(first + i * step, step), step)])
        for k in range(step // LANES):
            flat[pl.ds(i * (step // LANES) + k, D, stride=FF // LANES), :] = made[
                :, k * LANES : (k + 1) * LANES
            ]
        return carry

    locals_.finish(store_mixed)
    load_cotangent = locals_.copy(cotangent_in, cotangent)
    lax.fori_loop(0, FF // step, functools.partial(wide, first=0), 0)
    pack(0)
    lax.fori_loop(0, FF // step, functools.partial(wide, first=FF), 0)
    pack(1)

    def tall(i, carry):
        columns = pl.ds(pl.multiple_of(i * step, step), step)
        made = dot_tn(act[:, columns], grad_down[...])
        for k in range(D // LANES):
            flat[pl.ds(i * (step * D // LANES) + k, step, stride=D // LANES), :] = made[
                :, k * LANES : (k + 1) * LANES
            ]
        return carry

    lax.fori_loop(0, FF // step, tall, 0)
    flat[MATRIX:] = jnp.zeros_like(flat[MATRIX:])
    pack(2)
    begin()
    locals_.finish(load_cotangent)
    sum_feed = jnp.zeros((1, D), jnp.float32)
    for i in range(0, total // STEP, 2):
        sum_feed = lax.fori_loop(i, i + 2, back, sum_feed)
        tick()
    write_gain(flat, MATRIX, sum_feed)
    write_gain(flat, MATRIX + D // LANES, sum_out)
    last = blocks.count - 1
    low = blocks.count * blocks.stride - 2 * MATRIX
    split[*index(last), blocks.stride :] = flat[low:].astype(jnp.bfloat16)


class Scatter:
    def __init__(self, place, wires, other, own, lands, result, piece):
        self.place, self.wires, self.other, self.own, self.result = place, wires, other, own, result
        self.by_core, self.first_x, self.first_y, self.second_x, self.second_y, self.by_outer = lands
        first, cut, last, at_x, at_y = piece
        self.split = cut < last
        self.all = pl.ds(first, last - first)
        self.rows_x, self.rows_y = pl.ds(first, cut - first), pl.ds(cut, last - cut)
        self.land_x, self.land_y = pl.ds(at_x, cut - first), pl.ds(at_y, last - cut)
        p, plan = place, wires.plan
        mine, theirs = self.column_of(p.b), self.column_of(1 - p.b)
        self.from_core = plan(
            other.at[:, :, 1 - p.c, self.all], self.by_core.at[:, :, self.all], p.sibling()
        )
        self.from_x = plan(
            own.at[theirs, :, self.rows_x], self.first_x.at[:, :, self.land_x], p.x_peer()
        )
        self.over_y = plan(
            own.at[mine, 1 - p.y, self.rows_x], self.second_y.at[:, self.land_x], p.y_peer()
        )
        if self.split:
            self.from_y = plan(
                own.at[:, 1 - p.y, self.rows_y], self.first_y.at[:, self.land_y], p.y_peer()
            )
            self.over_x = plan(
                own.at[theirs, p.y, self.rows_y], self.second_x.at[:, self.land_y], p.x_peer()
            )
        self.from_outer = [
            plan(
                own.at[p.b * p.outer + p.flip(k), p.y, self.all],
                self.by_outer.at[k - 1, self.all],
                p.flip_peer(k),
            )
            for k in range(1, p.outer)
        ]

    def add(self, i, y, rows, land):
        self.own[i, y, rows] = (
            self.own[i, y, rows].astype(jnp.float32) + land.astype(jnp.float32)
        ).astype(jnp.bfloat16)

    def column_of(self, b):
        return pl.ds(b * self.place.outer, self.place.outer)

    def core(self):
        self.from_core.start()

    def plane(self):
        p = self.place
        self.from_core.wait_recv()

        def body(i, carry):
            for y in range(2):
                self.add(i, y, self.all, self.by_core[i, y, self.all])
            return carry

        lax.fori_loop(0, 2 * p.outer, body, 0)
        self.from_x.start()
        if self.split:
            self.from_y.start()

    def cross(self):
        p = self.place
        self.from_x.wait_recv()

        def body(hi, carry):
            for y in range(2):
                self.add(p.b * p.outer + hi, y, self.rows_x, self.first_x[hi, y, self.land_x])
            return carry

        lax.fori_loop(0, p.outer, body, 0)
        self.over_y.start()
        if self.split:
            self.from_y.wait_recv()

            def body(i, carry):
                self.add(i, p.y, self.rows_y, self.first_y[i, self.land_y])
                return carry

            lax.fori_loop(0, 2 * p.outer, body, 0)
            self.over_x.start()

    def column(self):
        p = self.place
        self.over_y.wait_recv()
        if self.split:
            self.over_x.wait_recv()

        def body(hi, carry):
            i = p.b * p.outer + hi
            self.add(i, p.y, self.rows_x, self.second_y[hi, self.land_x])
            if self.split:
                self.add(i, p.y, self.rows_y, self.second_x[hi, self.land_y])
            return carry

        lax.fori_loop(0, p.outer, body, 0)
        for made in self.from_outer:
            made.start()

    def end(self):
        p = self.place
        total = self.own[p.b * p.outer + p.hi, p.y, self.all].astype(jnp.float32)
        for k, made in enumerate(self.from_outer):
            made.wait_recv()
            total = total + self.by_outer[k, self.all].astype(jnp.float32)
        self.result[self.all] = total


def scatter_wires(outer):
    return 5 + outer - 1


def cut_pieces(bounds, shares):
    pieces, at_x, at_y = [], 0, 0
    for first, last, share in zip(bounds, bounds[1:], shares):
        cut = first + max(16, int((last - first) * share) // 16 * 16)
        pieces.append((first, cut, last, at_x, at_y))
        at_x, at_y = at_x + cut - first, at_y + last - cut
    return pieces, at_x, at_y


def land_shapes(rows, bounds, shares, outer):
    rows_x, rows_y = cut_pieces(bounds, shares)[1:]
    return [
        pltpu.VMEM(shape + (LANES,), jnp.bfloat16)
        for shape in (
            (2 * outer, 2, rows),
            (outer, 2, rows_x),
            (2 * outer, rows_y),
            (outer, rows_y),
            (outer, rows_x),
            (outer - 1, rows),
        )
    ]


class Return:
    def __init__(self, place, wires, kv, own, by_core, by_y, by_outer, block, first, size):
        self.place, self.wires, self.kv, self.own, self.block = place, wires, kv, own, block
        self.by_core, self.by_y, self.by_outer = by_core, by_y, by_outer
        self.group = pl.ds(first, size)
        self.each = range(first, first + size)

    def rows(self, at):
        return slice(at * self.block, (at + 1) * self.block)

    def slot(self, at):
        return self.kv.at[self.group, pl.ds(at * self.block, self.block)]

    def core(self):
        p = self.place
        self.from_core = [
            self.wires.copy(
                self.slot(at), self.by_core.at[self.group, pl.ds(i * self.block, self.block)], p.sibling()
            )
            for i, at in enumerate((1, 3))
        ]

    def grow(self, s, at, extra):
        rows = self.rows(at)
        self.kv[s, rows] = (self.kv[s, rows].astype(jnp.float32) + extra).astype(jnp.bfloat16)

    def plane(self):
        p = self.place
        for made in self.from_core:
            made.wait_recv()
        for s in self.each:

            @pl.when(p.c == 0)
            def _():
                self.grow(s, 2, self.by_core[s, self.rows(0)].astype(jnp.float32))
                self.own[s] += self.by_core[s, self.rows(1)].astype(jnp.float32)

            @pl.when(p.c == 1)
            def _():
                self.grow(s, 0, self.by_core[s, self.rows(0)].astype(jnp.float32))
                self.grow(s, 2, self.by_core[s, self.rows(1)].astype(jnp.float32))

        self.from_y = self.wires.copy(self.slot(2), self.by_y.at[self.group], p.y_peer())

    def outward(self):
        p = self.place
        self.from_y.wait_recv()
        for s in self.each:

            @pl.when(p.y == 0)
            def _():
                self.own[s] += self.by_y[s].astype(jnp.float32)

            @pl.when(p.y == 1)
            def _():
                self.grow(s, 0, self.by_y[s].astype(jnp.float32))

        self.from_outer = self.wires.copy(
            self.slot(0), self.by_outer.at[self.group], p.outer_peer(p.outer - 1), p.hi > 0
        )

    def end(self):
        p = self.place

        @pl.when(p.hi + 1 < p.outer)
        def _():
            self.from_outer.wait_recv()
            for s in self.each:
                self.own[s] += self.by_outer[s].astype(jnp.float32)


RETURN_WIRES = 4
FEED_SHARES = (0.5, 1.0, 1.0, 1.0)
ATTENTION_SHARES = (0.5, 0.5, 1.0)


def fill_blocks(blocks, split, flat, margin, base, stop):
    even = blocks.stride % 16 == 0
    for d in range(blocks.count):
        low, high = max(d * blocks.stride, base), min(d * blocks.stride + blocks.rows, stop)
        if low >= high:
            continue
        i, y, c = d // 4, d // 2 % 2, d % 2
        first, last = low - d * blocks.stride, high - d * blocks.stride
        if even:
            split[i, y, c, first:last] = flat[low - base + margin : high - base + margin].astype(
                jnp.bfloat16
            )
        else:
            start, end = first // 16 * 16, -(-last // 16) * 16
            source = low - base + margin - (first - start)
            split[i, y, c, start:end] = (
                split[i, y, c, start:end].astype(jnp.float32)
                + flat[source : source + end - start]
            ).astype(jnp.bfloat16)


MARGIN = 16


def backward_kernel(
    geo, positions, gains, tokens_in, wqkv_in, wo_in, q_in, kv_in, merged_in, projected_in,
    hidden_in, cosine_in, sine_in, held_in, cotangent_in, *refs
):
    grad_tokens, mixed_out, attention_sum, feed_sum = refs[:4]
    grad, split_f, split_a, by_core_kv, by_y_kv, by_outer_kv = refs[4:10]
    lands_a, lands_f = refs[10:16], refs[16:22]
    send, recv, local = refs[22:]
    place = Place()
    wires, locals_ = Wires(send, recv), Locals(local)
    bf, f4, rows, half = jnp.bfloat16, jnp.float32, geo.rows, HEAD_DIM // 2
    load_hidden = locals_.copy(hidden_in, grad)
    announce(place)
    pieces = cut_pieces(geo.feed_bounds, FEED_SHARES)[0]
    own_f = split_f.at[:, :, place.c]
    one, two, three, four = [
        Scatter(place, wires, split_f, own_f, lands_f, feed_sum, piece) for piece in pieces
    ]

    def begin():
        meet(place)
        for part in (one, two, three):
            part.core()

    pending = [
        [one.plane], [two.plane],
        [],
        [one.cross], [three.plane], [], [one.column],
        [two.cross],
        [four.plane],
        [two.column, three.cross, one.end],
        [four.cross, three.column],
        [two.end, four.column, three.end, four.end],
    ]

    def tick():
        for action in pending.pop(0):
            action()

    locals_.finish(load_hidden)
    pl.run_scoped(
        functools.partial(
            feed_phase, geo, locals_, held_in, cotangent_in, mixed_out, split_f, grad, begin, tick
        ),
        vmem((MATRIX + geo.feed.tail, LANES), f4),
        vmem((D, 2 * FF), bf),
        vmem((FF, D), bf),
        vmem((rows, FF), bf),
        vmem((rows, 2 * FF), bf),
        vmem((rows, D), bf),
        vmem((D, rows), bf),
        vmem((rows, D), bf),
    )
    four.core()
    pl.run_scoped(
        functools.partial(
            attention_phase, geo, place, wires, locals_, positions, gains,
            (tokens_in, wqkv_in, wo_in, q_in, kv_in, merged_in, projected_in, cosine_in, sine_in),
            grad_tokens, attention_sum, grad, split_a, by_core_kv, by_y_kv, by_outer_kv, lands_a,
            pending, tick,
        ),
        vmem((rows, D), bf),
        vmem(wqkv_in.shape, bf),
        vmem(wo_in.shape, bf),
        vmem(q_in.shape, bf),
        vmem(kv_in.shape, bf),
        vmem((rows, QUERY + 2 * HEAD_DIM), bf),
        vmem((rows, half), f4),
        vmem((rows, half), f4),
        vmem((2 * geo.reach, D), f4),
        vmem((rows, D), bf),
        vmem((max(D, geo.reach), max(rows, 2 * HEADS * geo.block)), bf),
        vmem((HEADS, rows, HEAD_DIM), bf),
        vmem((rows, D), bf),
        vmem((geo.seqs, geo.block, 2 * HEAD_DIM), f4),
        vmem((2 * MARGIN + QUERY * D // LANES, LANES), f4),
    )


def attention_phase(
    geo, place, wires, locals_, positions, gains, saved, grad_tokens, attention_sum, grad,
    split, by_core_kv, by_y_kv, by_outer_kv, lands_a, pending, tick, *refs
):
    tokens_in, wqkv_in, wo_in, q_in, kv_in, merged_in, projected_in, cosine_in, sine_in = saved
    (
        tokens, wqkv, wo, q, kv, pair, cosine, sine, work, normed, shared, grad_out, out_rows,
        own_kv, flat,
    ) = refs
    seqs, block, reach, total, step = geo.seqs, geo.block, geo.reach, geo.rows, STEP
    turned = shared.at[pl.ds(0, D), pl.ds(0, total)]
    probs = shared.at[pl.ds(0, reach), pl.ds(0, HEADS * block)]
    logits = shared.at[pl.ds(0, reach), pl.ds(HEADS * block, HEADS * block)]
    projected = work.at[pl.ds(0, total)]
    scores = work.at[pl.ds(0, reach), pl.ds(0, HEADS * block)]
    slopes = work.at[pl.ds(reach, reach), pl.ds(0, HEADS * block)]
    load_projected = locals_.copy(projected_in, projected)
    load_wo = locals_.copy(wo_in, wo)
    load_tokens = locals_.copy(tokens_in, tokens)
    load_merged = locals_.copy(merged_in, pair.at[:, pl.ds(0, QUERY)])
    load_q, load_kv = locals_.copy(q_in, q), locals_.copy(kv_in, kv)
    load_rest = [
        locals_.copy(wqkv_in, wqkv), locals_.copy(cosine_in, cosine), locals_.copy(sine_in, sine)
    ]
    gain_attention, gain_query = gains[0:1, :], gains[1:2, :HEAD_DIM]
    gain_key, gain_post = gains[2:3, :HEAD_DIM], gains[3:4, :]
    for made in (load_projected, load_wo, load_tokens):
        locals_.finish(made)

    def start_rows(i, summed):
        rows = pl.ds(pl.multiple_of(i * step, step), step)
        made, e = projected[rows], grad[rows]
        r = root_inverse(made)
        unit = made * r
        c = e * gain_post
        out_rows[rows] = (r * (c - unit * jnp.mean(unit * c, axis=-1, keepdims=True))).astype(
            jnp.bfloat16
        )
        x = tokens[rows].astype(jnp.float32)
        normed[rows] = (x * root_inverse(x) * gain_attention).astype(jnp.bfloat16)
        for h in range(HEADS):
            grad_out[h, rows] = dot_nt(
                out_rows[rows], wo[h * HEAD_DIM : (h + 1) * HEAD_DIM, :]
            ).astype(jnp.bfloat16)
        return summed + jnp.sum(e * unit, axis=0, keepdims=True)

    sum_post = lax.fori_loop(0, total // step, start_rows, jnp.zeros((1, D), jnp.float32))
    tick()
    blocks = geo.attention
    flat[0:MARGIN] = jnp.zeros((MARGIN, LANES), jnp.float32)
    flat[MARGIN + QUERY * D // LANES :] = jnp.zeros((MARGIN, LANES), jnp.float32)
    if blocks.stride % 16:
        split[...] = jnp.zeros_like(split)
    locals_.finish(load_merged)

    for made in [load_q, load_kv] + load_rest:
        locals_.finish(made)

    wide = HEADS * block
    chunk = 32
    lane = lax.rem(lax.broadcasted_iota(jnp.int32, (chunk, wide), 1), block)
    line = lax.broadcasted_iota(jnp.int32, (chunk, wide), 0)

    def attend(s, carry):
        rows = pl.ds(pl.multiple_of(s * block, block), block)
        queries = q[:, rows, :].reshape(wide, HEAD_DIM)
        given = grad_out[:, rows, :].reshape(wide, HEAD_DIM)
        scores[...] = dot_nt(kv[s, :, :HEAD_DIM], queries)
        slopes[...] = dot_nt(kv[s, :, HEAD_DIM:], given)
        spot = jnp.concatenate([positions[pl.ds(s, 1), :]] * HEADS, axis=-1)
        low = jnp.maximum(lane[0:1] + 1, lane[0:1] + WINDOW - spot)
        total_e = jnp.zeros((8, wide), jnp.float32)
        total_d = jnp.zeros((8, wide), jnp.float32)
        for r in range(0, reach, chunk):
            seen = (line + r >= low) & (line + (r - WINDOW) <= lane)
            raised = jnp.where(seen, jnp.exp(scores[r : r + chunk]), 0.0)
            scores[r : r + chunk] = raised
            moved = raised * slopes[r : r + chunk]
            for k in range(0, chunk, 8):
                total_e = total_e + raised[k : k + 8]
                total_d = total_d + moved[k : k + 8]
        share = 1.0 / jnp.sum(total_e, axis=0, keepdims=True)
        inner = jnp.sum(total_d, axis=0, keepdims=True) * share
        for r in range(0, reach, chunk):
            p = scores[r : r + chunk] * share
            probs[r : r + chunk] = p.astype(jnp.bfloat16)
            logits[r : r + chunk] = (p * (slopes[r : r + chunk] - inner)).astype(jnp.bfloat16)
        grad_q = dot_tn(logits[...], kv[s, :, :HEAD_DIM]) * HEAD_DIM**-0.5
        grad_k = dot_nn(logits[...], queries)
        grad_v = dot_nn(probs[...], given)
        early = reach - block
        kv[s, :early, :HEAD_DIM] = grad_k[:early].astype(jnp.bfloat16)
        kv[s, :early, HEAD_DIM:] = grad_v[:early].astype(jnp.bfloat16)
        own_kv[s, :, :HEAD_DIM] = grad_k[early:]
        own_kv[s, :, HEAD_DIM:] = grad_v[early:]
        for h in range(HEADS):
            q[h, rows] = grad_q[h * block : (h + 1) * block].astype(jnp.bfloat16)
        return carry

    size = 1
    returns = [
        Return(place, wires, kv, own_kv, by_core_kv, by_y_kv, by_outer_kv, block, s, size)
        for s in range(0, seqs, size)
    ]
    for g, group in enumerate(returns):
        lax.fori_loop(g * size, (g + 1) * size, attend, 0)
        group.core()
        if g >= 1:
            returns[g - 1].plane()
        if g >= 2:
            returns[g - 2].outward()
        if g % 2:
            tick()
    last = len(returns) - 1
    turned[...] = normed[...].T

    def tall(i, carry):
        columns = pl.ds(pl.multiple_of(i * step, step), step)
        made = dot_tn(pair[:, columns], out_rows[...])
        for k in range(D // LANES):
            flat[pl.ds(MARGIN + i * (step * D // LANES) + k, step, stride=D // LANES), :] = made[
                :, k * LANES : (k + 1) * LANES
            ]
        return carry

    lax.fori_loop(0, QUERY // step, tall, 0)
    fill_blocks(blocks, split, flat, MARGIN, BASE_OUT, BASE_GAINS)
    def query_rows(i, summed):
        rows = pl.ds(pl.multiple_of(i * step, step), step)
        made = dot_nn(normed[rows], wqkv[:, :QUERY])
        for h in range(HEADS):
            raw = made[:, h * HEAD_DIM : (h + 1) * HEAD_DIM]
            e = turn_back(q[h, rows].astype(jnp.float32), cosine[rows], sine[rows])
            r = root_inverse(raw)
            unit = raw * r
            summed = summed + jnp.sum(e * unit, axis=0, keepdims=True)
            c = e * gain_query
            pair[rows, h * HEAD_DIM : (h + 1) * HEAD_DIM] = (
                r * (c - unit * jnp.mean(unit * c, axis=-1, keepdims=True))
            ).astype(jnp.bfloat16)
        return summed

    returns[last].plane()
    returns[last - 1].outward()
    tick()
    sum_query = lax.fori_loop(0, total // step, query_rows, jnp.zeros((1, HEAD_DIM), jnp.float32))
    returns[last].outward()
    tick()

    def broad(i, carry, first, width):
        columns = pl.ds(pl.multiple_of(first + i * step, step), step)
        made = dot_nn(turned[...], pair[:, columns])
        for k in range(step // LANES):
            start = MARGIN + i * (step // LANES) + k
            flat[pl.ds(start, D, stride=width // LANES), :] = made[:, k * LANES : (k + 1) * LANES]
        return carry

    lax.fori_loop(0, QUERY // step, functools.partial(broad, first=0, width=QUERY), 0)
    fill_blocks(blocks, split, flat, MARGIN, 0, BASE_KEY)
    tick()
    for group in returns:
        group.end()

    def key_rows(i, summed):
        rows = pl.ds(pl.multiple_of(i * step, step), step)
        per = step // block
        raw = dot_nn(normed[rows], wqkv[:, QUERY : QUERY + HEAD_DIM])
        both = own_kv[pl.ds(i * per, per)].reshape(step, 2 * HEAD_DIM)
        e = turn_back(both[:, :HEAD_DIM], cosine[rows], sine[rows])
        r = root_inverse(raw)
        unit = raw * r
        c = e * gain_key
        pair[rows, QUERY : QUERY + HEAD_DIM] = (
            r * (c - unit * jnp.mean(unit * c, axis=-1, keepdims=True))
        ).astype(jnp.bfloat16)
        pair[rows, QUERY + HEAD_DIM :] = both[:, HEAD_DIM:].astype(jnp.bfloat16)
        return summed + jnp.sum(e * unit, axis=0, keepdims=True)

    sum_key = lax.fori_loop(0, total // step, key_rows, jnp.zeros((1, HEAD_DIM), jnp.float32))
    for first, base in ((QUERY, BASE_KEY), (QUERY + HEAD_DIM, BASE_VALUE)):
        broad(0, 0, first, HEAD_DIM)
        size_rows = D * HEAD_DIM // LANES
        flat[MARGIN + size_rows : 2 * MARGIN + size_rows] = jnp.zeros((MARGIN, LANES), jnp.float32)
        fill_blocks(blocks, split, flat, MARGIN, base, base + size_rows)

    def end_rows(i, summed):
        rows = pl.ds(pl.multiple_of(i * step, step), step)
        made = dot_nt(pair[rows], wqkv[...])
        x = tokens[rows].astype(jnp.float32)
        r = root_inverse(x)
        unit = x * r
        c = made * gain_attention
        grad[rows] = grad[rows] + r * (c - unit * jnp.mean(unit * c, axis=-1, keepdims=True))
        return summed + jnp.sum(made * unit, axis=0, keepdims=True)

    tail = geo.attention.tail
    own = split.at[:, :, place.c]
    one, two, three = [
        Scatter(place, wires, split, own, lands_a, attention_sum, piece)
        for piece in cut_pieces(geo.attention_bounds, ATTENTION_SHARES)[0]
    ]
    one.core()
    two.core()
    tick()
    sum_attention = jnp.zeros((1, D), jnp.float32)
    half = total // step // 2
    one.plane()
    sum_attention = lax.fori_loop(0, half, end_rows, sum_attention)
    two.plane()
    sum_attention = lax.fori_loop(half, 2 * half, end_rows, sum_attention)
    locals_.copy(grad, grad_tokens)
    tick()
    flat[MARGIN : 2 * MARGIN + tail] = jnp.zeros((MARGIN + tail, LANES), jnp.float32)
    at = MARGIN
    for made in (sum_attention, sum_query, sum_key, sum_post):
        write_gain(flat, at, made)
        at += made.shape[1] // LANES
    fill_blocks(blocks, split, flat, MARGIN, BASE_GAINS, blocks.count * blocks.stride + tail)
    three.core()
    for action in (
        one.cross, three.plane, two.cross, one.column, three.cross, two.column, three.column,
        one.end, two.end, three.end,
    ):
        action()
    wires.drain()
    locals_.drain()


def backward_pass(geo, tokens, positions, saved, hidden, feed_held, cotangent):
    bf, f4, rows, seqs, block = jnp.bfloat16, jnp.float32, geo.rows, geo.seqs, geo.block
    wqkv, wo, gains, q, kv, merged, projected, cosine, sine = saved
    rows_a, rows_f, outer = geo.attention.rows, geo.feed.rows, geo.outer
    outs = [((rows, D), f4), ((rows, D), bf), ((rows_a, LANES), f4), ((rows_f, LANES), f4)]
    full, hbm = pl.BlockSpec(memory_space=pltpu.VMEM), pl.BlockSpec(memory_space=pl.ANY)
    wires = (len(geo.feed_bounds) + len(geo.attention_bounds) - 2) * scatter_wires(
        outer
    ) + seqs * RETURN_WIRES
    return pl.pallas_call(
        functools.partial(backward_kernel, geo),
        out_shape=[jax.ShapeDtypeStruct(*out) for out in outs],
        in_specs=[full] * 2 + [hbm] * 12,
        out_specs=[hbm, hbm, full, full],
        scratch_shapes=[
            vmem((rows, D), f4),
            vmem((2 * outer, 2, 2, rows_f, LANES), bf),
            vmem((2 * outer, 2, 2, rows_a, LANES), bf),
            vmem((seqs, 2 * block, 2 * HEAD_DIM), bf),
            vmem((seqs, block, 2 * HEAD_DIM), bf),
            vmem((seqs, block, 2 * HEAD_DIM), bf),
        ]
        + land_shapes(rows_a, geo.attention_bounds, ATTENTION_SHARES, outer)
        + land_shapes(rows_f, geo.feed_bounds, FEED_SHARES, outer)
        + [
            pltpu.SemaphoreType.DMA((wires,)),
            pltpu.SemaphoreType.DMA((wires,)),
            pltpu.SemaphoreType.DMA((32,)),
        ],
        compiler_params=pltpu.CompilerParams(
            collective_id=1, has_side_effects=True, vmem_limit_bytes=63 << 20
        ),
    )(
        positions, gains, tokens.reshape(rows, D), wqkv, wo, q, kv, merged, projected, hidden,
        cosine, sine, feed_held.reshape(2 * outer, 2, 2, rows_f, LANES), cotangent.reshape(rows, D),
    )


def on_device(tokens, attention_params, feed_params, positions, cotangent):
    geo = Geo(tokens, attention_params, feed_params)
    device = lax.axis_index("batch") * lax.axis_size("seq") + lax.axis_index("seq")
    (
        feed_held, wqkv, weight_out, gains, q, kv, merged, projected, hidden, cosine, sine,
    ) = forward_pass(
        geo, tokens, positions, geo.attention.pad(attention_params), geo.feed.pad(feed_params)
    )
    grad_tokens, mixed, attention_sum, feed_sum = backward_pass(
        geo,
        tokens,
        positions,
        (wqkv, weight_out, gains, q, kv, merged, projected, cosine, sine),
        hidden,
        feed_held,
        cotangent,
    )
    return (
        mixed.reshape(tokens.shape),
        grad_tokens.reshape(tokens.shape),
        geo.attention.take(attention_sum, device),
        geo.feed.take(feed_sum, device),
    )


def solution(mesh):
    return jax.shard_map(
        on_device,
        mesh=mesh,
        in_specs=(
            P("batch", "seq", None),
            P(("batch", "seq")),
            P(("batch", "seq")),
            P("batch", "seq"),
            P("batch", "seq", None),
        ),
        out_specs=(
            P("batch", "seq", None),
            P("batch", "seq", None),
            P(("batch", "seq")),
            P(("batch", "seq")),
        ),
        check_vma=False,
    )
```

```python
import functools
import math

import jax
import jax.numpy as jnp
import numpy as np
from jax import lax
from jax.experimental import pallas as pl
from jax.experimental.pallas import tpu as pltpu
from jax.sharding import PartitionSpec as P

MESH = pl.DeviceIdType.MESH
LANES = 128

D = 640
HEADS = 4
HEAD_DIM = 256
FF = 2048
WINDOW = 512


rope_base = 10000.0


class Place:
    def __init__(self):
        self.devices_seq = lax.axis_size("seq")
        self.outer = self.devices_seq // 4
        self.count = 2 * self.devices_seq
        self.b = lax.axis_index("batch")
        s = lax.axis_index("seq")
        self.hi = lax.div(s, 4)
        self.y = lax.rem(lax.div(s, 2), 2)
        self.c = lax.rem(s, 2)

    def block(self, b, hi, y, c):
        return b * self.devices_seq + hi * 4 + y * 2 + c

    def seq_id(self, hi, y, c):
        return (self.b, hi * 4 + y * 2 + c)

    def mine(self):
        return self.block(self.b, self.hi, self.y, self.c)

    def x_peer(self):
        return (1 - self.b, self.hi * 4 + self.y * 2 + self.c)

    def y_peer(self):
        return self.seq_id(self.hi, 1 - self.y, self.c)

    def sibling(self):
        return self.seq_id(self.hi, self.y, 1 - self.c)

    def outer_at(self, k):
        return lax.rem(self.hi + k, self.outer)

    def flip(self, k):
        found, bit = 0, 1
        while bit < self.outer:
            own = lax.rem(lax.div(self.hi, bit), 2)
            found = found + bit * ((1 - own) if k & bit else own)
            bit *= 2
        return found

    def flip_peer(self, k):
        return self.seq_id(self.flip(k), self.y, self.c)

    def outer_peer(self, k):
        return self.seq_id(self.outer_at(k), self.y, self.c)

    def peers(self):
        return [self.x_peer(), self.y_peer(), self.sibling()] + [
            self.outer_peer(k) for k in range(1, self.outer)
        ]


def announce(place):
    barrier = pltpu.get_barrier_semaphore()
    for peer in place.peers():
        pl.semaphore_signal(barrier, inc=1, device_id=peer, device_id_type=MESH)


def meet(place):
    pl.semaphore_wait(pltpu.get_barrier_semaphore(), len(place.peers()))


def guarded(when, action):
    if when is None:
        action()
    else:
        pl.when(when)(action)


class Wires:
    def __init__(self, send_sems, recv_sems):
        self.send_sems, self.recv_sems = send_sems, recv_sems
        self.used = 0
        self.sent = []

    def plan(self, src, dst, peer, when=None):
        made = pltpu.make_async_remote_copy(
            src_ref=src,
            dst_ref=dst,
            send_sem=self.send_sems.at[self.used],
            recv_sem=self.recv_sems.at[self.used],
            device_id=peer,
            device_id_type=MESH,
        )
        self.used += 1
        self.sent.append((made, when))
        return made

    def copy(self, src, dst, peer, when=None):
        made = self.plan(src, dst, peer, when)
        guarded(when, made.start)
        return made

    def drain(self):
        for made, when in self.sent:
            guarded(when, made.wait_send)
        self.sent = []


def gather_wires(outer):
    return outer - 1 + 4 * outer + 4 * outer


class Gather:
    def __init__(self, place, wires, held, first, last, share):
        self.place, self.wires, self.held = place, wires, held
        self.first, self.last = first, last
        self.cut = first + int((last - first) * share) // 16 * 16
        self.from_outer = {}
        self.from_x, self.from_y, self.diag, self.twin = {}, {}, {}, []

    def send(self, index, peer, first=None, last=None):
        first = self.first if first is None else first
        last = self.last if last is None else last
        ref = self.held.at[index, pl.ds(first, last - first)]
        return self.wires.copy(ref, ref, peer)

    def begin(self):
        p = self.place
        for k in range(1, p.outer):
            self.from_outer[k] = self.send(p.mine(), p.flip_peer(k))

    def spread(self, j):
        p = self.place
        if j:
            self.from_outer[j].wait_recv()
        index = p.block(p.b, p.flip(j), p.y, p.c)
        self.from_y[j] = self.send(index, p.y_peer())
        self.from_x[j] = self.send(index, p.x_peer())
        self.twin.append(self.send(index, p.sibling()))

    def corner(self, j):
        p = self.place
        at = p.flip(j)
        self.from_y[j].wait_recv()
        got = p.block(p.b, at, 1 - p.y, p.c)
        down = self.send(got, p.x_peer(), self.first, self.cut)
        self.diag[j] = [down]
        self.twin.append(self.send(got, p.sibling()))
        self.from_x[j].wait_recv()
        got = p.block(1 - p.b, at, p.y, p.c)
        if self.cut < self.last:
            self.diag[j].append(self.send(got, p.y_peer(), self.cut, self.last))
        self.twin.append(self.send(got, p.sibling()))

    def finish(self, j):
        p = self.place
        for made in self.diag[j]:
            made.wait_recv()
        self.twin.append(self.send(p.block(1 - p.b, p.flip(j), 1 - p.y, p.c), p.sibling()))

    def end(self):
        for made in self.twin:
            made.wait_recv()


class Blocks:
    def __init__(self, length, count):
        self.length, self.count = length, count
        self.stride, self.rest = divmod(length, LANES)
        needed = -(-(length + self.rest * (count - 1)) // LANES)
        self.rows = -(-needed // 16) * 16
        self.tail = self.rows - self.stride
        self.total = length * count

    def spare(self):
        return self.rows * LANES - self.length

    def take(self, block, index):
        return lax.dynamic_slice(block.reshape(-1), (self.rest * index,), (self.length,))


EPS = 1e-06


def root_inverse(rows):
    return lax.rsqrt(jnp.mean(rows * rows, axis=-1, keepdims=True) + EPS)


def turn(rows, cosine, sine):
    half = rows.shape[-1] // 2
    first, second = rows[:, :half], rows[:, half:]
    return jnp.concatenate([first * cosine - second * sine, second * cosine + first * sine], axis=-1)


def turn_back(rows, cosine, sine):
    half = rows.shape[-1] // 2
    first, second = rows[:, :half], rows[:, half:]
    return jnp.concatenate([first * cosine + second * sine, second * cosine - first * sine], axis=-1)


def dot_nn(left, right):
    return jnp.dot(left, right, preferred_element_type=jnp.float32)


def dot_nt(left, right):
    return lax.dot_general(left, right, (((1,), (1,)), ((), ())), preferred_element_type=jnp.float32)


def dot_tn(left, right):
    return lax.dot_general(left, right, (((0,), (0,)), ((), ())), preferred_element_type=jnp.float32)


def align_shard(blocks, place, padded_ref, shifted, aligned):
    offset = blocks.rest * place.mine()
    down, right = lax.div(offset, LANES), lax.rem(offset, LANES)
    rows = blocks.rows
    shifted[0:16] = jnp.zeros((16, LANES), jnp.float32)
    shifted[16 : 16 + rows] = pltpu.roll(padded_ref[...].astype(jnp.float32), right, 1)
    lane = lax.broadcasted_iota(jnp.int32, (rows, LANES), 1)
    aligned[...] = jnp.where(
        lane >= right, shifted[pl.ds(16 - down, rows)], shifted[pl.ds(15 - down, rows)]
    ).astype(aligned.dtype)


def flatten_held(blocks, held, flat):
    stride, tail, rows = blocks.stride, blocks.tail, blocks.rows
    if stride % 16 == 0 and tail == 16:
        flat[0:tail] = held[0, 0:tail].astype(jnp.float32)
        flat[tail:rows] = held[0, tail:rows].astype(jnp.float32)

        def body(d, carry):
            start = pl.multiple_of(d * stride, 16)
            flat[pl.ds(start, tail)] += held[d, 0:tail].astype(jnp.float32)
            start = pl.multiple_of(d * stride + tail, 16)
            flat[pl.ds(start, stride)] = held[d, tail:rows].astype(jnp.float32)
            return carry

        lax.fori_loop(1, blocks.count, body, 0)
    else:
        flat[...] = jnp.zeros_like(flat)

        def body(d, carry):
            flat[pl.ds(d * stride, rows)] += held[d].astype(jnp.float32)
            return carry

        lax.fori_loop(0, blocks.count, body, 0)


def unflatten(flat, base, matrix, first, width):
    height, steps = matrix.shape[0], width // LANES
    for i in range(steps):
        matrix[:, first + i * LANES : first + (i + 1) * LANES] = flat[
            pl.ds(base + i, height, stride=steps), :
        ].astype(matrix.dtype)


def write_gain(flat, base, gain):
    for i in range(gain.shape[1] // LANES):
        flat[base + i : base + i + 1, :] = gain[:, i * LANES : (i + 1) * LANES]


def read_gain(flat, base, width):
    return jnp.concatenate([flat[base + i : base + i + 1, :] for i in range(width // LANES)], axis=-1)


class Halo:
    def __init__(self, place, wires, kv, block, first, size):
        self.place, self.wires, self.kv, self.block = place, wires, kv, block
        self.first, self.size = first, size

    def slot(self, at):
        return self.kv.at[pl.ds(self.first, self.size), pl.ds(pl.multiple_of(at * self.block, 128), self.block)]

    def outward(self):
        p = self.place
        self.outer = self.wires.copy(
            self.slot(4), self.slot(0), p.outer_peer(1), p.hi + 1 < p.outer
        )

    def plane(self):
        p = self.place
        guarded(p.hi > 0, self.outer.wait_recv)
        self.across = self.wires.copy(self.slot(4 * (1 - p.y)), self.slot(2), p.y_peer())
        self.near = self.wires.copy(self.slot(4 * (1 - p.c)), self.slot(3 - 2 * p.c), p.sibling())

    def relay(self):
        p = self.place
        self.across.wait_recv()
        self.far = self.wires.copy(self.slot(2), self.slot(1 + 2 * p.c), p.sibling())

    def end(self):
        self.near.wait_recv()
        self.far.wait_recv()


HALO_WIRES = 4


class Locals:
    def __init__(self, sems):
        self.sems, self.used, self.open = sems, 0, []

    def copy(self, src, dst):
        made = pltpu.make_async_copy(src, dst, self.sems.at[self.used])
        self.used += 1
        self.open.append(made)
        made.start()
        return made

    def finish(self, made):
        made.wait()
        self.open = [other for other in self.open if other is not made]

    def drain(self):
        for made in self.open:
            made.wait()
        self.open = []


class Geo:
    def __init__(self, tokens, attention_params, feed_params):
        self.seqs, self.block = tokens.shape[:2]
        self.rows = self.seqs * self.block
        self.count = lax.axis_size("batch") * lax.axis_size("seq")
        self.outer = lax.axis_size("seq") // 4
        self.attention = Blocks(attention_params.shape[0], self.count)
        self.feed = Blocks(feed_params.shape[0], self.count)
        self.reach = 5 * self.block
        rows = self.attention.rows
        early = (rows - 16) // 32 * 16
        self.attention_bounds = [0, early, rows - 16, rows]
        rows = self.feed.rows
        early = rows - 16
        self.feed_bounds = [0, early // 48 * 16, early // 48 * 32, early, rows]


QUERY = HEADS * HEAD_DIM
BASE_KEY = D * QUERY // LANES
BASE_VALUE = BASE_KEY + D * HEAD_DIM // LANES
BASE_OUT = BASE_VALUE + D * HEAD_DIM // LANES
BASE_GAINS = BASE_OUT + QUERY * D // LANES
STEP = 256
WIDE = 512


def forward_kernel(geo, tokens, positions, frequency, shards, *refs):
    (
        feed_held,
        out_wqkv,
        out_wo,
        out_gains,
        out_q,
        out_kv,
        out_merged,
        out_projected,
        out_hidden,
        out_cosine,
        out_sine,
    ) = refs[:11]
    (
        held,
        own_feed,
        shifted,
        flat,
        wqkv,
        wo,
        gains,
        cosine,
        sine,
        lows,
        normed,
        q,
        kv,
        scores,
        probs,
        merged,
        projected,
        hidden,
        send,
        recv,
        local,
    ) = refs[11:]
    place = Place()
    wires, locals_ = Wires(send, recv), Locals(local)
    seqs, block, reach = geo.seqs, geo.block, geo.reach
    announce(place)
    attention_in = shards.at[pl.ds(0, geo.attention.rows)]
    feed_in = shards.at[pl.ds(geo.attention.rows, geo.feed.rows)]
    align_shard(geo.attention, place, attention_in, shifted, held.at[place.mine()])
    meet(place)
    gather_a = Gather(place, wires, held, 0, geo.attention.rows, 0.5)
    gather_a.begin()
    gather_a.spread(0)
    align_shard(geo.feed, place, feed_in, shifted, own_feed)
    lead = locals_.copy(own_feed, feed_held.at[place.mine()])
    gather_f = Gather(place, wires, feed_held, 0, geo.feed.rows, 1.0)

    @pl.when(place.hi == 0)
    def _():
        kv[:, :block] = jnp.zeros((seqs, block, 2 * HEAD_DIM), jnp.bfloat16)

    columns = positions[...].astype(jnp.float32).T
    row = lax.broadcasted_iota(jnp.int32, (block, LANES), 0)
    for s in range(seqs):
        spot = columns[:, s : s + 1]
        angle = spot * frequency[...]
        rows = slice(s * block, (s + 1) * block)
        cosine[rows] = jnp.cos(angle)
        sine[rows] = jnp.sin(angle)
        lows[s] = jnp.maximum(row + 1, row + WINDOW - spot.astype(jnp.int32))

    locals_.finish(lead)
    gather_f.spread(0)
    for j in range(1, geo.outer):
        gather_a.spread(j)
    gather_f.begin()
    for j in range(geo.outer):
        gather_a.corner(j)
    for j in range(geo.outer):
        gather_a.finish(j)
    gather_f.corner(0)
    gather_a.end()
    pending = [[functools.partial(gather_f.spread, j) for j in range(1, geo.outer)]]
    pending += [[functools.partial(gather_f.corner, j)] for j in range(1, geo.outer)]
    pending += [[functools.partial(gather_f.finish, j)] for j in range(geo.outer)]

    def tick(amount=1):
        for _ in range(amount):
            if pending:
                for action in pending.pop(0):
                    action()

    flatten_held(geo.attention, held, flat)
    at = BASE_GAINS
    for i, width in enumerate((D, HEAD_DIM, HEAD_DIM, D)):
        gains[i : i + 1, :width] = read_gain(flat, at, width)
        at += width // LANES
    unflatten(flat, BASE_KEY, wqkv, QUERY, HEAD_DIM)
    unflatten(flat, BASE_VALUE, wqkv, QUERY + HEAD_DIM, HEAD_DIM)
    gain = gains[0:1, :]
    gain_key = gains[2:3, :HEAD_DIM]
    halos = []
    per_step = STEP // block
    for s in range(0, seqs, per_step):
        rows = slice(s * block, (s + per_step) * block)
        x = tokens[rows].astype(jnp.float32)
        normed[rows] = (x * root_inverse(x) * gain).astype(jnp.bfloat16)
        made = dot_nn(normed[rows], wqkv[:, QUERY:])
        keys = made[:, :HEAD_DIM]
        keys = turn(keys * root_inverse(keys) * gain_key, cosine[rows], sine[rows])
        for i in range(per_step):
            part = slice(i * block, (i + 1) * block)
            kv[s + i, reach - block :, :HEAD_DIM] = keys[part].astype(jnp.bfloat16)
            kv[s + i, reach - block :, HEAD_DIM:] = made[part, HEAD_DIM:].astype(jnp.bfloat16)
        halo = Halo(place, wires, kv, block, s, per_step)
        halo.outward()
        halos.append(halo)
    tick()
    unflatten(flat, 0, wqkv, 0, QUERY)
    gain_query = gains[1:2, :HEAD_DIM] * HEAD_DIM**-0.5
    for s in range(0, seqs, per_step):
        rows = slice(s * block, (s + per_step) * block)
        made = dot_nn(normed[rows], wqkv[:, :QUERY])
        for h in range(HEADS):
            one = made[:, h * HEAD_DIM : (h + 1) * HEAD_DIM]
            one = turn(one * root_inverse(one) * gain_query, cosine[rows], sine[rows])
            q[h, rows] = one.astype(jnp.bfloat16)
    unflatten(flat, BASE_OUT, wo, 0, D)
    for src, dst in (
        (wqkv, out_wqkv),
        (wo, out_wo),
        (gains, out_gains),
        (q, out_q),
        (cosine, out_cosine),
        (sine, out_sine),
    ):
        locals_.copy(src, dst)
    chunk = 32
    lane = lax.broadcasted_iota(jnp.int32, (chunk, reach), 1)
    over = lax.broadcasted_iota(jnp.int32, (chunk, reach), 1) - lax.broadcasted_iota(
        jnp.int32, (chunk, reach), 0
    )

    def attend(s, carry):
        start = pl.multiple_of(s * block, block)
        rows = pl.ds(start, block)
        queries = q[:, rows, :].reshape(HEADS * block, HEAD_DIM)
        scores[...] = dot_nt(queries, kv[s, :, :HEAD_DIM])
        for r in range(0, HEADS * block, chunk):
            i = r % block
            low = jnp.concatenate([lows[s, i : i + chunk, :]] * (reach // LANES), axis=-1)
            seen = (lane >= low) & (over <= WINDOW + i)
            raised = jnp.where(seen, jnp.exp(scores[r : r + chunk]), 0.0)
            share = 1.0 / jnp.sum(raised, axis=-1, keepdims=True)
            probs[r : r + chunk] = (raised * share).astype(jnp.bfloat16)
        made = dot_nn(probs[...], kv[s, :, HEAD_DIM:])
        for h in range(HEADS):
            merged[rows, h * HEAD_DIM : (h + 1) * HEAD_DIM] = made[
                h * block : (h + 1) * block
            ].astype(jnp.bfloat16)
        return carry

    count = len(halos)
    for g in range(count + 2):
        tick()
        if g < count:
            halos[g].plane()
        if 1 <= g <= count:
            halos[g - 1].relay()
        if g > 1:
            tick()
        if g >= 2:
            halos[g - 2].end()
            lax.fori_loop((g - 2) * per_step, (g - 1) * per_step, attend, 0)
    locals_.copy(kv, out_kv)
    locals_.copy(merged, out_merged)
    gain_post = gains[3:4, :]
    for s in range(0, seqs, per_step):
        rows = slice(s * block, (s + per_step) * block)
        made = dot_nn(merged[rows], wo[...])
        projected[rows] = made
        hidden[rows] = tokens[rows].astype(jnp.float32) + made * root_inverse(made) * gain_post
        locals_.copy(projected.at[rows], out_projected.at[rows])
        locals_.copy(hidden.at[rows], out_hidden.at[rows])
    tick(len(pending))
    gather_f.end()
    wires.drain()
    locals_.drain()


def vmem(shape, dtype):
    return pltpu.VMEM(shape, dtype)


def forward_pass(geo, tokens, positions, shards):
    count, rows, seqs, block = geo.count, geo.rows, geo.seqs, geo.block
    bf, f4 = jnp.bfloat16, jnp.float32
    half = HEAD_DIM // 2
    frequency = (
        rope_base ** (-(np.arange(half, dtype=np.float32) * np.float32(2.0) / HEAD_DIM))
    ).astype(np.float32)[None]
    wires = 2 * gather_wires(geo.outer) + geo.seqs // 2 * HALO_WIRES
    outs = [
        ((count, geo.feed.rows, LANES), bf),
        ((D, QUERY + 2 * HEAD_DIM), bf),
        ((QUERY, D), bf),
        ((8, D), f4),
        ((HEADS, rows, HEAD_DIM), bf),
        ((seqs, geo.reach, 2 * HEAD_DIM), bf),
        ((rows, QUERY), bf),
        ((rows, D), f4),
        ((rows, D), f4),
        ((rows, half), f4),
        ((rows, half), f4),
    ]
    flat_rows = geo.attention.count * geo.attention.stride + geo.attention.tail
    return pl.pallas_call(
        functools.partial(forward_kernel, geo),
        out_shape=[jax.ShapeDtypeStruct(*out) for out in outs],
        in_specs=[pl.BlockSpec(memory_space=pltpu.VMEM)] * 4,
        out_specs=[pl.BlockSpec(memory_space=pl.ANY)] * len(outs),
        scratch_shapes=[
            vmem((count, geo.attention.rows, LANES), bf),
            vmem((geo.feed.rows, LANES), bf),
            vmem((16 + geo.feed.rows, LANES), f4),
            vmem((flat_rows, LANES), f4),
            vmem((D, QUERY + 2 * HEAD_DIM), bf),
            vmem((QUERY, D), bf),
            vmem((8, D), f4),
            vmem((rows, half), f4),
            vmem((rows, half), f4),
            vmem((seqs, block, LANES), jnp.int32),
            vmem((rows, D), bf),
            vmem((HEADS, rows, HEAD_DIM), bf),
            vmem((seqs, geo.reach, 2 * HEAD_DIM), bf),
            vmem((HEADS * block, geo.reach), f4),
            vmem((HEADS * block, geo.reach), bf),
            vmem((rows, QUERY), bf),
            vmem((rows, D), f4),
            vmem((rows, D), f4),
            pltpu.SemaphoreType.DMA((wires,)),
            pltpu.SemaphoreType.DMA((wires,)),
            pltpu.SemaphoreType.DMA((32,)),
        ],
        compiler_params=pltpu.CompilerParams(
            collective_id=0, has_side_effects=True, vmem_limit_bytes=60 << 20
        ),
    )(tokens.reshape(rows, D), positions, jnp.asarray(frequency), shards)


MATRIX = D * FF // LANES
BEND = 0.044715
SLOPE = math.sqrt(2.0 / math.pi)


def feed_pieces(blocks, which):
    base, stop = which * MATRIX, (which + 1) * MATRIX
    if which == 2:
        stop = blocks.count * blocks.stride + blocks.tail
    found = []
    for d in range(blocks.count):
        low = max(d * blocks.stride, base)
        high = min(d * blocks.stride + blocks.rows, stop)
        if low < high:
            found.append((d, low - base, high - base, base - d * blocks.stride))
    return found


def feed_phase(geo, locals_, held_in, cotangent_in, mixed_out, split, grad, begin, tick, *refs):
    (flat, twin, down, act, pair, feed_in, turned_in, grad_down) = refs
    mixed = cotangent = feed_in
    blocks = geo.feed
    ends = [-(-(-(-(m + 1) * MATRIX // blocks.stride)) // 4) for m in range(3)]
    starts = [0] + ends[:-1]
    loads = [
        locals_.copy(held_in.at[pl.ds(a, b - a)], split.at[pl.ds(a, b - a)])
        for a, b in zip(starts, ends)
    ]
    load_cotangent = locals_.copy(cotangent_in, grad_down)

    def index(d):
        return d // 4, d // 2 % 2, d % 2

    def unpack(which):
        for d, low, high, shift in feed_pieces(blocks, which):
            mid = min(high, max(low, d * blocks.stride - which * MATRIX + blocks.tail))
            if d and low < mid:
                flat[low:mid] += split[*index(d), low + shift : mid + shift].astype(jnp.float32)
            else:
                mid = low
            flat[mid:high] = split[*index(d), mid + shift : high + shift].astype(jnp.float32)

    def pack(which):
        for d, low, high, shift in feed_pieces(blocks, which):
            split[*index(d), low + shift : high + shift] = flat[low:high].astype(jnp.bfloat16)

    for which, (matrix, first, width) in enumerate(
        ((twin, 0, FF), (twin, FF, FF), (down, 0, D))
    ):
        locals_.finish(loads[which])
        unpack(which)
        unflatten(flat, 0, matrix, first, width)
    gain_feed = read_gain(flat, MATRIX, D)
    gain_out = read_gain(flat, MATRIX + D // LANES, D)

    total, step = geo.rows, WIDE
    spans = [slice(r, r + STEP) for r in range(0, total, STEP)]
    for rows in spans:
        h = grad[rows]
        feed_in[rows] = (h * root_inverse(h) * gain_feed).astype(jnp.bfloat16)

    def rise(i, carry):
        columns = pl.ds(pl.multiple_of(i * step, step), step)
        others = pl.ds(pl.multiple_of(FF + i * step, step), step)
        for rows in spans:
            g = dot_nn(feed_in[rows], twin[:, columns])
            u = dot_nn(feed_in[rows], twin[:, others])
            square = g * g
            t = jnp.tanh(g * (SLOPE + SLOPE * BEND * square))
            half = 0.5 + 0.5 * t
            soft = g * half
            act[rows, columns] = (soft * u).astype(jnp.bfloat16)
            pair[rows, others] = soft.astype(jnp.bfloat16)
            slope = half * (1.0 + g * (1.0 - t) * (SLOPE + 3.0 * SLOPE * BEND * square))
            pair[rows, columns] = (u * slope).astype(jnp.bfloat16)
        return carry

    lax.fori_loop(0, FF // step, rise, 0)
    turned_in[...] = feed_in[...].T

    def settle(i, sum_out):
        rows = pl.ds(pl.multiple_of(i * STEP, STEP), STEP)
        made = dot_nn(act[rows], down[...])
        r = root_inverse(made)
        mixed[rows] = (grad[rows] + made * r * gain_out).astype(jnp.bfloat16)
        e = grad_down[rows].astype(jnp.float32)
        unit = made * r
        sum_out = sum_out + jnp.sum(e * unit, axis=0, keepdims=True)
        c = e * gain_out
        grad_down[rows] = (
            r * (c - unit * jnp.mean(unit * c, axis=-1, keepdims=True))
        ).astype(jnp.bfloat16)
        return sum_out

    locals_.finish(load_cotangent)
    sum_out = lax.fori_loop(0, total // STEP, settle, jnp.zeros((1, D), jnp.float32))
    store_mixed = locals_.copy(mixed, mixed_out)

    def fall(i, carry):
        columns = pl.ds(pl.multiple_of(i * step, step), step)
        others = pl.ds(pl.multiple_of(FF + i * step, step), step)
        for rows in spans:
            made = dot_nt(grad_down[rows], down[columns, :])
            for at in (columns, others):
                pair[rows, at] = (made * pair[rows, at].astype(jnp.float32)).astype(jnp.bfloat16)
        return carry

    lax.fori_loop(0, FF // step, fall, 0)

    def back(i, sum_feed):
        rows = pl.ds(pl.multiple_of(i * STEP, STEP), STEP)
        made = dot_nt(pair[rows], twin[...])
        h = grad[rows]
        r = root_inverse(h)
        unit = h * r
        sum_feed = sum_feed + jnp.sum(made * unit, axis=0, keepdims=True)
        c = made * gain_feed
        grad[rows] = cotangent[rows].astype(jnp.float32) + r * (
            c - unit * jnp.mean(unit * c, axis=-1, keepdims=True)
        )
        return sum_feed

    def wide(i, carry, first):
        made = dot_nn(turned_in[...], pair[:, pl.ds(pl.multiple_of(first + i * step, step), step)])
        for k in range(step // LANES):
            flat[pl.ds(i * (step // LANES) + k, D, stride=FF // LANES), :] = made[
                :, k * LANES : (k + 1) * LANES
            ]
        return carry

    locals_.finish(store_mixed)
    load_cotangent = locals_.copy(cotangent_in, cotangent)
    lax.fori_loop(0, FF // step, functools.partial(wide, first=0), 0)
    pack(0)
    lax.fori_loop(0, FF // step, functools.partial(wide, first=FF), 0)
    pack(1)

    def tall(i, carry):
        columns = pl.ds(pl.multiple_of(i * step, step), step)
        made = dot_tn(act[:, columns], grad_down[...])
        for k in range(D // LANES):
            flat[pl.ds(i * (step * D // LANES) + k, step, stride=D // LANES), :] = made[
                :, k * LANES : (k + 1) * LANES
            ]
        return carry

    lax.fori_loop(0, FF // step, tall, 0)
    flat[MATRIX:] = jnp.zeros_like(flat[MATRIX:])
    pack(2)
    begin()
    locals_.finish(load_cotangent)
    sum_feed = jnp.zeros((1, D), jnp.float32)
    for i in range(0, total // STEP, 2):
        sum_feed = lax.fori_loop(i, i + 2, back, sum_feed)
        tick()
    write_gain(flat, MATRIX, sum_feed)
    write_gain(flat, MATRIX + D // LANES, sum_out)
    last = blocks.count - 1
    low = blocks.count * blocks.stride - 2 * MATRIX
    split[*index(last), blocks.stride :] = flat[low:].astype(jnp.bfloat16)


class Scatter:
    def __init__(self, place, wires, other, own, lands, result, piece):
        self.place, self.wires, self.other, self.own, self.result = place, wires, other, own, result
        self.by_core, self.first_x, self.first_y, self.second_x, self.second_y, self.by_outer = lands
        first, cut, last, at_x, at_y = piece
        self.split = cut < last
        self.all = pl.ds(first, last - first)
        self.rows_x, self.rows_y = pl.ds(first, cut - first), pl.ds(cut, last - cut)
        self.land_x, self.land_y = pl.ds(at_x, cut - first), pl.ds(at_y, last - cut)
        p, plan = place, wires.plan
        mine, theirs = self.column_of(p.b), self.column_of(1 - p.b)
        self.from_core = plan(
            other.at[:, :, 1 - p.c, self.all], self.by_core.at[:, :, self.all], p.sibling()
        )
        self.from_x = plan(
            own.at[theirs, :, self.rows_x], self.first_x.at[:, :, self.land_x], p.x_peer()
        )
        self.over_y = plan(
            own.at[mine, 1 - p.y, self.rows_x], self.second_y.at[:, self.land_x], p.y_peer()
        )
        if self.split:
            self.from_y = plan(
                own.at[:, 1 - p.y, self.rows_y], self.first_y.at[:, self.land_y], p.y_peer()
            )
            self.over_x = plan(
                own.at[theirs, p.y, self.rows_y], self.second_x.at[:, self.land_y], p.x_peer()
            )
        self.from_outer = [
            plan(
                own.at[p.b * p.outer + p.flip(k), p.y, self.all],
                self.by_outer.at[k - 1, self.all],
                p.flip_peer(k),
            )
            for k in range(1, p.outer)
        ]

    def add(self, i, y, rows, land):
        self.own[i, y, rows] = (
            self.own[i, y, rows].astype(jnp.float32) + land.astype(jnp.float32)
        ).astype(jnp.bfloat16)

    def column_of(self, b):
        return pl.ds(b * self.place.outer, self.place.outer)

    def core(self):
        self.from_core.start()

    def plane(self):
        p = self.place
        self.from_core.wait_recv()

        def body(i, carry):
            for y in range(2):
                self.add(i, y, self.all, self.by_core[i, y, self.all])
            return carry

        lax.fori_loop(0, 2 * p.outer, body, 0)
        self.from_x.start()
        if self.split:
            self.from_y.start()

    def cross(self):
        p = self.place
        self.from_x.wait_recv()

        def body(hi, carry):
            for y in range(2):
                self.add(p.b * p.outer + hi, y, self.rows_x, self.first_x[hi, y, self.land_x])
            return carry

        lax.fori_loop(0, p.outer, body, 0)
        self.over_y.start()
        if self.split:
            self.from_y.wait_recv()

            def body(i, carry):
                self.add(i, p.y, self.rows_y, self.first_y[i, self.land_y])
                return carry

            lax.fori_loop(0, 2 * p.outer, body, 0)
            self.over_x.start()

    def column(self):
        p = self.place
        self.over_y.wait_recv()
        if self.split:
            self.over_x.wait_recv()

        def body(hi, carry):
            i = p.b * p.outer + hi
            self.add(i, p.y, self.rows_x, self.second_y[hi, self.land_x])
            if self.split:
                self.add(i, p.y, self.rows_y, self.second_x[hi, self.land_y])
            return carry

        lax.fori_loop(0, p.outer, body, 0)
        for made in self.from_outer:
            made.start()

    def end(self):
        p = self.place
        total = self.own[p.b * p.outer + p.hi, p.y, self.all].astype(jnp.float32)
        for k, made in enumerate(self.from_outer):
            made.wait_recv()
            total = total + self.by_outer[k, self.all].astype(jnp.float32)
        self.result[self.all] = total


def scatter_wires(outer):
    return 5 + outer - 1


def cut_pieces(bounds, shares):
    pieces, at_x, at_y = [], 0, 0
    for first, last, share in zip(bounds, bounds[1:], shares):
        cut = first + max(16, int((last - first) * share) // 16 * 16)
        pieces.append((first, cut, last, at_x, at_y))
        at_x, at_y = at_x + cut - first, at_y + last - cut
    return pieces, at_x, at_y


def land_shapes(rows, bounds, shares, outer):
    rows_x, rows_y = cut_pieces(bounds, shares)[1:]
    return [
        pltpu.VMEM(shape + (LANES,), jnp.bfloat16)
        for shape in (
            (2 * outer, 2, rows),
            (outer, 2, rows_x),
            (2 * outer, rows_y),
            (outer, rows_y),
            (outer, rows_x),
            (outer - 1, rows),
        )
    ]


class Return:
    def __init__(self, place, wires, kv, own, by_core, by_y, by_outer, block, first, size):
        self.place, self.wires, self.kv, self.own, self.block = place, wires, kv, own, block
        self.by_core, self.by_y, self.by_outer = by_core, by_y, by_outer
        self.group = pl.ds(first, size)
        self.each = range(first, first + size)

    def rows(self, at):
        return slice(at * self.block, (at + 1) * self.block)

    def slot(self, at):
        return self.kv.at[self.group, pl.ds(at * self.block, self.block)]

    def core(self):
        p = self.place
        self.from_core = [
            self.wires.copy(
                self.slot(at), self.by_core.at[self.group, pl.ds(i * self.block, self.block)], p.sibling()
            )
            for i, at in enumerate((1, 3))
        ]

    def grow(self, s, at, extra):
        rows = self.rows(at)
        self.kv[s, rows] = (self.kv[s, rows].astype(jnp.float32) + extra).astype(jnp.bfloat16)

    def plane(self):
        p = self.place
        for made in self.from_core:
            made.wait_recv()
        for s in self.each:

            @pl.when(p.c == 0)
            def _():
                self.grow(s, 2, self.by_core[s, self.rows(0)].astype(jnp.float32))
                self.own[s] += self.by_core[s, self.rows(1)].astype(jnp.float32)

            @pl.when(p.c == 1)
            def _():
                self.grow(s, 0, self.by_core[s, self.rows(0)].astype(jnp.float32))
                self.grow(s, 2, self.by_core[s, self.rows(1)].astype(jnp.float32))

        self.from_y = self.wires.copy(self.slot(2), self.by_y.at[self.group], p.y_peer())

    def outward(self):
        p = self.place
        self.from_y.wait_recv()
        for s in self.each:

            @pl.when(p.y == 0)
            def _():
                self.own[s] += self.by_y[s].astype(jnp.float32)

            @pl.when(p.y == 1)
            def _():
                self.grow(s, 0, self.by_y[s].astype(jnp.float32))

        self.from_outer = self.wires.copy(
            self.slot(0), self.by_outer.at[self.group], p.outer_peer(p.outer - 1), p.hi > 0
        )

    def end(self):
        p = self.place

        @pl.when(p.hi + 1 < p.outer)
        def _():
            self.from_outer.wait_recv()
            for s in self.each:
                self.own[s] += self.by_outer[s].astype(jnp.float32)


RETURN_WIRES = 4
FEED_SHARES = (0.5, 1.0, 1.0, 1.0)
ATTENTION_SHARES = (0.5, 0.5, 1.0)


def fill_blocks(blocks, split, flat, margin, base, stop):
    even = blocks.stride % 16 == 0
    for d in range(blocks.count):
        low, high = max(d * blocks.stride, base), min(d * blocks.stride + blocks.rows, stop)
        if low >= high:
            continue
        i, y, c = d // 4, d // 2 % 2, d % 2
        first, last = low - d * blocks.stride, high - d * blocks.stride
        if even:
            split[i, y, c, first:last] = flat[low - base + margin : high - base + margin].astype(
                jnp.bfloat16
            )
        else:
            start, end = first // 16 * 16, -(-last // 16) * 16
            source = low - base + margin - (first - start)
            split[i, y, c, start:end] = (
                split[i, y, c, start:end].astype(jnp.float32)
                + flat[source : source + end - start]
            ).astype(jnp.bfloat16)


MARGIN = 16


def backward_kernel(
    geo, positions, gains, tokens_in, wqkv_in, wo_in, q_in, kv_in, merged_in, projected_in,
    hidden_in, cosine_in, sine_in, held_in, cotangent_in, *refs
):
    grad_tokens, mixed_out, attention_sum, feed_sum = refs[:4]
    grad, split_f, split_a, by_core_kv, by_y_kv, by_outer_kv = refs[4:10]
    lands_a, lands_f = refs[10:16], refs[16:22]
    send, recv, local = refs[22:]
    place = Place()
    wires, locals_ = Wires(send, recv), Locals(local)
    bf, f4, rows, half = jnp.bfloat16, jnp.float32, geo.rows, HEAD_DIM // 2
    load_hidden = locals_.copy(hidden_in, grad)
    announce(place)
    pieces = cut_pieces(geo.feed_bounds, FEED_SHARES)[0]
    own_f = split_f.at[:, :, place.c]
    one, two, three, four = [
        Scatter(place, wires, split_f, own_f, lands_f, feed_sum, piece) for piece in pieces
    ]

    def begin():
        meet(place)
        for part in (one, two, three):
            part.core()

    pending = [
        [one.plane], [two.plane],
        [],
        [one.cross], [three.plane], [], [one.column],
        [two.cross],
        [four.plane],
        [two.column, three.cross, one.end],
        [four.cross, three.column],
        [two.end, four.column, three.end, four.end],
    ]

    def tick():
        for action in pending.pop(0):
            action()

    locals_.finish(load_hidden)
    pl.run_scoped(
        functools.partial(
            feed_phase, geo, locals_, held_in, cotangent_in, mixed_out, split_f, grad, begin, tick
        ),
        vmem((MATRIX + geo.feed.tail, LANES), f4),
        vmem((D, 2 * FF), bf),
        vmem((FF, D), bf),
        vmem((rows, FF), bf),
        vmem((rows, 2 * FF), bf),
        vmem((rows, D), bf),
        vmem((D, rows), bf),
        vmem((rows, D), bf),
    )
    four.core()
    pl.run_scoped(
        functools.partial(
            attention_phase, geo, place, wires, locals_, positions, gains,
            (tokens_in, wqkv_in, wo_in, q_in, kv_in, merged_in, projected_in, cosine_in, sine_in),
            grad_tokens, attention_sum, grad, split_a, by_core_kv, by_y_kv, by_outer_kv, lands_a,
            pending, tick,
        ),
        vmem((rows, D), bf),
        vmem(wqkv_in.shape, bf),
        vmem(wo_in.shape, bf),
        vmem(q_in.shape, bf),
        vmem(kv_in.shape, bf),
        vmem((rows, QUERY + 2 * HEAD_DIM), bf),
        vmem((rows, half), f4),
        vmem((rows, half), f4),
        vmem((2 * geo.reach, D), f4),
        vmem((rows, D), bf),
        vmem((max(D, geo.reach), max(rows, 2 * HEADS * geo.block)), bf),
        vmem((HEADS, rows, HEAD_DIM), bf),
        vmem((rows, D), bf),
        vmem((geo.seqs, geo.block, 2 * HEAD_DIM), f4),
        vmem((2 * MARGIN + QUERY * D // LANES, LANES), f4),
    )


def attention_phase(
    geo, place, wires, locals_, positions, gains, saved, grad_tokens, attention_sum, grad,
    split, by_core_kv, by_y_kv, by_outer_kv, lands_a, pending, tick, *refs
):
    tokens_in, wqkv_in, wo_in, q_in, kv_in, merged_in, projected_in, cosine_in, sine_in = saved
    (
        tokens, wqkv, wo, q, kv, pair, cosine, sine, work, normed, shared, grad_out, out_rows,
        own_kv, flat,
    ) = refs
    seqs, block, reach, total, step = geo.seqs, geo.block, geo.reach, geo.rows, STEP
    turned = shared.at[pl.ds(0, D), pl.ds(0, total)]
    probs = shared.at[pl.ds(0, reach), pl.ds(0, HEADS * block)]
    logits = shared.at[pl.ds(0, reach), pl.ds(HEADS * block, HEADS * block)]
    projected = work.at[pl.ds(0, total)]
    scores = work.at[pl.ds(0, reach), pl.ds(0, HEADS * block)]
    slopes = work.at[pl.ds(reach, reach), pl.ds(0, HEADS * block)]
    load_projected = locals_.copy(projected_in, projected)
    load_wo = locals_.copy(wo_in, wo)
    load_tokens = locals_.copy(tokens_in, tokens)
    load_merged = locals_.copy(merged_in, pair.at[:, pl.ds(0, QUERY)])
    load_q, load_kv = locals_.copy(q_in, q), locals_.copy(kv_in, kv)
    load_rest = [
        locals_.copy(wqkv_in, wqkv), locals_.copy(cosine_in, cosine), locals_.copy(sine_in, sine)
    ]
    gain_attention, gain_query = gains[0:1, :], gains[1:2, :HEAD_DIM]
    gain_key, gain_post = gains[2:3, :HEAD_DIM], gains[3:4, :]
    for made in (load_projected, load_wo, load_tokens):
        locals_.finish(made)

    def start_rows(i, summed):
        rows = pl.ds(pl.multiple_of(i * step, step), step)
        made, e = projected[rows], grad[rows]
        r = root_inverse(made)
        unit = made * r
        c = e * gain_post
        out_rows[rows] = (r * (c - unit * jnp.mean(unit * c, axis=-1, keepdims=True))).astype(
            jnp.bfloat16
        )
        x = tokens[rows].astype(jnp.float32)
        normed[rows] = (x * root_inverse(x) * gain_attention).astype(jnp.bfloat16)
        for h in range(HEADS):
            grad_out[h, rows] = dot_nt(
                out_rows[rows], wo[h * HEAD_DIM : (h + 1) * HEAD_DIM, :]
            ).astype(jnp.bfloat16)
        return summed + jnp.sum(e * unit, axis=0, keepdims=True)

    sum_post = lax.fori_loop(0, total // step, start_rows, jnp.zeros((1, D), jnp.float32))
    tick()
    blocks = geo.attention
    flat[0:MARGIN] = jnp.zeros((MARGIN, LANES), jnp.float32)
    flat[MARGIN + QUERY * D // LANES :] = jnp.zeros((MARGIN, LANES), jnp.float32)
    if blocks.stride % 16:
        split[...] = jnp.zeros_like(split)
    locals_.finish(load_merged)

    for made in [load_q, load_kv] + load_rest:
        locals_.finish(made)

    wide = HEADS * block
    chunk = 32
    lane = lax.rem(lax.broadcasted_iota(jnp.int32, (chunk, wide), 1), block)
    line = lax.broadcasted_iota(jnp.int32, (chunk, wide), 0)

    def attend(s, carry):
        rows = pl.ds(pl.multiple_of(s * block, block), block)
        queries = q[:, rows, :].reshape(wide, HEAD_DIM)
        given = grad_out[:, rows, :].reshape(wide, HEAD_DIM)
        scores[...] = dot_nt(kv[s, :, :HEAD_DIM], queries)
        slopes[...] = dot_nt(kv[s, :, HEAD_DIM:], given)
        spot = jnp.concatenate([positions[pl.ds(s, 1), :]] * HEADS, axis=-1)
        low = jnp.maximum(lane[0:1] + 1, lane[0:1] + WINDOW - spot)
        total_e = jnp.zeros((8, wide), jnp.float32)
        total_d = jnp.zeros((8, wide), jnp.float32)
        for r in range(0, reach, chunk):
            seen = (line + r >= low) & (line + (r - WINDOW) <= lane)
            raised = jnp.where(seen, jnp.exp(scores[r : r + chunk]), 0.0)
            scores[r : r + chunk] = raised
            moved = raised * slopes[r : r + chunk]
            for k in range(0, chunk, 8):
                total_e = total_e + raised[k : k + 8]
                total_d = total_d + moved[k : k + 8]
        share = 1.0 / jnp.sum(total_e, axis=0, keepdims=True)
        inner = jnp.sum(total_d, axis=0, keepdims=True) * share
        for r in range(0, reach, chunk):
            p = scores[r : r + chunk] * share
            probs[r : r + chunk] = p.astype(jnp.bfloat16)
            logits[r : r + chunk] = (p * (slopes[r : r + chunk] - inner)).astype(jnp.bfloat16)
        grad_q = dot_tn(logits[...], kv[s, :, :HEAD_DIM]) * HEAD_DIM**-0.5
        grad_k = dot_nn(logits[...], queries)
        grad_v = dot_nn(probs[...], given)
        early = reach - block
        kv[s, :early, :HEAD_DIM] = grad_k[:early].astype(jnp.bfloat16)
        kv[s, :early, HEAD_DIM:] = grad_v[:early].astype(jnp.bfloat16)
        own_kv[s, :, :HEAD_DIM] = grad_k[early:]
        own_kv[s, :, HEAD_DIM:] = grad_v[early:]
        for h in range(HEADS):
            q[h, rows] = grad_q[h * block : (h + 1) * block].astype(jnp.bfloat16)
        return carry

    size = 1
    returns = [
        Return(place, wires, kv, own_kv, by_core_kv, by_y_kv, by_outer_kv, block, s, size)
        for s in range(0, seqs, size)
    ]
    for g, group in enumerate(returns):
        lax.fori_loop(g * size, (g + 1) * size, attend, 0)
        group.core()
        if g >= 1:
            returns[g - 1].plane()
        if g >= 2:
            returns[g - 2].outward()
        if g % 2:
            tick()
    last = len(returns) - 1
    turned[...] = normed[...].T

    def tall(i, carry):
        columns = pl.ds(pl.multiple_of(i * step, step), step)
        made = dot_tn(pair[:, columns], out_rows[...])
        for k in range(D // LANES):
            flat[pl.ds(MARGIN + i * (step * D // LANES) + k, step, stride=D // LANES), :] = made[
                :, k * LANES : (k + 1) * LANES
            ]
        return carry

    lax.fori_loop(0, QUERY // step, tall, 0)
    fill_blocks(blocks, split, flat, MARGIN, BASE_OUT, BASE_GAINS)
    def query_rows(i, summed):
        rows = pl.ds(pl.multiple_of(i * step, step), step)
        made = dot_nn(normed[rows], wqkv[:, :QUERY])
        for h in range(HEADS):
            raw = made[:, h * HEAD_DIM : (h + 1) * HEAD_DIM]
            e = turn_back(q[h, rows].astype(jnp.float32), cosine[rows], sine[rows])
            r = root_inverse(raw)
            unit = raw * r
            summed = summed + jnp.sum(e * unit, axis=0, keepdims=True)
            c = e * gain_query
            pair[rows, h * HEAD_DIM : (h + 1) * HEAD_DIM] = (
                r * (c - unit * jnp.mean(unit * c, axis=-1, keepdims=True))
            ).astype(jnp.bfloat16)
        return summed

    returns[last].plane()
    returns[last - 1].outward()
    tick()
    sum_query = lax.fori_loop(0, total // step, query_rows, jnp.zeros((1, HEAD_DIM), jnp.float32))
    returns[last].outward()
    tick()

    def broad(i, carry, first, width):
        columns = pl.ds(pl.multiple_of(first + i * step, step), step)
        made = dot_nn(turned[...], pair[:, columns])
        for k in range(step // LANES):
            start = MARGIN + i * (step // LANES) + k
            flat[pl.ds(start, D, stride=width // LANES), :] = made[:, k * LANES : (k + 1) * LANES]
        return carry

    lax.fori_loop(0, QUERY // step, functools.partial(broad, first=0, width=QUERY), 0)
    fill_blocks(blocks, split, flat, MARGIN, 0, BASE_KEY)
    tick()
    for group in returns:
        group.end()

    def key_rows(i, summed):
        rows = pl.ds(pl.multiple_of(i * step, step), step)
        per = step // block
        raw = dot_nn(normed[rows], wqkv[:, QUERY : QUERY + HEAD_DIM])
        both = own_kv[pl.ds(i * per, per)].reshape(step, 2 * HEAD_DIM)
        e = turn_back(both[:, :HEAD_DIM], cosine[rows], sine[rows])
        r = root_inverse(raw)
        unit = raw * r
        c = e * gain_key
        pair[rows, QUERY : QUERY + HEAD_DIM] = (
            r * (c - unit * jnp.mean(unit * c, axis=-1, keepdims=True))
        ).astype(jnp.bfloat16)
        pair[rows, QUERY + HEAD_DIM :] = both[:, HEAD_DIM:].astype(jnp.bfloat16)
        return summed + jnp.sum(e * unit, axis=0, keepdims=True)

    sum_key = lax.fori_loop(0, total // step, key_rows, jnp.zeros((1, HEAD_DIM), jnp.float32))
    for first, base in ((QUERY, BASE_KEY), (QUERY + HEAD_DIM, BASE_VALUE)):
        broad(0, 0, first, HEAD_DIM)
        size_rows = D * HEAD_DIM // LANES
        flat[MARGIN + size_rows : 2 * MARGIN + size_rows] = jnp.zeros((MARGIN, LANES), jnp.float32)
        fill_blocks(blocks, split, flat, MARGIN, base, base + size_rows)

    def end_rows(i, summed):
        rows = pl.ds(pl.multiple_of(i * step, step), step)
        made = dot_nt(pair[rows], wqkv[...])
        x = tokens[rows].astype(jnp.float32)
        r = root_inverse(x)
        unit = x * r
        c = made * gain_attention
        grad[rows] = grad[rows] + r * (c - unit * jnp.mean(unit * c, axis=-1, keepdims=True))
        return summed + jnp.sum(made * unit, axis=0, keepdims=True)

    tail = geo.attention.tail
    own = split.at[:, :, place.c]
    one, two, three = [
        Scatter(place, wires, split, own, lands_a, attention_sum, piece)
        for piece in cut_pieces(geo.attention_bounds, ATTENTION_SHARES)[0]
    ]
    one.core()
    two.core()
    tick()
    sum_attention = jnp.zeros((1, D), jnp.float32)
    half = total // step // 2
    one.plane()
    sum_attention = lax.fori_loop(0, half, end_rows, sum_attention)
    two.plane()
    sum_attention = lax.fori_loop(half, 2 * half, end_rows, sum_attention)
    locals_.copy(grad, grad_tokens)
    tick()
    flat[MARGIN : 2 * MARGIN + tail] = jnp.zeros((MARGIN + tail, LANES), jnp.float32)
    at = MARGIN
    for made in (sum_attention, sum_query, sum_key, sum_post):
        write_gain(flat, at, made)
        at += made.shape[1] // LANES
    fill_blocks(blocks, split, flat, MARGIN, BASE_GAINS, blocks.count * blocks.stride + tail)
    three.core()
    for action in (
        one.cross, three.plane, two.cross, one.column, three.cross, two.column, three.column,
        one.end, two.end, three.end,
    ):
        action()
    wires.drain()
    locals_.drain()


def backward_pass(geo, tokens, positions, saved, hidden, feed_held, cotangent):
    bf, f4, rows, seqs, block = jnp.bfloat16, jnp.float32, geo.rows, geo.seqs, geo.block
    wqkv, wo, gains, q, kv, merged, projected, cosine, sine = saved
    rows_a, rows_f, outer = geo.attention.rows, geo.feed.rows, geo.outer
    outs = [((rows, D), f4), ((rows, D), bf), ((rows_a, LANES), f4), ((rows_f, LANES), f4)]
    full, hbm = pl.BlockSpec(memory_space=pltpu.VMEM), pl.BlockSpec(memory_space=pl.ANY)
    wires = (len(geo.feed_bounds) + len(geo.attention_bounds) - 2) * scatter_wires(
        outer
    ) + seqs * RETURN_WIRES
    return pl.pallas_call(
        functools.partial(backward_kernel, geo),
        out_shape=[jax.ShapeDtypeStruct(*out) for out in outs],
        in_specs=[full] * 2 + [hbm] * 12,
        out_specs=[hbm, hbm, full, full],
        scratch_shapes=[
            vmem((rows, D), f4),
            vmem((2 * outer, 2, 2, rows_f, LANES), bf),
            vmem((2 * outer, 2, 2, rows_a, LANES), bf),
            vmem((seqs, 2 * block, 2 * HEAD_DIM), bf),
            vmem((seqs, block, 2 * HEAD_DIM), bf),
            vmem((seqs, block, 2 * HEAD_DIM), bf),
        ]
        + land_shapes(rows_a, geo.attention_bounds, ATTENTION_SHARES, outer)
        + land_shapes(rows_f, geo.feed_bounds, FEED_SHARES, outer)
        + [
            pltpu.SemaphoreType.DMA((wires,)),
            pltpu.SemaphoreType.DMA((wires,)),
            pltpu.SemaphoreType.DMA((32,)),
        ],
        compiler_params=pltpu.CompilerParams(
            collective_id=1, has_side_effects=True, vmem_limit_bytes=63 << 20
        ),
    )(
        positions, gains, tokens.reshape(rows, D), wqkv, wo, q, kv, merged, projected, hidden,
        cosine, sine, feed_held.reshape(2 * outer, 2, 2, rows_f, LANES), cotangent.reshape(rows, D),
    )


def on_device(tokens, attention_params, feed_params, positions, cotangent):
    geo = Geo(tokens, attention_params, feed_params)
    start = geo.attention.rows * LANES
    after = geo.feed.spare()
    shards = (
        jnp.pad(attention_params, (0, geo.attention.spare() + geo.feed.rows * LANES))
        + jnp.pad(feed_params, (start, after))
    ).reshape(-1, LANES)
    device = lax.axis_index("batch") * lax.axis_size("seq") + lax.axis_index("seq")
    (
        feed_held, wqkv, weight_out, gains, q, kv, merged, projected, hidden, cosine, sine,
    ) = forward_pass(geo, tokens, positions, shards)
    grad_tokens, mixed, attention_sum, feed_sum = backward_pass(
        geo,
        tokens,
        positions,
        (wqkv, weight_out, gains, q, kv, merged, projected, cosine, sine),
        hidden,
        feed_held,
        cotangent,
    )
    return (
        mixed.reshape(tokens.shape),
        grad_tokens.reshape(tokens.shape),
        geo.attention.take(attention_sum, device),
        geo.feed.take(feed_sum, device),
    )


def solution(mesh):
    return jax.shard_map(
        on_device,
        mesh=mesh,
        in_specs=(
            P("batch", "seq", None),
            P(("batch", "seq")),
            P(("batch", "seq")),
            P("batch", "seq"),
            P("batch", "seq", None),
        ),
        out_specs=(
            P("batch", "seq", None),
            P("batch", "seq", None),
            P(("batch", "seq")),
            P(("batch", "seq")),
        ),
        check_vma=False,
    )
```

```python
import functools
import math

import jax
import jax.numpy as jnp
import numpy as np
from jax import lax
from jax.experimental import pallas as pl
from jax.experimental.pallas import tpu as pltpu
from jax.sharding import PartitionSpec as P

MESH = pl.DeviceIdType.MESH
LANES = 128

D = 640
HEADS = 4
HEAD_DIM = 256
FF = 2048
WINDOW = 512


rope_base = 10000.0


class Place:
    def __init__(self):
        self.devices_seq = lax.axis_size("seq")
        self.outer = self.devices_seq // 4
        self.count = 2 * self.devices_seq
        self.b = lax.axis_index("batch")
        s = lax.axis_index("seq")
        self.hi = lax.div(s, 4)
        self.y = lax.rem(lax.div(s, 2), 2)
        self.c = lax.rem(s, 2)

    def block(self, b, hi, y, c):
        return b * self.devices_seq + hi * 4 + y * 2 + c

    def seq_id(self, hi, y, c):
        return (self.b, hi * 4 + y * 2 + c)

    def mine(self):
        return self.block(self.b, self.hi, self.y, self.c)

    def x_peer(self):
        return (1 - self.b, self.hi * 4 + self.y * 2 + self.c)

    def y_peer(self):
        return self.seq_id(self.hi, 1 - self.y, self.c)

    def sibling(self):
        return self.seq_id(self.hi, self.y, 1 - self.c)

    def outer_at(self, k):
        return lax.rem(self.hi + k, self.outer)

    def flip(self, k):
        found, bit = 0, 1
        while bit < self.outer:
            own = lax.rem(lax.div(self.hi, bit), 2)
            found = found + bit * ((1 - own) if k & bit else own)
            bit *= 2
        return found

    def flip_peer(self, k):
        return self.seq_id(self.flip(k), self.y, self.c)

    def outer_peer(self, k):
        return self.seq_id(self.outer_at(k), self.y, self.c)

    def peers(self):
        return [self.x_peer(), self.y_peer(), self.sibling()] + [
            self.outer_peer(k) for k in range(1, self.outer)
        ]


def announce(place):
    barrier = pltpu.get_barrier_semaphore()
    for peer in place.peers():
        pl.semaphore_signal(barrier, inc=1, device_id=peer, device_id_type=MESH)


def meet(place):
    pl.semaphore_wait(pltpu.get_barrier_semaphore(), len(place.peers()))


def guarded(when, action):
    if when is None:
        action()
    else:
        pl.when(when)(action)


class Wires:
    def __init__(self, send_sems, recv_sems):
        self.send_sems, self.recv_sems = send_sems, recv_sems
        self.used = 0
        self.sent = []

    def plan(self, src, dst, peer, when=None):
        made = pltpu.make_async_remote_copy(
            src_ref=src,
            dst_ref=dst,
            send_sem=self.send_sems.at[self.used],
            recv_sem=self.recv_sems.at[self.used],
            device_id=peer,
            device_id_type=MESH,
        )
        self.used += 1
        self.sent.append((made, when))
        return made

    def copy(self, src, dst, peer, when=None):
        made = self.plan(src, dst, peer, when)
        guarded(when, made.start)
        return made

    def drain(self):
        for made, when in self.sent:
            guarded(when, made.wait_send)
        self.sent = []


def gather_wires(outer):
    return outer - 1 + 4 * outer + 4 * outer


class Gather:
    def __init__(self, place, wires, held, first, last, share):
        self.place, self.wires, self.held = place, wires, held
        self.first, self.last = first, last
        self.cut = first + int((last - first) * share) // 16 * 16
        self.from_outer = {}
        self.from_x, self.from_y, self.diag, self.twin = {}, {}, {}, []

    def send(self, index, peer, first=None, last=None):
        first = self.first if first is None else first
        last = self.last if last is None else last
        ref = self.held.at[index, pl.ds(first, last - first)]
        return self.wires.copy(ref, ref, peer)

    def begin(self):
        p = self.place
        for k in range(1, p.outer):
            self.from_outer[k] = self.send(p.mine(), p.flip_peer(k))

    def spread(self, j):
        p = self.place
        if j:
            self.from_outer[j].wait_recv()
        index = p.block(p.b, p.flip(j), p.y, p.c)
        self.from_y[j] = self.send(index, p.y_peer())
        self.from_x[j] = self.send(index, p.x_peer())
        self.twin.append(self.send(index, p.sibling()))

    def corner(self, j):
        p = self.place
        at = p.flip(j)
        self.from_y[j].wait_recv()
        got = p.block(p.b, at, 1 - p.y, p.c)
        down = self.send(got, p.x_peer(), self.first, self.cut)
        self.diag[j] = [down]
        self.twin.append(self.send(got, p.sibling()))
        self.from_x[j].wait_recv()
        got = p.block(1 - p.b, at, p.y, p.c)
        if self.cut < self.last:
            self.diag[j].append(self.send(got, p.y_peer(), self.cut, self.last))
        self.twin.append(self.send(got, p.sibling()))

    def finish(self, j):
        p = self.place
        for made in self.diag[j]:
            made.wait_recv()
        self.twin.append(self.send(p.block(1 - p.b, p.flip(j), 1 - p.y, p.c), p.sibling()))

    def end(self):
        for made in self.twin:
            made.wait_recv()


class Blocks:
    def __init__(self, length, count):
        self.length, self.count = length, count
        self.stride, self.rest = divmod(length, LANES)
        needed = -(-(length + self.rest * (count - 1)) // LANES)
        self.rows = -(-needed // 16) * 16
        self.tail = self.rows - self.stride
        self.total = length * count

    def spare(self):
        return self.rows * LANES - self.length

    def take(self, block, index):
        return lax.dynamic_slice(block.reshape(-1), (self.rest * index,), (self.length,))


EPS = 1e-06


def root_inverse(rows):
    return lax.rsqrt(jnp.mean(rows * rows, axis=-1, keepdims=True) + EPS)


def turn(rows, cosine, sine):
    half = rows.shape[-1] // 2
    first, second = rows[:, :half], rows[:, half:]
    return jnp.concatenate([first * cosine - second * sine, second * cosine + first * sine], axis=-1)


def turn_back(rows, cosine, sine):
    half = rows.shape[-1] // 2
    first, second = rows[:, :half], rows[:, half:]
    return jnp.concatenate([first * cosine + second * sine, second * cosine - first * sine], axis=-1)


def dot_nn(left, right):
    return jnp.dot(left, right, preferred_element_type=jnp.float32)


def dot_nt(left, right):
    return lax.dot_general(left, right, (((1,), (1,)), ((), ())), preferred_element_type=jnp.float32)


def dot_tn(left, right):
    return lax.dot_general(left, right, (((0,), (0,)), ((), ())), preferred_element_type=jnp.float32)


def align_shard(blocks, place, padded_ref, shifted, aligned):
    offset = blocks.rest * place.mine()
    down, right = lax.div(offset, LANES), lax.rem(offset, LANES)
    rows = blocks.rows
    shifted[0:16] = jnp.zeros((16, LANES), jnp.float32)
    shifted[16 : 16 + rows] = pltpu.roll(padded_ref[...].astype(jnp.float32), right, 1)
    lane = lax.broadcasted_iota(jnp.int32, (rows, LANES), 1)
    aligned[...] = jnp.where(
        lane >= right, shifted[pl.ds(16 - down, rows)], shifted[pl.ds(15 - down, rows)]
    ).astype(aligned.dtype)


def flatten_held(blocks, held, flat):
    stride, tail, rows = blocks.stride, blocks.tail, blocks.rows
    if stride % 16 == 0 and tail == 16:
        flat[0:tail] = held[0, 0:tail].astype(jnp.float32)
        flat[tail:rows] = held[0, tail:rows].astype(jnp.float32)

        def body(d, carry):
            start = pl.multiple_of(d * stride, 16)
            flat[pl.ds(start, tail)] += held[d, 0:tail].astype(jnp.float32)
            start = pl.multiple_of(d * stride + tail, 16)
            flat[pl.ds(start, stride)] = held[d, tail:rows].astype(jnp.float32)
            return carry

        lax.fori_loop(1, blocks.count, body, 0)
    else:
        flat[...] = jnp.zeros_like(flat)

        def body(d, carry):
            flat[pl.ds(d * stride, rows)] += held[d].astype(jnp.float32)
            return carry

        lax.fori_loop(0, blocks.count, body, 0)


def unflatten(flat, base, matrix, first, width):
    height, steps = matrix.shape[0], width // LANES
    for i in range(steps):
        matrix[:, first + i * LANES : first + (i + 1) * LANES] = flat[
            pl.ds(base + i, height, stride=steps), :
        ].astype(matrix.dtype)


def write_gain(flat, base, gain):
    for i in range(gain.shape[1] // LANES):
        flat[base + i : base + i + 1, :] = gain[:, i * LANES : (i + 1) * LANES]


def read_gain(flat, base, width):
    return jnp.concatenate([flat[base + i : base + i + 1, :] for i in range(width // LANES)], axis=-1)


class Halo:
    def __init__(self, place, wires, kv, block, first, size):
        self.place, self.wires, self.kv, self.block = place, wires, kv, block
        self.first, self.size = first, size

    def slot(self, at):
        return self.kv.at[pl.ds(self.first, self.size), pl.ds(pl.multiple_of(at * self.block, 128), self.block)]

    def outward(self):
        p = self.place
        self.outer = self.wires.copy(
            self.slot(4), self.slot(0), p.outer_peer(1), p.hi + 1 < p.outer
        )

    def plane(self):
        p = self.place
        guarded(p.hi > 0, self.outer.wait_recv)
        self.across = self.wires.copy(self.slot(4 * (1 - p.y)), self.slot(2), p.y_peer())
        self.near = self.wires.copy(self.slot(4 * (1 - p.c)), self.slot(3 - 2 * p.c), p.sibling())

    def relay(self):
        p = self.place
        self.across.wait_recv()
        self.far = self.wires.copy(self.slot(2), self.slot(1 + 2 * p.c), p.sibling())

    def end(self):
        self.near.wait_recv()
        self.far.wait_recv()


HALO_WIRES = 4


class Locals:
    def __init__(self, sems):
        self.sems, self.used, self.open = sems, 0, []

    def copy(self, src, dst):
        made = pltpu.make_async_copy(src, dst, self.sems.at[self.used])
        self.used += 1
        self.open.append(made)
        made.start()
        return made

    def finish(self, made):
        made.wait()
        self.open = [other for other in self.open if other is not made]

    def drain(self):
        for made in self.open:
            made.wait()
        self.open = []


class Geo:
    def __init__(self, tokens, attention_params, feed_params):
        self.seqs, self.block = tokens.shape[:2]
        self.rows = self.seqs * self.block
        self.count = lax.axis_size("batch") * lax.axis_size("seq")
        self.outer = lax.axis_size("seq") // 4
        self.attention = Blocks(attention_params.shape[0], self.count)
        self.feed = Blocks(feed_params.shape[0], self.count)
        self.reach = 5 * self.block
        rows = self.attention.rows
        early = (rows - 16) // 32 * 16
        self.attention_bounds = [0, early, rows - 16, rows]
        rows = self.feed.rows
        early = rows - 16
        self.feed_bounds = [0, early // 48 * 16, early // 48 * 32, early, rows]


QUERY = HEADS * HEAD_DIM
BASE_KEY = D * QUERY // LANES
BASE_VALUE = BASE_KEY + D * HEAD_DIM // LANES
BASE_OUT = BASE_VALUE + D * HEAD_DIM // LANES
BASE_GAINS = BASE_OUT + QUERY * D // LANES
STEP = 256
WIDE = 512


def forward_kernel(geo, tokens, positions, frequency, shards, *refs):
    (
        feed_held,
        out_wqkv,
        out_wo,
        out_gains,
        out_q,
        out_kv,
        out_merged,
        out_projected,
        out_hidden,
        out_cosine,
        out_sine,
    ) = refs[:11]
    (
        held,
        own_feed,
        shifted,
        flat,
        wqkv,
        wo,
        gains,
        cosine,
        sine,
        lows,
        normed,
        q,
        kv,
        scores,
        probs,
        merged,
        projected,
        hidden,
        send,
        recv,
        local,
    ) = refs[11:]
    place = Place()
    wires, locals_ = Wires(send, recv), Locals(local)
    seqs, block, reach = geo.seqs, geo.block, geo.reach
    announce(place)
    attention_in = shards.at[pl.ds(0, geo.attention.rows)]
    feed_in = shards.at[pl.ds(geo.attention.rows, geo.feed.rows)]
    align_shard(geo.attention, place, attention_in, shifted, held.at[place.mine()])
    meet(place)
    gather_a = Gather(place, wires, held, 0, geo.attention.rows, 0.5)
    gather_a.begin()
    gather_a.spread(0)
    align_shard(geo.feed, place, feed_in, shifted, own_feed)
    lead = locals_.copy(own_feed, feed_held.at[place.mine()])
    gather_f = Gather(place, wires, feed_held, 0, geo.feed.rows, 1.0)

    @pl.when(place.hi == 0)
    def _():
        kv[:, :block] = jnp.zeros((seqs, block, 2 * HEAD_DIM), jnp.bfloat16)

    columns = positions[...].astype(jnp.float32).T
    row = lax.broadcasted_iota(jnp.int32, (block, LANES), 0)
    for s in range(seqs):
        spot = columns[:, s : s + 1]
        angle = spot * frequency[...]
        rows = slice(s * block, (s + 1) * block)
        cosine[rows] = jnp.cos(angle)
        sine[rows] = jnp.sin(angle)
        lows[s] = jnp.maximum(row + 1, row + WINDOW - spot.astype(jnp.int32))

    locals_.finish(lead)
    gather_f.spread(0)
    for j in range(1, geo.outer):
        gather_a.spread(j)
    gather_f.begin()
    for j in range(geo.outer):
        gather_a.corner(j)
    for j in range(geo.outer):
        gather_a.finish(j)
    gather_f.corner(0)
    gather_a.end()
    pending = [[functools.partial(gather_f.spread, j) for j in range(1, geo.outer)]]
    pending += [[functools.partial(gather_f.corner, j)] for j in range(1, geo.outer)]
    pending += [[functools.partial(gather_f.finish, j)] for j in range(geo.outer)]

    def tick(amount=1):
        for _ in range(amount):
            if pending:
                for action in pending.pop(0):
                    action()

    flatten_held(geo.attention, held, flat)
    at = BASE_GAINS
    for i, width in enumerate((D, HEAD_DIM, HEAD_DIM, D)):
        gains[i : i + 1, :width] = read_gain(flat, at, width)
        at += width // LANES
    unflatten(flat, BASE_KEY, wqkv, QUERY, HEAD_DIM)
    unflatten(flat, BASE_VALUE, wqkv, QUERY + HEAD_DIM, HEAD_DIM)
    gain = gains[0:1, :]
    gain_key = gains[2:3, :HEAD_DIM]
    halos = []
    per_step = STEP // block
    for s in range(0, seqs, per_step):
        rows = slice(s * block, (s + per_step) * block)
        x = tokens[rows].astype(jnp.float32)
        normed[rows] = (x * root_inverse(x) * gain).astype(jnp.bfloat16)
        made = dot_nn(normed[rows], wqkv[:, QUERY:])
        keys = made[:, :HEAD_DIM]
        keys = turn(keys * root_inverse(keys) * gain_key, cosine[rows], sine[rows])
        for i in range(per_step):
            part = slice(i * block, (i + 1) * block)
            kv[s + i, reach - block :, :HEAD_DIM] = keys[part].astype(jnp.bfloat16)
            kv[s + i, reach - block :, HEAD_DIM:] = made[part, HEAD_DIM:].astype(jnp.bfloat16)
        halo = Halo(place, wires, kv, block, s, per_step)
        halo.outward()
        halos.append(halo)
    tick()
    unflatten(flat, 0, wqkv, 0, QUERY)
    gain_query = gains[1:2, :HEAD_DIM] * HEAD_DIM**-0.5
    for s in range(0, seqs, per_step):
        rows = slice(s * block, (s + per_step) * block)
        made = dot_nn(normed[rows], wqkv[:, :QUERY])
        for h in range(HEADS):
            one = made[:, h * HEAD_DIM : (h + 1) * HEAD_DIM]
            one = turn(one * root_inverse(one) * gain_query, cosine[rows], sine[rows])
            q[h, rows] = one.astype(jnp.bfloat16)
    unflatten(flat, BASE_OUT, wo, 0, D)
    for src, dst in (
        (wqkv, out_wqkv),
        (wo, out_wo),
        (gains, out_gains),
        (q, out_q),
        (cosine, out_cosine),
        (sine, out_sine),
    ):
        locals_.copy(src, dst)
    chunk = 32
    lane = lax.broadcasted_iota(jnp.int32, (chunk, reach), 1)
    over = lax.broadcasted_iota(jnp.int32, (chunk, reach), 1) - lax.broadcasted_iota(
        jnp.int32, (chunk, reach), 0
    )

    def attend(s, carry):
        start = pl.multiple_of(s * block, block)
        rows = pl.ds(start, block)
        queries = q[:, rows, :].reshape(HEADS * block, HEAD_DIM)
        scores[...] = dot_nt(queries, kv[s, :, :HEAD_DIM])
        for r in range(0, HEADS * block, chunk):
            i = r % block
            low = jnp.concatenate([lows[s, i : i + chunk, :]] * (reach // LANES), axis=-1)
            seen = (lane >= low) & (over <= WINDOW + i)
            raised = jnp.where(seen, jnp.exp(scores[r : r + chunk]), 0.0)
            share = 1.0 / jnp.sum(raised, axis=-1, keepdims=True)
            probs[r : r + chunk] = (raised * share).astype(jnp.bfloat16)
        made = dot_nn(probs[...], kv[s, :, HEAD_DIM:])
        for h in range(HEADS):
            merged[rows, h * HEAD_DIM : (h + 1) * HEAD_DIM] = made[
                h * block : (h + 1) * block
            ].astype(jnp.bfloat16)
        return carry

    count = len(halos)
    for g in range(count + 2):
        tick()
        if g < count:
            halos[g].plane()
        if 1 <= g <= count:
            halos[g - 1].relay()
        if g > 1:
            tick()
        if g >= 2:
            halos[g - 2].end()
            lax.fori_loop((g - 2) * per_step, (g - 1) * per_step, attend, 0)
    locals_.copy(kv, out_kv)
    locals_.copy(merged, out_merged)
    gain_post = gains[3:4, :]
    for s in range(0, seqs, per_step):
        rows = slice(s * block, (s + per_step) * block)
        made = dot_nn(merged[rows], wo[...])
        projected[rows] = made
        hidden[rows] = tokens[rows].astype(jnp.float32) + made * root_inverse(made) * gain_post
        locals_.copy(projected.at[rows], out_projected.at[rows])
        locals_.copy(hidden.at[rows], out_hidden.at[rows])
    tick(len(pending))
    gather_f.end()
    wires.drain()
    locals_.drain()


def vmem(shape, dtype):
    return pltpu.VMEM(shape, dtype)


def forward_pass(geo, tokens, positions, shards):
    count, rows, seqs, block = geo.count, geo.rows, geo.seqs, geo.block
    bf, f4 = jnp.bfloat16, jnp.float32
    half = HEAD_DIM // 2
    frequency = (
        rope_base ** (-(np.arange(half, dtype=np.float32) * np.float32(2.0) / HEAD_DIM))
    ).astype(np.float32)[None]
    wires = 2 * gather_wires(geo.outer) + geo.seqs // 2 * HALO_WIRES
    outs = [
        ((count, geo.feed.rows, LANES), bf),
        ((D, QUERY + 2 * HEAD_DIM), bf),
        ((QUERY, D), bf),
        ((8, D), f4),
        ((HEADS, rows, HEAD_DIM), bf),
        ((seqs, geo.reach, 2 * HEAD_DIM), bf),
        ((rows, QUERY), bf),
        ((rows, D), f4),
        ((rows, D), f4),
        ((rows, half), f4),
        ((rows, half), f4),
    ]
    flat_rows = geo.attention.count * geo.attention.stride + geo.attention.tail
    return pl.pallas_call(
        functools.partial(forward_kernel, geo),
        out_shape=[jax.ShapeDtypeStruct(*out) for out in outs],
        in_specs=[pl.BlockSpec(memory_space=pltpu.VMEM)] * 4,
        out_specs=[pl.BlockSpec(memory_space=pl.ANY)] * len(outs),
        scratch_shapes=[
            vmem((count, geo.attention.rows, LANES), bf),
            vmem((geo.feed.rows, LANES), bf),
            vmem((16 + geo.feed.rows, LANES), f4),
            vmem((flat_rows, LANES), f4),
            vmem((D, QUERY + 2 * HEAD_DIM), bf),
            vmem((QUERY, D), bf),
            vmem((8, D), f4),
            vmem((rows, half), f4),
            vmem((rows, half), f4),
            vmem((seqs, block, LANES), jnp.int32),
            vmem((rows, D), bf),
            vmem((HEADS, rows, HEAD_DIM), bf),
            vmem((seqs, geo.reach, 2 * HEAD_DIM), bf),
            vmem((HEADS * block, geo.reach), f4),
            vmem((HEADS * block, geo.reach), bf),
            vmem((rows, QUERY), bf),
            vmem((rows, D), f4),
            vmem((rows, D), f4),
            pltpu.SemaphoreType.DMA((wires,)),
            pltpu.SemaphoreType.DMA((wires,)),
            pltpu.SemaphoreType.DMA((32,)),
        ],
        compiler_params=pltpu.CompilerParams(
            collective_id=0, has_side_effects=True, vmem_limit_bytes=60 << 20
        ),
    )(tokens.reshape(rows, D), positions, jnp.asarray(frequency), shards)


MATRIX = D * FF // LANES
BEND = 0.044715
SLOPE = math.sqrt(2.0 / math.pi)


def feed_pieces(blocks, which):
    base, stop = which * MATRIX, (which + 1) * MATRIX
    if which == 2:
        stop = blocks.count * blocks.stride + blocks.tail
    found = []
    for d in range(blocks.count):
        low = max(d * blocks.stride, base)
        high = min(d * blocks.stride + blocks.rows, stop)
        if low < high:
            found.append((d, low - base, high - base, base - d * blocks.stride))
    return found


def feed_phase(
    geo, locals_, load_hidden, held_in, cotangent_in, mixed_out, split, grad, begin, tick, *refs
):
    (flat, twin, down, act, pair, feed_in, turned_in, grad_down) = refs
    mixed = cotangent = feed_in
    blocks = geo.feed
    ends = [-(-(-(-(m + 1) * MATRIX // blocks.stride)) // 4) for m in range(3)]
    starts = [0] + ends[:-1]
    loads = [
        locals_.copy(held_in.at[pl.ds(a, b - a)], split.at[pl.ds(a, b - a)])
        for a, b in zip(starts, ends)
    ]
    load_cotangent = locals_.copy(cotangent_in, grad_down)

    def index(d):
        return d // 4, d // 2 % 2, d % 2

    def unpack(which):
        for d, low, high, shift in feed_pieces(blocks, which):
            mid = min(high, max(low, d * blocks.stride - which * MATRIX + blocks.tail))
            if d and low < mid:
                flat[low:mid] += split[*index(d), low + shift : mid + shift].astype(jnp.float32)
            else:
                mid = low
            flat[mid:high] = split[*index(d), mid + shift : high + shift].astype(jnp.float32)

    def pack(which):
        for d, low, high, shift in feed_pieces(blocks, which):
            split[*index(d), low + shift : high + shift] = flat[low:high].astype(jnp.bfloat16)

    for which, (matrix, first, width) in enumerate(
        ((twin, 0, FF), (twin, FF, FF), (down, 0, D))
    ):
        locals_.finish(loads[which])
        unpack(which)
        unflatten(flat, 0, matrix, first, width)
    gain_feed = read_gain(flat, MATRIX, D)
    gain_out = read_gain(flat, MATRIX + D // LANES, D)

    total, step = geo.rows, WIDE
    spans = [slice(r, r + STEP) for r in range(0, total, STEP)]
    locals_.finish(load_hidden)
    for rows in spans:
        h = grad[rows]
        feed_in[rows] = (h * root_inverse(h) * gain_feed).astype(jnp.bfloat16)

    def rise(i, carry):
        columns = pl.ds(pl.multiple_of(i * step, step), step)
        others = pl.ds(pl.multiple_of(FF + i * step, step), step)
        for rows in spans:
            g = dot_nn(feed_in[rows], twin[:, columns])
            u = dot_nn(feed_in[rows], twin[:, others])
            square = g * g
            t = jnp.tanh(g * (SLOPE + SLOPE * BEND * square))
            half = 0.5 + 0.5 * t
            soft = g * half
            act[rows, columns] = (soft * u).astype(jnp.bfloat16)
            pair[rows, others] = soft.astype(jnp.bfloat16)
            slope = half * (1.0 + g * (1.0 - t) * (SLOPE + 3.0 * SLOPE * BEND * square))
            pair[rows, columns] = (u * slope).astype(jnp.bfloat16)
        return carry

    lax.fori_loop(0, FF // step, rise, 0)
    turned_in[...] = feed_in[...].T

    def settle(i, sum_out):
        rows = pl.ds(pl.multiple_of(i * STEP, STEP), STEP)
        made = dot_nn(act[rows], down[...])
        r = root_inverse(made)
        mixed[rows] = (grad[rows] + made * r * gain_out).astype(jnp.bfloat16)
        e = grad_down[rows].astype(jnp.float32)
        unit = made * r
        sum_out = sum_out + jnp.sum(e * unit, axis=0, keepdims=True)
        c = e * gain_out
        grad_down[rows] = (
            r * (c - unit * jnp.mean(unit * c, axis=-1, keepdims=True))
        ).astype(jnp.bfloat16)
        return sum_out

    locals_.finish(load_cotangent)
    sum_out = lax.fori_loop(0, total // STEP, settle, jnp.zeros((1, D), jnp.float32))
    store_mixed = locals_.copy(mixed, mixed_out)

    def fall(i, carry):
        columns = pl.ds(pl.multiple_of(i * step, step), step)
        others = pl.ds(pl.multiple_of(FF + i * step, step), step)
        for rows in spans:
            made = dot_nt(grad_down[rows], down[columns, :])
            for at in (columns, others):
                pair[rows, at] = (made * pair[rows, at].astype(jnp.float32)).astype(jnp.bfloat16)
        return carry

    lax.fori_loop(0, FF // step, fall, 0)

    def back(i, sum_feed):
        rows = pl.ds(pl.multiple_of(i * STEP, STEP), STEP)
        made = dot_nt(pair[rows], twin[...])
        h = grad[rows]
        r = root_inverse(h)
        unit = h * r
        sum_feed = sum_feed + jnp.sum(made * unit, axis=0, keepdims=True)
        c = made * gain_feed
        grad[rows] = cotangent[rows].astype(jnp.float32) + r * (
            c - unit * jnp.mean(unit * c, axis=-1, keepdims=True)
        )
        return sum_feed

    def wide(i, carry, first):
        made = dot_nn(turned_in[...], pair[:, pl.ds(pl.multiple_of(first + i * step, step), step)])
        for k in range(step // LANES):
            flat[pl.ds(i * (step // LANES) + k, D, stride=FF // LANES), :] = made[
                :, k * LANES : (k + 1) * LANES
            ]
        return carry

    locals_.finish(store_mixed)
    load_cotangent = locals_.copy(cotangent_in, cotangent)
    lax.fori_loop(0, FF // step, functools.partial(wide, first=0), 0)
    pack(0)
    lax.fori_loop(0, FF // step, functools.partial(wide, first=FF), 0)
    pack(1)

    def tall(i, carry):
        columns = pl.ds(pl.multiple_of(i * step, step), step)
        made = dot_tn(act[:, columns], grad_down[...])
        for k in range(D // LANES):
            flat[pl.ds(i * (step * D // LANES) + k, step, stride=D // LANES), :] = made[
                :, k * LANES : (k + 1) * LANES
            ]
        return carry

    lax.fori_loop(0, FF // step, tall, 0)
    flat[MATRIX:] = jnp.zeros_like(flat[MATRIX:])
    pack(2)
    begin()
    locals_.finish(load_cotangent)
    sum_feed = jnp.zeros((1, D), jnp.float32)
    for i in range(0, total // STEP, 2):
        sum_feed = lax.fori_loop(i, i + 2, back, sum_feed)
        tick()
    write_gain(flat, MATRIX, sum_feed)
    write_gain(flat, MATRIX + D // LANES, sum_out)
    last = blocks.count - 1
    low = blocks.count * blocks.stride - 2 * MATRIX
    split[*index(last), blocks.stride :] = flat[low:].astype(jnp.bfloat16)


class Scatter:
    def __init__(self, place, wires, other, own, lands, result, piece):
        self.place, self.wires, self.other, self.own, self.result = place, wires, other, own, result
        self.by_core, self.first_x, self.first_y, self.second_x, self.second_y, self.by_outer = lands
        first, cut, last, at_x, at_y = piece
        self.split = cut < last
        self.all = pl.ds(first, last - first)
        self.rows_x, self.rows_y = pl.ds(first, cut - first), pl.ds(cut, last - cut)
        self.land_x, self.land_y = pl.ds(at_x, cut - first), pl.ds(at_y, last - cut)
        p, plan = place, wires.plan
        mine, theirs = self.column_of(p.b), self.column_of(1 - p.b)
        self.from_core = plan(
            other.at[:, :, 1 - p.c, self.all], self.by_core.at[:, :, self.all], p.sibling()
        )
        self.from_x = plan(
            own.at[theirs, :, self.rows_x], self.first_x.at[:, :, self.land_x], p.x_peer()
        )
        self.over_y = plan(
            own.at[mine, 1 - p.y, self.rows_x], self.second_y.at[:, self.land_x], p.y_peer()
        )
        if self.split:
            self.from_y = plan(
                own.at[:, 1 - p.y, self.rows_y], self.first_y.at[:, self.land_y], p.y_peer()
            )
            self.over_x = plan(
                own.at[theirs, p.y, self.rows_y], self.second_x.at[:, self.land_y], p.x_peer()
            )
        self.from_outer = [
            plan(
                own.at[p.b * p.outer + p.flip(k), p.y, self.all],
                self.by_outer.at[k - 1, self.all],
                p.flip_peer(k),
            )
            for k in range(1, p.outer)
        ]

    def add(self, i, y, rows, land):
        self.own[i, y, rows] = (
            self.own[i, y, rows].astype(jnp.float32) + land.astype(jnp.float32)
        ).astype(jnp.bfloat16)

    def column_of(self, b):
        return pl.ds(b * self.place.outer, self.place.outer)

    def core(self):
        self.from_core.start()

    def plane(self):
        p = self.place
        self.from_core.wait_recv()

        def body(i, carry):
            for y in range(2):
                self.add(i, y, self.all, self.by_core[i, y, self.all])
            return carry

        lax.fori_loop(0, 2 * p.outer, body, 0)
        self.from_x.start()
        if self.split:
            self.from_y.start()

    def cross(self):
        p = self.place
        self.from_x.wait_recv()

        def body(hi, carry):
            for y in range(2):
                self.add(p.b * p.outer + hi, y, self.rows_x, self.first_x[hi, y, self.land_x])
            return carry

        lax.fori_loop(0, p.outer, body, 0)
        self.over_y.start()
        if self.split:
            self.from_y.wait_recv()

            def body(i, carry):
                self.add(i, p.y, self.rows_y, self.first_y[i, self.land_y])
                return carry

            lax.fori_loop(0, 2 * p.outer, body, 0)
            self.over_x.start()

    def column(self):
        p = self.place
        self.over_y.wait_recv()
        if self.split:
            self.over_x.wait_recv()

        def body(hi, carry):
            i = p.b * p.outer + hi
            self.add(i, p.y, self.rows_x, self.second_y[hi, self.land_x])
            if self.split:
                self.add(i, p.y, self.rows_y, self.second_x[hi, self.land_y])
            return carry

        lax.fori_loop(0, p.outer, body, 0)
        for made in self.from_outer:
            made.start()

    def end(self):
        p = self.place
        total = self.own[p.b * p.outer + p.hi, p.y, self.all].astype(jnp.float32)
        for k, made in enumerate(self.from_outer):
            made.wait_recv()
            total = total + self.by_outer[k, self.all].astype(jnp.float32)
        self.result[self.all] = total


def scatter_wires(outer):
    return 5 + outer - 1


def cut_pieces(bounds, shares):
    pieces, at_x, at_y = [], 0, 0
    for first, last, share in zip(bounds, bounds[1:], shares):
        cut = first + max(16, int((last - first) * share) // 16 * 16)
        pieces.append((first, cut, last, at_x, at_y))
        at_x, at_y = at_x + cut - first, at_y + last - cut
    return pieces, at_x, at_y


def land_shapes(rows, bounds, shares, outer):
    rows_x, rows_y = cut_pieces(bounds, shares)[1:]
    return [
        pltpu.VMEM(shape + (LANES,), jnp.bfloat16)
        for shape in (
            (2 * outer, 2, rows),
            (outer, 2, rows_x),
            (2 * outer, rows_y),
            (outer, rows_y),
            (outer, rows_x),
            (outer - 1, rows),
        )
    ]


class Return:
    def __init__(self, place, wires, kv, own, by_core, by_y, by_outer, block, first, size):
        self.place, self.wires, self.kv, self.own, self.block = place, wires, kv, own, block
        self.by_core, self.by_y, self.by_outer = by_core, by_y, by_outer
        self.group = pl.ds(first, size)
        self.each = range(first, first + size)

    def rows(self, at):
        return slice(at * self.block, (at + 1) * self.block)

    def slot(self, at):
        return self.kv.at[self.group, pl.ds(at * self.block, self.block)]

    def core(self):
        p = self.place
        self.from_core = [
            self.wires.copy(
                self.slot(at), self.by_core.at[self.group, pl.ds(i * self.block, self.block)], p.sibling()
            )
            for i, at in enumerate((1, 3))
        ]

    def grow(self, s, at, extra):
        rows = self.rows(at)
        self.kv[s, rows] = (self.kv[s, rows].astype(jnp.float32) + extra).astype(jnp.bfloat16)

    def plane(self):
        p = self.place
        for made in self.from_core:
            made.wait_recv()
        for s in self.each:

            @pl.when(p.c == 0)
            def _():
                self.grow(s, 2, self.by_core[s, self.rows(0)].astype(jnp.float32))
                self.own[s] += self.by_core[s, self.rows(1)].astype(jnp.float32)

            @pl.when(p.c == 1)
            def _():
                self.grow(s, 0, self.by_core[s, self.rows(0)].astype(jnp.float32))
                self.grow(s, 2, self.by_core[s, self.rows(1)].astype(jnp.float32))

        self.from_y = self.wires.copy(self.slot(2), self.by_y.at[self.group], p.y_peer())

    def outward(self):
        p = self.place
        self.from_y.wait_recv()
        for s in self.each:

            @pl.when(p.y == 0)
            def _():
                self.own[s] += self.by_y[s].astype(jnp.float32)

            @pl.when(p.y == 1)
            def _():
                self.grow(s, 0, self.by_y[s].astype(jnp.float32))

        self.from_outer = self.wires.copy(
            self.slot(0), self.by_outer.at[self.group], p.outer_peer(p.outer - 1), p.hi > 0
        )

    def end(self):
        p = self.place

        @pl.when(p.hi + 1 < p.outer)
        def _():
            self.from_outer.wait_recv()
            for s in self.each:
                self.own[s] += self.by_outer[s].astype(jnp.float32)


RETURN_WIRES = 4
FEED_SHARES = (0.5, 1.0, 1.0, 1.0)
ATTENTION_SHARES = (0.5, 0.5, 1.0)


def fill_blocks(blocks, split, flat, margin, base, stop):
    even = blocks.stride % 16 == 0
    for d in range(blocks.count):
        low, high = max(d * blocks.stride, base), min(d * blocks.stride + blocks.rows, stop)
        if low >= high:
            continue
        i, y, c = d // 4, d // 2 % 2, d % 2
        first, last = low - d * blocks.stride, high - d * blocks.stride
        if even:
            split[i, y, c, first:last] = flat[low - base + margin : high - base + margin].astype(
                jnp.bfloat16
            )
        else:
            start, end = first // 16 * 16, -(-last // 16) * 16
            source = low - base + margin - (first - start)
            split[i, y, c, start:end] = (
                split[i, y, c, start:end].astype(jnp.float32)
                + flat[source : source + end - start]
            ).astype(jnp.bfloat16)


MARGIN = 16


def backward_kernel(
    geo, positions, gains, tokens_in, wqkv_in, wo_in, q_in, kv_in, merged_in, projected_in,
    hidden_in, cosine_in, sine_in, held_in, cotangent_in, *refs
):
    grad_tokens, mixed_out, attention_sum, feed_sum = refs[:4]
    grad, split_f, split_a, by_core_kv, by_y_kv, by_outer_kv = refs[4:10]
    lands_a, lands_f = refs[10:16], refs[16:22]
    send, recv, local = refs[22:]
    place = Place()
    wires, locals_ = Wires(send, recv), Locals(local)
    bf, f4, rows, half = jnp.bfloat16, jnp.float32, geo.rows, HEAD_DIM // 2
    load_hidden = locals_.copy(hidden_in, grad)
    announce(place)
    pieces = cut_pieces(geo.feed_bounds, FEED_SHARES)[0]
    own_f = split_f.at[:, :, place.c]
    one, two, three, four = [
        Scatter(place, wires, split_f, own_f, lands_f, feed_sum, piece) for piece in pieces
    ]

    def begin():
        meet(place)
        for part in (one, two, three):
            part.core()

    pending = [
        [one.plane], [two.plane],
        [],
        [one.cross], [three.plane], [], [one.column],
        [two.cross],
        [four.plane],
        [two.column, three.cross, one.end],
        [four.cross, three.column],
        [two.end, four.column, three.end, four.end],
    ]

    def tick():
        for action in pending.pop(0):
            action()

    pl.run_scoped(
        functools.partial(
            feed_phase, geo, locals_, load_hidden, held_in, cotangent_in, mixed_out, split_f, grad,
            begin, tick,
        ),
        vmem((MATRIX + geo.feed.tail, LANES), f4),
        vmem((D, 2 * FF), bf),
        vmem((FF, D), bf),
        vmem((rows, FF), bf),
        vmem((rows, 2 * FF), bf),
        vmem((rows, D), bf),
        vmem((D, rows), bf),
        vmem((rows, D), bf),
    )
    four.core()
    pl.run_scoped(
        functools.partial(
            attention_phase, geo, place, wires, locals_, positions, gains,
            (tokens_in, wqkv_in, wo_in, q_in, kv_in, merged_in, projected_in, cosine_in, sine_in),
            grad_tokens, attention_sum, grad, split_a, by_core_kv, by_y_kv, by_outer_kv, lands_a,
            pending, tick,
        ),
        vmem((rows, D), bf),
        vmem(wqkv_in.shape, bf),
        vmem(wo_in.shape, bf),
        vmem(q_in.shape, bf),
        vmem(kv_in.shape, bf),
        vmem((rows, QUERY + 2 * HEAD_DIM), bf),
        vmem((rows, half), f4),
        vmem((rows, half), f4),
        vmem((2 * geo.reach, D), f4),
        vmem((rows, D), bf),
        vmem((max(D, geo.reach), max(rows, 2 * HEADS * geo.block)), bf),
        vmem((HEADS, rows, HEAD_DIM), bf),
        vmem((rows, D), bf),
        vmem((geo.seqs, geo.block, 2 * HEAD_DIM), f4),
        vmem((2 * MARGIN + QUERY * D // LANES, LANES), f4),
    )


def attention_phase(
    geo, place, wires, locals_, positions, gains, saved, grad_tokens, attention_sum, grad,
    split, by_core_kv, by_y_kv, by_outer_kv, lands_a, pending, tick, *refs
):
    tokens_in, wqkv_in, wo_in, q_in, kv_in, merged_in, projected_in, cosine_in, sine_in = saved
    (
        tokens, wqkv, wo, q, kv, pair, cosine, sine, work, normed, shared, grad_out, out_rows,
        own_kv, flat,
    ) = refs
    seqs, block, reach, total, step = geo.seqs, geo.block, geo.reach, geo.rows, STEP
    turned = shared.at[pl.ds(0, D), pl.ds(0, total)]
    probs = shared.at[pl.ds(0, reach), pl.ds(0, HEADS * block)]
    logits = shared.at[pl.ds(0, reach), pl.ds(HEADS * block, HEADS * block)]
    projected = work.at[pl.ds(0, total)]
    scores = work.at[pl.ds(0, reach), pl.ds(0, HEADS * block)]
    slopes = work.at[pl.ds(reach, reach), pl.ds(0, HEADS * block)]
    load_projected = locals_.copy(projected_in, projected)
    load_wo = locals_.copy(wo_in, wo)
    load_tokens = locals_.copy(tokens_in, tokens)
    load_merged = locals_.copy(merged_in, pair.at[:, pl.ds(0, QUERY)])
    load_q, load_kv = locals_.copy(q_in, q), locals_.copy(kv_in, kv)
    load_rest = [
        locals_.copy(wqkv_in, wqkv), locals_.copy(cosine_in, cosine), locals_.copy(sine_in, sine)
    ]
    gain_attention, gain_query = gains[0:1, :], gains[1:2, :HEAD_DIM]
    gain_key, gain_post = gains[2:3, :HEAD_DIM], gains[3:4, :]
    for made in (load_projected, load_wo, load_tokens):
        locals_.finish(made)

    def start_rows(i, summed):
        rows = pl.ds(pl.multiple_of(i * step, step), step)
        made, e = projected[rows], grad[rows]
        r = root_inverse(made)
        unit = made * r
        c = e * gain_post
        out_rows[rows] = (r * (c - unit * jnp.mean(unit * c, axis=-1, keepdims=True))).astype(
            jnp.bfloat16
        )
        x = tokens[rows].astype(jnp.float32)
        normed[rows] = (x * root_inverse(x) * gain_attention).astype(jnp.bfloat16)
        for h in range(HEADS):
            grad_out[h, rows] = dot_nt(
                out_rows[rows], wo[h * HEAD_DIM : (h + 1) * HEAD_DIM, :]
            ).astype(jnp.bfloat16)
        return summed + jnp.sum(e * unit, axis=0, keepdims=True)

    sum_post = lax.fori_loop(0, total // step, start_rows, jnp.zeros((1, D), jnp.float32))
    tick()
    blocks = geo.attention
    flat[0:MARGIN] = jnp.zeros((MARGIN, LANES), jnp.float32)
    flat[MARGIN + QUERY * D // LANES :] = jnp.zeros((MARGIN, LANES), jnp.float32)
    if blocks.stride % 16:
        split[...] = jnp.zeros_like(split)
    locals_.finish(load_merged)

    for made in [load_q, load_kv] + load_rest:
        locals_.finish(made)

    wide = HEADS * block
    chunk = 32
    lane = lax.rem(lax.broadcasted_iota(jnp.int32, (chunk, wide), 1), block)
    line = lax.broadcasted_iota(jnp.int32, (chunk, wide), 0)

    def attend(s, carry):
        rows = pl.ds(pl.multiple_of(s * block, block), block)
        queries = q[:, rows, :].reshape(wide, HEAD_DIM)
        given = grad_out[:, rows, :].reshape(wide, HEAD_DIM)
        scores[...] = dot_nt(kv[s, :, :HEAD_DIM], queries)
        slopes[...] = dot_nt(kv[s, :, HEAD_DIM:], given)
        spot = jnp.concatenate([positions[pl.ds(s, 1), :]] * HEADS, axis=-1)
        low = jnp.maximum(lane[0:1] + 1, lane[0:1] + WINDOW - spot)
        total_e = jnp.zeros((8, wide), jnp.float32)
        total_d = jnp.zeros((8, wide), jnp.float32)
        for r in range(0, reach, chunk):
            seen = (line + r >= low) & (line + (r - WINDOW) <= lane)
            raised = jnp.where(seen, jnp.exp(scores[r : r + chunk]), 0.0)
            scores[r : r + chunk] = raised
            moved = raised * slopes[r : r + chunk]
            for k in range(0, chunk, 8):
                total_e = total_e + raised[k : k + 8]
                total_d = total_d + moved[k : k + 8]
        share = 1.0 / jnp.sum(total_e, axis=0, keepdims=True)
        inner = jnp.sum(total_d, axis=0, keepdims=True) * share
        for r in range(0, reach, chunk):
            p = scores[r : r + chunk] * share
            probs[r : r + chunk] = p.astype(jnp.bfloat16)
            logits[r : r + chunk] = (p * (slopes[r : r + chunk] - inner)).astype(jnp.bfloat16)
        grad_q = dot_tn(logits[...], kv[s, :, :HEAD_DIM]) * HEAD_DIM**-0.5
        grad_k = dot_nn(logits[...], queries)
        grad_v = dot_nn(probs[...], given)
        early = reach - block
        kv[s, :early, :HEAD_DIM] = grad_k[:early].astype(jnp.bfloat16)
        kv[s, :early, HEAD_DIM:] = grad_v[:early].astype(jnp.bfloat16)
        own_kv[s, :, :HEAD_DIM] = grad_k[early:]
        own_kv[s, :, HEAD_DIM:] = grad_v[early:]
        for h in range(HEADS):
            q[h, rows] = grad_q[h * block : (h + 1) * block].astype(jnp.bfloat16)
        return carry

    size = 1
    returns = [
        Return(place, wires, kv, own_kv, by_core_kv, by_y_kv, by_outer_kv, block, s, size)
        for s in range(0, seqs, size)
    ]
    for g, group in enumerate(returns):
        lax.fori_loop(g * size, (g + 1) * size, attend, 0)
        group.core()
        if g >= 1:
            returns[g - 1].plane()
        if g >= 2:
            returns[g - 2].outward()
        if g % 2:
            tick()
    last = len(returns) - 1
    turned[...] = normed[...].T

    def tall(i, carry):
        columns = pl.ds(pl.multiple_of(i * step, step), step)
        made = dot_tn(pair[:, columns], out_rows[...])
        for k in range(D // LANES):
            flat[pl.ds(MARGIN + i * (step * D // LANES) + k, step, stride=D // LANES), :] = made[
                :, k * LANES : (k + 1) * LANES
            ]
        return carry

    lax.fori_loop(0, QUERY // step, tall, 0)
    fill_blocks(blocks, split, flat, MARGIN, BASE_OUT, BASE_GAINS)
    def query_rows(i, summed):
        rows = pl.ds(pl.multiple_of(i * step, step), step)
        made = dot_nn(normed[rows], wqkv[:, :QUERY])
        for h in range(HEADS):
            raw = made[:, h * HEAD_DIM : (h + 1) * HEAD_DIM]
            e = turn_back(q[h, rows].astype(jnp.float32), cosine[rows], sine[rows])
            r = root_inverse(raw)
            unit = raw * r
            summed = summed + jnp.sum(e * unit, axis=0, keepdims=True)
            c = e * gain_query
            pair[rows, h * HEAD_DIM : (h + 1) * HEAD_DIM] = (
                r * (c - unit * jnp.mean(unit * c, axis=-1, keepdims=True))
            ).astype(jnp.bfloat16)
        return summed

    returns[last].plane()
    returns[last - 1].outward()
    tick()
    sum_query = lax.fori_loop(0, total // step, query_rows, jnp.zeros((1, HEAD_DIM), jnp.float32))
    returns[last].outward()
    tick()

    def broad(i, carry, first, width):
        columns = pl.ds(pl.multiple_of(first + i * step, step), step)
        made = dot_nn(turned[...], pair[:, columns])
        for k in range(step // LANES):
            start = MARGIN + i * (step // LANES) + k
            flat[pl.ds(start, D, stride=width // LANES), :] = made[:, k * LANES : (k + 1) * LANES]
        return carry

    lax.fori_loop(0, QUERY // step, functools.partial(broad, first=0, width=QUERY), 0)
    fill_blocks(blocks, split, flat, MARGIN, 0, BASE_KEY)
    tick()
    for group in returns:
        group.end()

    def key_rows(i, summed):
        rows = pl.ds(pl.multiple_of(i * step, step), step)
        per = step // block
        raw = dot_nn(normed[rows], wqkv[:, QUERY : QUERY + HEAD_DIM])
        both = own_kv[pl.ds(i * per, per)].reshape(step, 2 * HEAD_DIM)
        e = turn_back(both[:, :HEAD_DIM], cosine[rows], sine[rows])
        r = root_inverse(raw)
        unit = raw * r
        c = e * gain_key
        pair[rows, QUERY : QUERY + HEAD_DIM] = (
            r * (c - unit * jnp.mean(unit * c, axis=-1, keepdims=True))
        ).astype(jnp.bfloat16)
        pair[rows, QUERY + HEAD_DIM :] = both[:, HEAD_DIM:].astype(jnp.bfloat16)
        return summed + jnp.sum(e * unit, axis=0, keepdims=True)

    sum_key = lax.fori_loop(0, total // step, key_rows, jnp.zeros((1, HEAD_DIM), jnp.float32))
    for first, base in ((QUERY, BASE_KEY), (QUERY + HEAD_DIM, BASE_VALUE)):
        broad(0, 0, first, HEAD_DIM)
        size_rows = D * HEAD_DIM // LANES
        flat[MARGIN + size_rows : 2 * MARGIN + size_rows] = jnp.zeros((MARGIN, LANES), jnp.float32)
        fill_blocks(blocks, split, flat, MARGIN, base, base + size_rows)

    def end_rows(i, summed):
        rows = pl.ds(pl.multiple_of(i * step, step), step)
        made = dot_nt(pair[rows], wqkv[...])
        x = tokens[rows].astype(jnp.float32)
        r = root_inverse(x)
        unit = x * r
        c = made * gain_attention
        grad[rows] = grad[rows] + r * (c - unit * jnp.mean(unit * c, axis=-1, keepdims=True))
        return summed + jnp.sum(made * unit, axis=0, keepdims=True)

    tail = geo.attention.tail
    own = split.at[:, :, place.c]
    one, two, three = [
        Scatter(place, wires, split, own, lands_a, attention_sum, piece)
        for piece in cut_pieces(geo.attention_bounds, ATTENTION_SHARES)[0]
    ]
    one.core()
    two.core()
    tick()
    sum_attention = jnp.zeros((1, D), jnp.float32)
    half = total // step // 2
    one.plane()
    sum_attention = lax.fori_loop(0, half, end_rows, sum_attention)
    two.plane()
    sum_attention = lax.fori_loop(half, 2 * half, end_rows, sum_attention)
    locals_.copy(grad, grad_tokens)
    tick()
    flat[MARGIN : 2 * MARGIN + tail] = jnp.zeros((MARGIN + tail, LANES), jnp.float32)
    at = MARGIN
    for made in (sum_attention, sum_query, sum_key, sum_post):
        write_gain(flat, at, made)
        at += made.shape[1] // LANES
    fill_blocks(blocks, split, flat, MARGIN, BASE_GAINS, blocks.count * blocks.stride + tail)
    three.core()
    for action in (
        one.cross, three.plane, two.cross, one.column, three.cross, two.column, three.column,
        one.end, two.end, three.end,
    ):
        action()
    wires.drain()
    locals_.drain()


def backward_pass(geo, tokens, positions, saved, hidden, feed_held, cotangent):
    bf, f4, rows, seqs, block = jnp.bfloat16, jnp.float32, geo.rows, geo.seqs, geo.block
    wqkv, wo, gains, q, kv, merged, projected, cosine, sine = saved
    rows_a, rows_f, outer = geo.attention.rows, geo.feed.rows, geo.outer
    outs = [((rows, D), f4), ((rows, D), bf), ((rows_a, LANES), f4), ((rows_f, LANES), f4)]
    full, hbm = pl.BlockSpec(memory_space=pltpu.VMEM), pl.BlockSpec(memory_space=pl.ANY)
    wires = (len(geo.feed_bounds) + len(geo.attention_bounds) - 2) * scatter_wires(
        outer
    ) + seqs * RETURN_WIRES
    return pl.pallas_call(
        functools.partial(backward_kernel, geo),
        out_shape=[jax.ShapeDtypeStruct(*out) for out in outs],
        in_specs=[full] * 2 + [hbm] * 12,
        out_specs=[hbm, hbm, full, full],
        scratch_shapes=[
            vmem((rows, D), f4),
            vmem((2 * outer, 2, 2, rows_f, LANES), bf),
            vmem((2 * outer, 2, 2, rows_a, LANES), bf),
            vmem((seqs, 2 * block, 2 * HEAD_DIM), bf),
            vmem((seqs, block, 2 * HEAD_DIM), bf),
            vmem((seqs, block, 2 * HEAD_DIM), bf),
        ]
        + land_shapes(rows_a, geo.attention_bounds, ATTENTION_SHARES, outer)
        + land_shapes(rows_f, geo.feed_bounds, FEED_SHARES, outer)
        + [
            pltpu.SemaphoreType.DMA((wires,)),
            pltpu.SemaphoreType.DMA((wires,)),
            pltpu.SemaphoreType.DMA((32,)),
        ],
        compiler_params=pltpu.CompilerParams(
            collective_id=1, has_side_effects=True, vmem_limit_bytes=63 << 20
        ),
    )(
        positions, gains, tokens.reshape(rows, D), wqkv, wo, q, kv, merged, projected, hidden,
        cosine, sine, feed_held.reshape(2 * outer, 2, 2, rows_f, LANES), cotangent.reshape(rows, D),
    )


def on_device(tokens, attention_params, feed_params, positions, cotangent):
    geo = Geo(tokens, attention_params, feed_params)
    start = geo.attention.rows * LANES
    after = geo.feed.spare()
    shards = (
        jnp.pad(attention_params, (0, geo.attention.spare() + geo.feed.rows * LANES))
        + jnp.pad(feed_params, (start, after))
    ).reshape(-1, LANES)
    device = lax.axis_index("batch") * lax.axis_size("seq") + lax.axis_index("seq")
    (
        feed_held, wqkv, weight_out, gains, q, kv, merged, projected, hidden, cosine, sine,
    ) = forward_pass(geo, tokens, positions, shards)
    grad_tokens, mixed, attention_sum, feed_sum = backward_pass(
        geo,
        tokens,
        positions,
        (wqkv, weight_out, gains, q, kv, merged, projected, cosine, sine),
        hidden,
        feed_held,
        cotangent,
    )
    return (
        mixed.reshape(tokens.shape),
        grad_tokens.reshape(tokens.shape),
        geo.attention.take(attention_sum, device),
        geo.feed.take(feed_sum, device),
    )


def solution(mesh):
    return jax.shard_map(
        on_device,
        mesh=mesh,
        in_specs=(
            P("batch", "seq", None),
            P(("batch", "seq")),
            P(("batch", "seq")),
            P("batch", "seq"),
            P("batch", "seq", None),
        ),
        out_specs=(
            P("batch", "seq", None),
            P("batch", "seq", None),
            P(("batch", "seq")),
            P(("batch", "seq")),
        ),
        check_vma=False,
    )
```
